32 devices in a mesh: grp: 4 (over y, x), docs: 8 (over z, core).
Axes of the slice: x: 2, y: 2, z: 4, core: 2. Of those that a mesh axis runs over, the one named last changes fastest.
Arguments:
- embeddings: float32 [131072, 1024], P(('grp', 'docs'))
- assign: int32 [131072], P(('grp', 'docs')), may hold values from 0 to 767, as said below
- cluster_slot: int32 [768], replicated, may hold values from 0 to 767, as said below
Outputs:
- centroids: float32 [768, 1024], P('docs')
- max_sim: float32 [131072], P(('grp', 'docs'))
- centroid_cos: float32 [131072], P(('grp', 'docs'))
The draws below stay inside these ranges and needn't reach their ends.
Inputs may be any that keep to these rules, and one draw needn't show every extreme that they name: Each device's rows are ordered by owner, cluster_slot[assign] // 96; a device sends at most 640 rows to one owner and some device sends exactly 640; every owner receives exactly 4096 rows from the devices of its group; in each group every cluster is named by 2 to 128 rows, and some cluster by exactly 128. A permutation: cluster c is held at slot cluster_slot[c] by the owner of index cluster_slot[c] // 96 along docs.
All inputs are finite; a program needn't handle non-finite values.
Results may differ from the reference program's by a relative error of at most 0.0003.
Values may be sent and summed in bfloat16 or wider, within the bound.
No kernel may reach another device: no remote copies, remote signals or barrier semaphores. Data moves between devices by JAX's collectives and lax.ppermute only.
A program may use at most 192 MiB of HBM per device.

```python
import math
import jax
import jax.numpy as jnp
from jax import lax

D = 1024
KL = 96
R = 4096
MAXC = 128
K = 768
GROUP_ROWS = 32768
ROWS = 131072
N_GRP = 4
N_DOCS = 8


def distinct_order(key, shape):
    length = shape[-1]
    scores = jax.random.randint(key, shape, 0, 2 ** 30 // length) * length + jnp.arange(length, dtype=jnp.int32)
    return jnp.argsort(scores, axis=-1).astype(jnp.int32)


def layout(key):
    key_list = jax.random.split(key, 7)
    mean_load = R // N_DOCS
    lift_top = mean_load // 4
    lifts = jax.random.randint(key_list[0], (N_GRP, N_DOCS // 2), 0, lift_top + 1)
    lifts = lifts.at[:, 0].set(lift_top)
    loads = mean_load + jnp.stack([lifts, -lifts], -1).reshape(N_GRP, N_DOCS)
    source_order = distinct_order(key_list[1], (N_GRP, N_DOCS))
    owner_order = distinct_order(key_list[2], (N_GRP, N_DOCS))
    pattern = (source_order[:, :, None] + owner_order[:, None, :]) % N_DOCS
    sends = jnp.take_along_axis(jnp.broadcast_to(loads[:, None, :], (N_GRP, N_DOCS, N_DOCS)), pattern, axis=2)
    weights = jax.random.randint(key_list[3], (N_GRP, N_DOCS, KL - 1), 2, 5)
    spare = R - MAXC - (KL - 1)
    shares = spare * weights // jnp.sum(weights, -1, keepdims=True)
    leftover = spare - jnp.sum(shares, -1, keepdims=True)
    bumped = (jnp.arange(KL - 1, dtype=jnp.int32) < leftover).astype(jnp.int32)
    cluster_rows = jnp.concatenate([jnp.full((N_GRP, N_DOCS, 1), MAXC, jnp.int32), 1 + shares + bumped], -1)
    cluster_rows = jnp.take_along_axis(cluster_rows, distinct_order(key_list[4], (N_GRP, N_DOCS, KL)), axis=-1)
    cluster_ends = jnp.cumsum(cluster_rows, -1)
    positions = jnp.arange(R, dtype=jnp.int32)
    labels = jnp.sum((positions[:, None] >= cluster_ends[:, :, None, :]).astype(jnp.int32), -1)
    sequence = jnp.take_along_axis(labels, distinct_order(key_list[5], (N_GRP, N_DOCS, R)), axis=-1)
    send_ends = jnp.cumsum(sends, 2)
    send_first = send_ends - sends
    owner_first = jnp.cumsum(sends, 1) - sends
    target = jnp.sum((positions[None, None, :, None] >= send_ends[:, :, None, :]).astype(jnp.int32), -1)
    within = jnp.take_along_axis(owner_first, target, 2) + positions[None, None, :] - jnp.take_along_axis(send_first, target, 2)
    flat_index = (target * R + within).reshape(N_GRP, N_DOCS * R)
    local_label = jnp.take_along_axis(sequence.reshape(N_GRP, N_DOCS * R), flat_index, axis=1)
    cluster_at = distinct_order(key_list[6], (KL * N_DOCS,))
    assign = cluster_at[target.reshape(N_GRP, N_DOCS * R) * KL + local_label].reshape(-1)
    return (assign.astype(jnp.int32), jnp.argsort(cluster_at).astype(jnp.int32))


def draw_assign(key, part):
    return layout(key)[0]


def draw_cluster_slot(key, part):
    return layout(key)[1]


def draw_embeddings(key, part):
    assign = layout(key)[0]
    key = jax.random.fold_in(key, 7)
    key_list = jax.random.split(key, 5)
    centers = jax.random.normal(key_list[0], (KL * N_DOCS, D), jnp.float32)
    row_scale = jnp.exp(jax.random.uniform(key_list[1], (ROWS, 1), jnp.float32, 0.0, math.log(10.0)))
    column_scale = jnp.exp(jax.random.uniform(key_list[2], (1, D), jnp.float32, 0.0, math.log(3.0)))
    spread = jax.random.uniform(key_list[3], (ROWS, 1), jnp.float32, 0.3, 1.5)
    noise = jax.random.normal(key_list[4], (ROWS, D), jnp.float32)
    return row_scale * column_scale * (centers[assign] + spread * noise)


def setup_inputs(seed: int = 0) -> dict:
    streams_of = jax.random.split(jax.random.key(seed), 4)
    return {
        "embeddings": draw_embeddings(jax.random.fold_in(streams_of[3], 71), 0),
        "assign": draw_assign(jax.random.fold_in(streams_of[3], 71), 0),
        "cluster_slot": draw_cluster_slot(jax.random.fold_in(streams_of[3], 71), 0),
    }


epsilon = 1e-06

def unit_rows(values):
    return values * lax.rsqrt(lax.optimization_barrier(jnp.sum(values * values, -1, keepdims=True)) + epsilon)

def group_result(unit_group, slot_group, centroid_unit):
    group_count = slot_group.shape[0]
    row_order = jnp.argsort(slot_group, stable=True).astype(jnp.int32)
    padded = jnp.concatenate([unit_group[row_order], jnp.zeros((MAXC, D), unit_group.dtype)], 0)
    members = jax.ops.segment_sum(jnp.ones((group_count,), jnp.int32), slot_group, num_segments=K)
    starts = (jnp.cumsum(members) - members).astype(jnp.int32)
    row_range = jnp.arange(MAXC, dtype=jnp.int32)

    def one_block(block_args):
        block_start, member_count = block_args
        block_unit = lax.dynamic_slice_in_dim(padded, block_start, MAXC, 0).astype(jnp.float32)
        gram_block = jnp.dot(block_unit, block_unit.T, precision=lax.Precision.HIGHEST)
        allowed = (row_range[None, :] < member_count) & (row_range[:, None] != row_range[None, :])
        return lax.optimization_barrier(jnp.max(jnp.where(allowed, gram_block, -2.0), -1))
    nearest = lax.map(one_block, (starts, members))
    sorted_slots = slot_group[row_order]
    within = jnp.arange(group_count, dtype=jnp.int32) - starts[sorted_slots]
    nearest_sorted = nearest[sorted_slots, within]
    max_sim = jnp.zeros((group_count,), jnp.float32).at[row_order].set(nearest_sorted)
    centroid_cos = lax.optimization_barrier(jnp.sum(unit_group.astype(jnp.float32) * centroid_unit[slot_group].astype(jnp.float32), -1))
    return (max_sim, centroid_cos)

def reference(embeddings, assign, cluster_slot):
    slot_of_row = cluster_slot[assign]
    slot_sums = jax.ops.segment_sum(embeddings, slot_of_row, num_segments=K)
    row_tally = jax.ops.segment_sum(jnp.ones(slot_of_row.shape, jnp.float32), slot_of_row, num_segments=K)
    centroids = slot_sums / row_tally[:, None]
    centroid_unit = unit_rows(centroids).astype(jnp.bfloat16)
    unit_vectors = unit_rows(embeddings).astype(jnp.bfloat16)
    unit_groups = unit_vectors.reshape(N_GRP, GROUP_ROWS, D)
    slot_groups = slot_of_row.reshape(N_GRP, GROUP_ROWS)

    def per_group(group_args):
        return group_result(group_args[0], group_args[1], centroid_unit)
    max_sim, centroid_cos = lax.map(per_group, (unit_groups, slot_groups))
    return (centroids, max_sim.reshape(-1), centroid_cos.reshape(-1))
```

```python
import functools

import jax
import jax.numpy as jnp
from jax import lax
from jax.experimental import pallas as pl
from jax.experimental.pallas import tpu as pltpu
from jax.sharding import PartitionSpec as P

epsilon = 1e-06
LANES = 128
SUBLANES = 8
VMEM_BYTES = 48 * 1024 * 1024
in_vmem = pl.BlockSpec(memory_space=pltpu.VMEM)
in_smem = pl.BlockSpec(memory_space=pltpu.SMEM)
anywhere = pl.BlockSpec(memory_space=pl.ANY)


def round_up(value, step):
    return -(-value // step) * step


def params(**extra):
    return pltpu.CompilerParams(vmem_limit_bytes=VMEM_BYTES, **extra)


def look_up(table_ref, index):
    lane = jnp.bitwise_and(index, LANES - 1)
    row = jnp.right_shift(index, 7)
    found = jnp.zeros(index.shape, jnp.int32)
    for part in range(table_ref.shape[0]):
        entries = jnp.broadcast_to(table_ref[part : part + 1, :], index.shape)
        found = jnp.where(row == part, jnp.take_along_axis(entries, lane, axis=1), found)
    return found


def rows_below(slots, bound):
    return jnp.sum((slots < bound).astype(jnp.float32)).astype(jnp.int32)


def plan_kernel(per_owner, limit, assign_ref, table_ref, slot_ref, start_ref):
    slots = look_up(table_ref, assign_ref[...])
    slot_ref[...] = slots
    for owner in range(start_ref.shape[0]):
        start_ref[owner] = jnp.minimum(rows_below(slots, owner * per_owner), limit)


def make_plan(assign_rows, table, owner_count, per_owner, limit):
    return pl.pallas_call(
        functools.partial(plan_kernel, per_owner, limit),
        out_shape=(
            jax.ShapeDtypeStruct(assign_rows.shape, jnp.int32),
            jax.ShapeDtypeStruct((owner_count,), jnp.int32),
        ),
        in_specs=[in_vmem, in_vmem],
        out_specs=(in_vmem, in_smem),
        compiler_params=params(),
        name="plan",
    )(assign_rows, table)


def unit_kernel(steps, start_ref, owner_ref, rows_ref, unit_ref, held, sem):
    capacity = unit_ref.shape[0]
    row_count = rows_ref.shape[0]
    part = capacity // steps
    window = part + SUBLANES
    start = start_ref[owner_ref[0]]

    def first(step):
        begin = start + step * part
        aligned = jnp.minimum(begin // SUBLANES * SUBLANES, row_count - window)
        return pl.multiple_of(aligned, SUBLANES)

    copies = [
        pltpu.make_async_copy(rows_ref.at[pl.ds(first(step), window), :], held.at[step], sem.at[step])
        for step in range(steps)
    ]
    for copy in copies:
        copy.start()
    for step in range(steps):
        copies[step].wait()
        shift = start + step * part - first(step)
        groups = held[step].reshape(window // SUBLANES, SUBLANES, -1)
        turned = pltpu.roll(groups, SUBLANES - shift, 1)
        line = lax.broadcasted_iota(jnp.int32, (part // SUBLANES, SUBLANES, groups.shape[2]), 1)
        values = jnp.where(line < SUBLANES - shift, turned[:-1], turned[1:]).reshape(part, -1)
        scale = lax.rsqrt(jnp.sum(values * values, -1, keepdims=True) + epsilon)
        unit_ref[step * part : (step + 1) * part, :] = (values * scale).astype(jnp.bfloat16)


def unit_chunk(starts, owner, embeddings, capacity):
    width = embeddings.shape[1]
    steps = 5 if capacity % 80 == 0 and capacity >= 320 else 1
    part = capacity // steps
    return pl.pallas_call(
        functools.partial(unit_kernel, steps),
        out_shape=jax.ShapeDtypeStruct((capacity, width), jnp.bfloat16),
        in_specs=[in_smem, in_smem, anywhere],
        out_specs=in_vmem,
        scratch_shapes=[
            pltpu.VMEM((steps, part + SUBLANES, width), jnp.float32),
            pltpu.SemaphoreType.DMA((steps,)),
        ],
        compiler_params=params(),
        cost_estimate=pl.CostEstimate(
            flops=4 * capacity * width, bytes_accessed=6 * capacity * width, transcendentals=capacity
        ),
        name="unit",
    )(starts, owner, embeddings)


def aligned_start(start, row_count, window):
    begin = jnp.minimum(jnp.left_shift(jnp.right_shift(start, 3), 3), row_count - window)
    return pl.multiple_of(begin, SUBLANES)


def flat_window(held, start, rows):
    span = round_up(rows + 1, SUBLANES)
    shift = jnp.bitwise_and(start, LANES - 1)
    block = held[pl.ds(jnp.right_shift(start, 7), span), :]
    turned = pltpu.roll(block, jnp.bitwise_and(LANES - shift, LANES - 1), 1)
    following = pltpu.roll(turned, span - 1, 0)
    lane = lax.broadcasted_iota(jnp.int32, block.shape, 1)
    return jnp.where(lane < LANES - shift, turned, following)


def window_labels(held, slots, owner, start, per_owner, capacity, blocks):
    low = owner * per_owner
    mine = (slots >= low) & (slots < low + per_owner)
    held[: slots.shape[0], :] = jnp.where(mine, slots - low, -1)
    labels = flat_window(held, start, blocks)
    place = lax.broadcasted_iota(jnp.int32, labels.shape, 0) * LANES + lax.broadcasted_iota(
        jnp.int32, labels.shape, 1
    )
    return jnp.where(place < capacity, labels, -1)


def label_kernel(
    per_owner, limit, capacity, order_ref, me_ref, start_ref, slot_ref, group_ref, table_ref,
    sent_ref, row_ref, column_ref, tally_ref, held,
):
    source_count, padded = row_ref.shape
    blocks = padded // LANES
    held[...] = jnp.full(held.shape, -1, jnp.int32)
    slots = slot_ref[...]
    window = capacity + SUBLANES
    for owner in range(source_count):
        start = aligned_start(start_ref[owner], slots.size, window)
        wide = sent_ref.shape[1] // LANES
        labels = window_labels(held, slots, owner, start, per_owner, window, wide)
        for block in range(wide):
            sent_ref[owner : owner + 1, block * LANES : (block + 1) * LANES] = labels[block : block + 1, :]
    me = me_ref[0]
    tally = jnp.zeros(tally_ref.shape, jnp.float32)
    cluster = lax.broadcasted_iota(jnp.int32, tally.shape, 0)
    for place in range(source_count):
        slots = look_up(table_ref, group_ref[order_ref[place]])
        start = jnp.minimum(rows_below(slots, me * per_owner), limit)
        labels = window_labels(held, slots, me, start, per_owner, capacity, blocks)
        for block in range(blocks):
            row = labels[block : block + 1, :]
            spread = jnp.broadcast_to(row, (LANES, LANES))
            row_ref[place : place + 1, block * LANES : (block + 1) * LANES] = row
            column_ref[place, block * LANES : (block + 1) * LANES, :] = spread.T
            tally += (jnp.broadcast_to(row, tally.shape) == cluster).astype(jnp.float32)
    tally_ref[...] = jnp.broadcast_to(jnp.sum(tally, 1, keepdims=True), tally_ref.shape)


def make_labels(order, me, starts, slots, group_assign, table, per_owner, limit, capacity, padded):
    source_count = group_assign.shape[0]
    return pl.pallas_call(
        functools.partial(label_kernel, per_owner, limit, capacity),
        out_shape=(
            jax.ShapeDtypeStruct((source_count, round_up(capacity + SUBLANES, LANES)), jnp.int32),
            jax.ShapeDtypeStruct((source_count, padded), jnp.int32),
            jax.ShapeDtypeStruct((source_count, padded, LANES), jnp.int32),
            jax.ShapeDtypeStruct((per_owner, LANES), jnp.float32),
        ),
        in_specs=[in_smem, in_smem, in_smem, in_vmem, in_vmem, in_vmem],
        out_specs=(in_vmem, in_vmem, in_vmem, in_vmem),
        scratch_shapes=[pltpu.VMEM((slots.shape[0] + 2 * SUBLANES, LANES), jnp.int32)],
        compiler_params=params(),
        name="labels",
    )(order, me, starts, slots, group_assign, table)


def sum_kernel(start_ref, label_ref, rows_ref, sum_ref, held, sem):
    owner_count, per_owner, _ = sum_ref.shape
    window = held.shape[1]

    def copy(owner, slot):
        first = aligned_start(start_ref[owner], rows_ref.shape[0], window)
        return pltpu.make_async_copy(rows_ref.at[pl.ds(first, window), :], held.at[slot], sem.at[slot])

    copy(0, 0).start()

    def body(owner, carry):
        slot = lax.rem(owner, 2)

        @pl.when(owner + 1 < owner_count)
        def _():
            copy(owner + 1, 1 - slot).start()

        copy(owner, slot).wait()
        labels = label_ref[pl.ds(owner, 1), :][:, :window]
        cluster = lax.broadcasted_iota(jnp.int32, (per_owner, window), 0)
        member = (labels == cluster).astype(jnp.float32).astype(jnp.bfloat16)
        values = held[slot]
        high = values.astype(jnp.bfloat16)
        rest = values - high.astype(jnp.float32)
        middle = rest.astype(jnp.bfloat16)
        low = (rest - middle.astype(jnp.float32)).astype(jnp.bfloat16)
        total = jnp.dot(member, high, preferred_element_type=jnp.float32)
        total += jnp.dot(member, middle, preferred_element_type=jnp.float32)
        total += jnp.dot(member, low, preferred_element_type=jnp.float32)
        sum_ref[pl.ds(owner, 1)] = total[None]
        return carry

    lax.fori_loop(0, owner_count, body, 0)


def slot_sums(starts, sent_labels, embeddings, per_owner, capacity):
    owner_count = sent_labels.shape[0]
    width = embeddings.shape[1]
    return pl.pallas_call(
        sum_kernel,
        out_shape=jax.ShapeDtypeStruct((owner_count, per_owner, width), jnp.float32),
        in_specs=[in_smem, in_vmem, anywhere],
        out_specs=in_vmem,
        scratch_shapes=[
            pltpu.VMEM((2, capacity + SUBLANES, width), jnp.float32),
            pltpu.SemaphoreType.DMA((2,)),
        ],
        compiler_params=params(),
        cost_estimate=pl.CostEstimate(
            flops=6 * owner_count * per_owner * capacity * width,
            bytes_accessed=4 * embeddings.size,
            transcendentals=0,
        ),
        name="sums",
    )(starts, sent_labels, embeddings)


def gram_kernel(count, capacity, row_ref, column_ref, best_ref, *refs):
    chunks, out_ref, held, best, sem = refs[:count], *refs[count:]
    padded = held.shape[1]
    last = count - 1
    copies = [
        pltpu.make_async_copy(chunks[place], held.at[place, pl.ds(0, capacity), :], sem.at[place])
        for place in range(count)
    ]
    for place in (last, *range(last)):
        copies[place].start()
    if capacity < padded:
        for place in range(count):
            held[place, capacity:, :] = jnp.zeros((padded - capacity, held.shape[2]), held.dtype)
    out_ref[...] = best_ref[...]
    labels = column_ref[0]
    spread = jnp.concatenate([labels] * (padded // LANES), 1)

    def similarity(place):
        return lax.dot_general(
            held[last], held[place], (((1,), (1,)), ((), ())), preferred_element_type=jnp.float32
        )

    copies[last].wait()
    row = lax.broadcasted_iota(jnp.int32, (padded, padded), 0)
    column = lax.broadcasted_iota(jnp.int32, (padded, padded), 1)
    allowed = (spread == row_ref[last : last + 1, :]) & (row != column)
    nearest = jnp.max(jnp.where(allowed, similarity(last), -2.0), 0, keepdims=True)
    best[...] = jnp.full(best.shape, -2.0, jnp.float32)
    for place in range(last):
        copies[place].wait()

    def body(place, carry):
        near = jnp.where(spread == row_ref[pl.ds(place, 1), :], similarity(place), -2.0)
        out_ref[pl.ds(place, 1), :] = jnp.maximum(
            out_ref[pl.ds(place, 1), :], jnp.max(near, 0, keepdims=True)
        )
        folded = best[...]
        for block in range(padded // LANES):
            folded = jnp.maximum(folded, near[:, block * LANES : (block + 1) * LANES])
        best[...] = folded
        return carry

    if last:
        lax.fori_loop(0, last, body, 0)
        for block in range(padded // LANES):
            part = slice(block * LANES, (block + 1) * LANES)
            other = jnp.max(best[part, :].T, 0, keepdims=True)
            out_ref[last : last + 1, part] = jnp.maximum(nearest[:, part], other)
    else:
        out_ref[last : last + 1, :] = nearest


def gram_step(rows, columns, best, chunks, capacity):
    count = len(chunks)
    padded = rows.shape[1]
    width = chunks[0].shape[1]
    last = count - 1
    return pl.pallas_call(
        functools.partial(gram_kernel, count, capacity),
        out_shape=jax.ShapeDtypeStruct(best.shape, jnp.float32),
        grid=(1,),
        in_specs=[
            pl.BlockSpec(rows.shape, lambda step: (0, 0)),
            pl.BlockSpec((1, padded, LANES), lambda step: (last, 0, 0)),
            pl.BlockSpec(best.shape, lambda step: (0, 0)),
        ]
        + [anywhere] * count,
        out_specs=pl.BlockSpec(best.shape, lambda step: (0, 0)),
        scratch_shapes=[
            pltpu.VMEM((count, padded, width), jnp.bfloat16),
            pltpu.VMEM((padded, LANES), jnp.float32),
            pltpu.SemaphoreType.DMA((count,)),
        ],
        compiler_params=params(),
        cost_estimate=pl.CostEstimate(
            flops=2 * count * padded * padded * width,
            bytes_accessed=2 * count * capacity * width,
            transcendentals=0,
        ),
        name="gram",
    )(rows, columns, best, *chunks)


def centroid_kernel(sum_ref, tally_ref, centroid_ref, unit_ref):
    tally = jnp.concatenate([tally_ref[...]] * (sum_ref.shape[1] // LANES), 1)
    centroids = sum_ref[...] / tally
    centroid_ref[...] = centroids
    scale = lax.rsqrt(jnp.sum(centroids * centroids, -1, keepdims=True) + epsilon)
    unit_ref[...] = (centroids * scale).astype(jnp.bfloat16)


def make_centroids(sums, tally):
    return pl.pallas_call(
        centroid_kernel,
        out_shape=(
            jax.ShapeDtypeStruct(sums.shape, jnp.float32),
            jax.ShapeDtypeStruct(sums.shape, jnp.bfloat16),
        ),
        in_specs=[in_vmem, in_vmem],
        out_specs=(in_vmem, in_vmem),
        compiler_params=params(),
        name="centroids",
    )(sums, tally)


def cosine_kernel(order_ref, row_ref, best_ref, centroid_ref, *refs):
    count = row_ref.shape[0]
    chunks, out_ref = refs[:count], refs[count]
    capacity = chunks[0].shape[0]
    for place in range(count):
        products = lax.dot_general(
            centroid_ref[...], chunks[place][...], (((1,), (1,)), ((), ())), preferred_element_type=jnp.float32
        )
        cluster = lax.broadcasted_iota(jnp.int32, products.shape, 0)
        mine = row_ref[place : place + 1, :][:, :capacity] == cluster
        cosine = jnp.sum(jnp.where(mine, products, 0.0), 0, keepdims=True)
        source = order_ref[place]
        out_ref[source, 0:1, :] = best_ref[place : place + 1, :]
        if capacity < row_ref.shape[1]:
            out_ref[source, 1:2, :] = jnp.zeros((1, row_ref.shape[1]), jnp.float32)
        out_ref[source, 1:2, :capacity] = cosine


def make_cosines(order, rows, best, centroid_unit, chunks):
    count, padded = rows.shape
    return pl.pallas_call(
        cosine_kernel,
        out_shape=jax.ShapeDtypeStruct((count, 2, padded), jnp.float32),
        in_specs=[in_smem] + [in_vmem] * (3 + count),
        out_specs=in_vmem,
        compiler_params=params(),
        name="cosines",
    )(order, rows, best, centroid_unit, *chunks)


def place_kernel(per_owner, start_ref, slot_ref, back_ref, near_ref, cosine_ref, held, lines, result):
    owner_count, _, padded = back_ref.shape
    blocks = padded // LANES
    rows = slot_ref.shape[0]
    span = round_up(blocks + 1, SUBLANES)
    held[...] = jnp.full(held.shape, -1, jnp.int32)
    held[:rows, :] = slot_ref[...]
    result[...] = jnp.zeros(result.shape, jnp.float32)
    lines[...] = jnp.zeros(lines.shape, jnp.float32)
    lane = lax.broadcasted_iota(jnp.int32, (span, LANES), 1)
    for owner in range(owner_count):
        start = start_ref[owner]
        first = pl.ds(jnp.right_shift(start, 7), span)
        shift = jnp.bitwise_and(start, LANES - 1)
        slots = held[first, :]
        mine = (slots >= owner * per_owner) & (slots < (owner + 1) * per_owner)
        for kind in range(2):
            for block in range(blocks):
                lines[block : block + 1, :] = back_ref[owner, kind : kind + 1, block * LANES : (block + 1) * LANES]
            turned = pltpu.roll(lines[...], shift, 1)
            earlier = pltpu.roll(turned, 1, 0)
            moved = jnp.where(lane >= shift, turned, earlier)
            result[kind, first, :] = jnp.where(mine, moved, result[kind, first, :])
    near_ref[...] = result[0, :rows, :]
    cosine_ref[...] = result[1, :rows, :]


def place_rows(starts, slots, back, per_owner):
    padded = back.shape[2]
    span = round_up(padded // LANES + 1, SUBLANES)
    rows = slots.shape[0]
    return pl.pallas_call(
        functools.partial(place_kernel, per_owner),
        out_shape=(jax.ShapeDtypeStruct(slots.shape, jnp.float32),) * 2,
        in_specs=[in_smem, in_vmem, in_vmem],
        out_specs=(in_vmem, in_vmem),
        scratch_shapes=[
            pltpu.VMEM((rows + span, LANES), jnp.int32),
            pltpu.VMEM((span, LANES), jnp.float32),
            pltpu.VMEM((2, rows + span, LANES), jnp.float32),
        ],
        compiler_params=params(),
        name="place",
    )(starts, slots, back)


def turns(count):
    return sorted(range(count), key=lambda turn: (turn != 0, abs(turn - count // 2), turn))


def per_device(embeddings, assign, cluster_slot):
    row_count, width = embeddings.shape
    owner_count = lax.axis_size("docs")
    group_count = lax.axis_size("grp")
    per_owner = cluster_slot.shape[0] // owner_count
    capacity = row_count // owner_count + row_count // (4 * owner_count)
    padded = round_up(capacity, LANES)
    limit = row_count - capacity
    me = lax.axis_index("docs").astype(jnp.int32)
    order_of = turns(owner_count)

    assign_rows = assign.reshape(-1, LANES)
    table = cluster_slot.reshape(-1, LANES)
    group_assign = lax.all_gather(assign_rows, "docs")
    slots, starts = make_plan(assign_rows, table, owner_count, per_owner, limit)

    chunks = {}
    for turn in order_of[1:] + order_of[:1]:
        owner = lax.rem(me + turn, owner_count).reshape(1)
        chunk = unit_chunk(starts, owner, embeddings, capacity)
        if turn:
            pairs = [(i, (i + turn) % owner_count) for i in range(owner_count)]
            chunk = lax.ppermute(chunk, "docs", pairs)
        chunks[turn] = chunk
    arrived = [chunks[turn] for turn in order_of]
    order = jnp.stack([lax.rem(me + owner_count - turn, owner_count) for turn in order_of])

    sent_labels, rows, columns, group_tally = make_labels(
        order, me.reshape(1), starts, slots, group_assign, table, per_owner, limit, capacity, padded
    )
    partial_sums = slot_sums(starts, sent_labels, embeddings, per_owner, capacity)
    share = lax.psum_scatter(partial_sums, "grp", scatter_dimension=1, tiled=True)
    share = lax.psum_scatter(share, "docs", scatter_dimension=0, tiled=True)[0]
    sums = lax.all_gather(share, "grp", axis=0, tiled=True)
    tally = lax.psum(group_tally, "grp")
    centroids, centroid_unit = make_centroids(sums, tally)

    best = jnp.full((owner_count, padded), -2.0, jnp.float32)
    for count in range(1, owner_count + 1):
        best = gram_step(rows, columns, best, arrived[:count], capacity)
    results = make_cosines(order, rows, best, centroid_unit, arrived)
    back = lax.all_to_all(results, "docs", split_axis=0, concat_axis=0, tiled=True)
    near, cosine = place_rows(starts, slots, back, per_owner)
    return (centroids, near.reshape(-1), cosine.reshape(-1))


def solution(mesh):
    placed = (P(("grp", "docs"), None), P(("grp", "docs")), P())
    return jax.shard_map(
        per_device,
        mesh=mesh,
        in_specs=placed,
        out_specs=(P("docs", None), P(("grp", "docs")), P(("grp", "docs"))),
        check_vma=False,
    )
```

```python
import functools

import jax
import jax.numpy as jnp
from jax import lax
from jax.experimental import pallas as pl
from jax.experimental.pallas import tpu as pltpu
from jax.sharding import PartitionSpec as P

epsilon = 1e-06
LANES = 128
SUBLANES = 8
VMEM_BYTES = 48 * 1024 * 1024
in_vmem = pl.BlockSpec(memory_space=pltpu.VMEM)
in_smem = pl.BlockSpec(memory_space=pltpu.SMEM)
anywhere = pl.BlockSpec(memory_space=pl.ANY)


def round_up(value, step):
    return -(-value // step) * step


def params(**extra):
    return pltpu.CompilerParams(vmem_limit_bytes=VMEM_BYTES, **extra)


def look_up(table_ref, index):
    lane = jnp.bitwise_and(index, LANES - 1)
    row = jnp.right_shift(index, 7)
    found = jnp.zeros(index.shape, jnp.int32)
    for part in range(table_ref.shape[0]):
        entries = jnp.broadcast_to(table_ref[part : part + 1, :], index.shape)
        found = jnp.where(row == part, jnp.take_along_axis(entries, lane, axis=1), found)
    return found


def rows_below(slots, bound):
    return jnp.sum((slots < bound).astype(jnp.float32)).astype(jnp.int32)


def plan_kernel(per_owner, limit, assign_ref, table_ref, slot_ref, start_ref):
    slots = look_up(table_ref, assign_ref[...])
    slot_ref[...] = slots
    for owner in range(start_ref.shape[0]):
        start_ref[owner] = jnp.minimum(rows_below(slots, owner * per_owner), limit)


def make_plan(assign_rows, table, owner_count, per_owner, limit):
    return pl.pallas_call(
        functools.partial(plan_kernel, per_owner, limit),
        out_shape=(
            jax.ShapeDtypeStruct(assign_rows.shape, jnp.int32),
            jax.ShapeDtypeStruct((owner_count,), jnp.int32),
        ),
        in_specs=[in_vmem, in_vmem],
        out_specs=(in_vmem, in_smem),
        compiler_params=params(),
        name="plan",
    )(assign_rows, table)


def unit_kernel(steps, offset, start_ref, owner_ref, rows_ref, *refs):
    unit_ref, held, sem = refs[-3:]
    part = unit_ref.shape[0] // steps
    window = part + SUBLANES
    start = start_ref[owner_ref[0]] + offset

    def first(step):
        return aligned_start(start + step * part, rows_ref.shape[0], window)

    copies = [
        pltpu.make_async_copy(rows_ref.at[pl.ds(first(step), window), :], held.at[step], sem.at[step])
        for step in range(steps)
    ]
    for copy in copies:
        copy.start()
    for step in range(steps):
        copies[step].wait()
        shift = start + step * part - first(step)
        groups = held[step].reshape(window // SUBLANES, SUBLANES, -1)
        turned = pltpu.roll(groups, SUBLANES - shift, 1)
        line = lax.broadcasted_iota(jnp.int32, (part // SUBLANES, SUBLANES, groups.shape[2]), 1)
        values = jnp.where(line < SUBLANES - shift, turned[:-1], turned[1:]).reshape(part, -1)
        scale = lax.rsqrt(jnp.sum(values * values, -1, keepdims=True) + epsilon)
        unit_ref[step * part : (step + 1) * part, :] = (values * scale).astype(jnp.bfloat16)


def unit_piece(starts, owner, embeddings, offset, rows, after):
    width = embeddings.shape[1]
    steps = rows // LANES if rows % LANES == 0 else 1
    return pl.pallas_call(
        functools.partial(unit_kernel, steps, offset),
        out_shape=jax.ShapeDtypeStruct((rows, width), jnp.bfloat16),
        in_specs=[in_smem, in_smem, anywhere] + [anywhere] * len(after),
        out_specs=in_vmem,
        scratch_shapes=[
            pltpu.VMEM((steps, rows // steps + SUBLANES, width), jnp.float32),
            pltpu.SemaphoreType.DMA((steps,)),
        ],
        compiler_params=params(),
        cost_estimate=pl.CostEstimate(
            flops=4 * rows * width, bytes_accessed=6 * rows * width, transcendentals=rows
        ),
        name="unit",
    )(starts, owner, embeddings, *after)


def hold_until(values, arrived):
    def nothing(*refs):
        pass

    return pl.pallas_call(
        nothing,
        out_shape=jax.ShapeDtypeStruct(values.shape, values.dtype),
        in_specs=[anywhere] * (1 + len(arrived)),
        out_specs=anywhere,
        input_output_aliases={0: 0},
        compiler_params=params(),
        name="hold",
    )(values, *arrived)


def aligned_start(start, row_count, window):
    begin = jnp.minimum(jnp.left_shift(jnp.right_shift(start, 3), 3), row_count - window)
    return pl.multiple_of(begin, SUBLANES)


def flat_window(held, start, rows):
    span = round_up(rows + 1, SUBLANES)
    shift = jnp.bitwise_and(start, LANES - 1)
    block = held[pl.ds(jnp.right_shift(start, 7), span), :]
    turned = pltpu.roll(block, jnp.bitwise_and(LANES - shift, LANES - 1), 1)
    following = pltpu.roll(turned, span - 1, 0)
    lane = lax.broadcasted_iota(jnp.int32, block.shape, 1)
    return jnp.where(lane < LANES - shift, turned, following)


def window_labels(held, slots, owner, start, per_owner, capacity, blocks):
    low = owner * per_owner
    mine = (slots >= low) & (slots < low + per_owner)
    held[: slots.shape[0], :] = jnp.where(mine, slots - low, -1)
    labels = flat_window(held, start, blocks)
    place = lax.broadcasted_iota(jnp.int32, labels.shape, 0) * LANES + lax.broadcasted_iota(
        jnp.int32, labels.shape, 1
    )
    return jnp.where(place < capacity, labels, -1)


def sent_kernel(per_owner, capacity, start_ref, slot_ref, sum_ref, sent_ref, held):
    owner_count, padded = sent_ref.shape
    held[...] = jnp.full(held.shape, -1, jnp.int32)
    slots = slot_ref[...]
    window = capacity + SUBLANES
    for owner in range(owner_count):
        aligned = aligned_start(start_ref[owner], slots.size, window)
        for ref, start, length in ((sum_ref, aligned, window), (sent_ref, start_ref[owner], capacity)):
            blocks = ref.shape[1] // LANES
            labels = window_labels(held, slots, owner, start, per_owner, length, blocks)
            for block in range(blocks):
                ref[owner : owner + 1, block * LANES : (block + 1) * LANES] = labels[block : block + 1, :]


def sent_labels(starts, slots, owner_count, per_owner, capacity, padded):
    return pl.pallas_call(
        functools.partial(sent_kernel, per_owner, capacity),
        out_shape=(
            jax.ShapeDtypeStruct((owner_count, round_up(capacity + SUBLANES, LANES)), jnp.int32),
            jax.ShapeDtypeStruct((owner_count, padded), jnp.int32),
        ),
        in_specs=[in_smem, in_vmem],
        out_specs=(in_vmem, in_vmem),
        scratch_shapes=[pltpu.VMEM((slots.shape[0] + 2 * SUBLANES, LANES), jnp.int32)],
        compiler_params=params(),
        name="sent",
    )(starts, slots)


def arrived_kernel(order_ref, got_ref, row_ref, column_ref, tally_ref):
    place_count, padded = row_ref.shape
    tally = jnp.zeros((LANES, LANES), jnp.float32)
    cluster = lax.broadcasted_iota(jnp.int32, tally.shape, 0)
    for place in range(place_count):
        row_ref[place : place + 1, :] = got_ref[pl.ds(order_ref[place], 1), :]
        for block in range(padded // LANES):
            part = slice(block * LANES, (block + 1) * LANES)
            spread = jnp.broadcast_to(row_ref[place : place + 1, part], tally.shape)
            column_ref[place, part, :] = spread.T
            tally += (spread == cluster).astype(jnp.float32)
    total = jnp.broadcast_to(jnp.sum(tally, 1, keepdims=True), tally.shape)
    tally_ref[...] = jnp.zeros(tally_ref.shape, jnp.float32)
    tally_ref[:, :LANES] = total.T[:SUBLANES, :]


def arrived_labels(order, got, width):
    place_count, padded = got.shape
    return pl.pallas_call(
        arrived_kernel,
        out_shape=(
            jax.ShapeDtypeStruct(got.shape, jnp.int32),
            jax.ShapeDtypeStruct((place_count, padded, LANES), jnp.int32),
            jax.ShapeDtypeStruct((SUBLANES, width), jnp.float32),
        ),
        in_specs=[in_smem, in_vmem],
        out_specs=(in_vmem, in_vmem, in_vmem),
        compiler_params=params(),
        name="arrived",
    )(order, got)


def sum_kernel(start_ref, label_ref, rows_ref, *refs):
    sum_ref, held, sem = refs[-3:]
    owner_count, per_owner, _ = sum_ref.shape
    window = held.shape[1]

    def copy(owner, slot):
        first = aligned_start(start_ref[owner], rows_ref.shape[0], window)
        return pltpu.make_async_copy(rows_ref.at[pl.ds(first, window), :], held.at[slot], sem.at[slot])

    copy(0, 0).start()

    def body(owner, carry):
        slot = lax.rem(owner, 2)

        @pl.when(owner + 1 < owner_count)
        def _():
            copy(owner + 1, 1 - slot).start()

        copy(owner, slot).wait()
        labels = label_ref[pl.ds(owner, 1), :][:, :window]
        cluster = lax.broadcasted_iota(jnp.int32, (per_owner, window), 0)
        member = (labels == cluster).astype(jnp.float32).astype(jnp.bfloat16)
        values = held[slot]
        high = values.astype(jnp.bfloat16)
        rest = values - high.astype(jnp.float32)
        middle = rest.astype(jnp.bfloat16)
        low = (rest - middle.astype(jnp.float32)).astype(jnp.bfloat16)
        total = jnp.dot(member, high, preferred_element_type=jnp.float32)
        total += jnp.dot(member, middle, preferred_element_type=jnp.float32)
        total += jnp.dot(member, low, preferred_element_type=jnp.float32)
        sum_ref[pl.ds(owner, 1)] = total[None]
        return carry

    lax.fori_loop(0, owner_count, body, 0)


def slot_sums(starts, labels, embeddings, per_owner, capacity, after):
    owner_count = labels.shape[0]
    width = embeddings.shape[1]
    return pl.pallas_call(
        sum_kernel,
        out_shape=jax.ShapeDtypeStruct((owner_count, per_owner, width), jnp.float32),
        in_specs=[in_smem, in_vmem, anywhere] + [anywhere] * len(after),
        out_specs=in_vmem,
        scratch_shapes=[
            pltpu.VMEM((2, capacity + SUBLANES, width), jnp.float32),
            pltpu.SemaphoreType.DMA((2,)),
        ],
        compiler_params=params(),
        cost_estimate=pl.CostEstimate(
            flops=6 * owner_count * per_owner * capacity * width,
            bytes_accessed=4 * embeddings.size,
            transcendentals=0,
        ),
        name="sums",
    )(starts, labels, embeddings, *after)


def gram_kernel(pieces, counts, row_ref, column_ref, best_ref, *refs):
    piece_count, extra_count, is_final = counts
    chunks, refs = refs[:piece_count], refs[piece_count + extra_count :]
    if is_final:
        order_ref, cosine_ref, centroid_ref, result_ref, *refs = refs
        out_ref = refs.pop()
    else:
        out_ref, *refs = refs
    held, mine, other, best, sem = refs
    place, offset, rows = pieces[-1]
    wide = mine.shape[0]
    whole = [index for index, piece in enumerate(pieces[:-1]) if piece[0] != place]
    before = [index for index, piece in enumerate(pieces[:-1]) if piece[0] == place]
    copies = [pltpu.make_async_copy(chunks[-1], mine.at[pl.ds(0, rows), :], sem.at[piece_count - 1])]
    for index in whole:
        target = held.at[index, pl.ds(0, pieces[index][2]), :]
        copies.append(pltpu.make_async_copy(chunks[index], target, sem.at[index]))
    for index in before:
        copies.append(pltpu.make_async_copy(chunks[index], other, sem.at[index]))
    for copy in copies:
        copy.start()
    if rows < wide:
        mine[rows:, :] = jnp.zeros((wide - rows, mine.shape[1]), mine.dtype)
    for index in whole:
        length = pieces[index][2]
        if length < held.shape[1]:
            held[index, length:, :] = jnp.zeros((held.shape[1] - length, held.shape[2]), held.dtype)
    out_ref[...] = best_ref[...]
    labels = column_ref[0, offset : offset + wide, :]
    here = slice(offset, offset + wide)

    def similarity(against):
        return lax.dot_general(
            mine[...], against, (((1,), (1,)), ((), ())), preferred_element_type=jnp.float32
        )

    def spread(length):
        return jnp.concatenate([labels] * (length // LANES), 1)

    def fold(near):
        folded = best[...]
        for block in range(near.shape[1] // LANES):
            folded = jnp.maximum(folded, near[:, block * LANES : (block + 1) * LANES])
        best[...] = folded

    copies[0].wait()
    row = lax.broadcasted_iota(jnp.int32, (wide, wide), 0)
    column = lax.broadcasted_iota(jnp.int32, (wide, wide), 1)
    allowed = (spread(wide) == row_ref[place : place + 1, here]) & (row != column)
    nearest = jnp.max(jnp.where(allowed, similarity(mine[...]), -2.0), 0, keepdims=True)
    best[...] = jnp.full(best.shape, -2.0, jnp.float32)

    def against_whole(index, carry):
        pltpu.make_async_copy(
            chunks[0], held.at[index, pl.ds(0, pieces[0][2]), :], sem.at[index]
        ).wait()
        near = jnp.where(
            spread(held.shape[1]) == row_ref[pl.ds(index, 1), :], similarity(held[index]), -2.0
        )
        out_ref[pl.ds(index, 1), :] = jnp.maximum(
            out_ref[pl.ds(index, 1), :], jnp.max(near, 0, keepdims=True)
        )
        fold(near)
        return carry

    if len(whole) <= 8:
        for index in whole:
            against_whole(index, 0)
    else:
        lax.fori_loop(0, len(whole), against_whole, 0)
    for index in before:
        _, begin, length = pieces[index]
        there = slice(begin, begin + length)
        pltpu.make_async_copy(chunks[index], other, sem.at[index]).wait()
        near = jnp.where(spread(length) == row_ref[place : place + 1, there], similarity(other[...]), -2.0)
        out_ref[place : place + 1, there] = jnp.maximum(
            out_ref[place : place + 1, there], jnp.max(near, 0, keepdims=True)
        )
        fold(near)
    if len(pieces) > 1:
        sides = [
            jnp.max(best[block * LANES : (block + 1) * LANES, :].T, 0, keepdims=True)
            for block in range(wide // LANES)
        ]
        nearest = jnp.maximum(nearest, jnp.concatenate(sides, 1))
    out_ref[place : place + 1, here] = nearest
    if is_final:
        own = cosines_of(centroid_ref[...], mine[...], row_ref[place : place + 1, here])
        for index in range(row_ref.shape[0]):
            source = order_ref[index]
            result_ref[source, 0:1, :] = out_ref[index : index + 1, :]
            result_ref[source, 1:2, :] = cosine_ref[index : index + 1, :]
            if index == place:
                result_ref[source, 1:2, here] = own


def gram_step(rows, columns, best, pieces, chunks, after=(), final=None):
    places, padded = rows.shape
    width = chunks[0].shape[1]
    place, _, length = pieces[-1]
    wide = round_up(length, LANES)
    whole = sum(piece[0] != place for piece in pieces)
    before = [piece[2] for piece in pieces[:-1] if piece[0] == place]
    in_specs = [
        pl.BlockSpec(rows.shape, lambda step: (0, 0)),
        pl.BlockSpec((1, padded, LANES), lambda step: (place, 0, 0)),
        pl.BlockSpec(best.shape, lambda step: (0, 0)),
    ] + [anywhere] * (len(chunks) + len(after))
    best_shape = jax.ShapeDtypeStruct(best.shape, jnp.float32)
    scratch = [
        pltpu.VMEM((max(whole, 1), padded, width), jnp.bfloat16),
        pltpu.VMEM((wide, width), jnp.bfloat16),
        pltpu.VMEM((before[0] if before else SUBLANES * 2, width), jnp.bfloat16),
        pltpu.VMEM((wide, LANES), jnp.float32),
        pltpu.SemaphoreType.DMA((len(pieces),)),
    ]
    if final:
        order, cosines, centroid_unit = final
        in_specs += [
            in_smem,
            pl.BlockSpec(cosines.shape, lambda step: (0, 0)),
            pl.BlockSpec(centroid_unit.shape, lambda step: (0, 0)),
        ]
        out_shape = jax.ShapeDtypeStruct((places, 2, padded), jnp.float32)
        out_specs = pl.BlockSpec(out_shape.shape, lambda step: (0, 0, 0))
        scratch.append(pltpu.VMEM(best.shape, jnp.float32))
    else:
        out_shape, out_specs = best_shape, pl.BlockSpec(best.shape, lambda step: (0, 0))
    return pl.pallas_call(
        functools.partial(gram_kernel, pieces, (len(chunks), len(after), bool(final))),
        out_shape=out_shape,
        grid=(1,),
        in_specs=in_specs,
        out_specs=out_specs,
        scratch_shapes=scratch,
        compiler_params=params(),
        cost_estimate=pl.CostEstimate(
            flops=2 * padded * wide * width // 8,
            bytes_accessed=2 * padded * width // 8,
            transcendentals=0,
        ),
        name="gram",
    )(rows, columns, best, *chunks, *after, *(final or ()))


def pack_kernel(share_ref, tally_ref, after_ref, packed_ref):
    packed_ref[: share_ref.shape[0], :] = share_ref[...]
    packed_ref[share_ref.shape[0] :, :] = tally_ref[...]


def pack_share(share, tally, after):
    length = share.shape[0] + tally.shape[0]
    return pl.pallas_call(
        pack_kernel,
        out_shape=jax.ShapeDtypeStruct((length, share.shape[1]), jnp.float32),
        in_specs=[in_vmem, in_vmem, anywhere],
        out_specs=in_vmem,
        compiler_params=params(),
        name="pack",
    )(share, tally, after)


def centroid_kernel(gathered_ref, centroid_ref, unit_ref):
    groups, length, width = gathered_ref.shape
    share = length - SUBLANES
    per_owner = centroid_ref.shape[0]
    tally = jnp.sum(gathered_ref[:, share, :LANES], 0, keepdims=True)
    column = jnp.broadcast_to(tally, (LANES, LANES)).T[:per_owner, :]
    sums = jnp.concatenate([gathered_ref[group, :share, :] for group in range(groups)], 0)
    centroids = sums / jnp.concatenate([column] * (width // LANES), 1)
    centroid_ref[...] = centroids
    scale = lax.rsqrt(jnp.sum(centroids * centroids, -1, keepdims=True) + epsilon)
    unit_ref[...] = (centroids * scale).astype(jnp.bfloat16)


def make_centroids(gathered, per_owner):
    shape = (per_owner, gathered.shape[2])
    return pl.pallas_call(
        centroid_kernel,
        out_shape=(
            jax.ShapeDtypeStruct(shape, jnp.float32),
            jax.ShapeDtypeStruct(shape, jnp.bfloat16),
        ),
        in_specs=[in_vmem],
        out_specs=(in_vmem, in_vmem),
        compiler_params=params(),
        name="centroids",
    )(gathered)


def cosines_of(centroid_unit, units, labels):
    products = lax.dot_general(
        centroid_unit, units, (((1,), (1,)), ((), ())), preferred_element_type=jnp.float32
    )
    cluster = lax.broadcasted_iota(jnp.int32, products.shape, 0)
    return jnp.sum(jnp.where(labels == cluster, products, 0.0), 0, keepdims=True)


def cosine_kernel(pieces, row_ref, centroid_ref, *refs):
    chunks, out_ref = refs[:-1], refs[-1]
    out_ref[...] = jnp.zeros(out_ref.shape, jnp.float32)
    for (place, offset, length), chunk in zip(pieces, chunks):
        here = slice(offset, offset + length)
        out_ref[place : place + 1, here] = cosines_of(
            centroid_ref[...], chunk[...], row_ref[place : place + 1, here]
        )


def make_cosines(rows, centroid_unit, pieces, chunks):
    return pl.pallas_call(
        functools.partial(cosine_kernel, pieces),
        out_shape=jax.ShapeDtypeStruct(rows.shape, jnp.float32),
        in_specs=[in_vmem] * (2 + len(chunks)),
        out_specs=in_vmem,
        compiler_params=params(),
        cost_estimate=pl.CostEstimate(
            flops=2 * len(chunks) * rows.shape[1] * centroid_unit.size,
            bytes_accessed=2 * len(chunks) * rows.shape[1] * centroid_unit.shape[1],
            transcendentals=0,
        ),
        name="cosines",
    )(rows, centroid_unit, *chunks)


def place_kernel(per_owner, start_ref, slot_ref, back_ref, near_ref, cosine_ref, held, lines, result):
    owner_count, _, padded = back_ref.shape
    blocks = padded // LANES
    rows = slot_ref.shape[0]
    span = round_up(blocks + 1, SUBLANES)
    held[...] = jnp.full(held.shape, -1, jnp.int32)
    held[:rows, :] = slot_ref[...]
    result[...] = jnp.zeros(result.shape, jnp.float32)
    lines[...] = jnp.zeros(lines.shape, jnp.float32)
    lane = lax.broadcasted_iota(jnp.int32, (span, LANES), 1)
    for owner in range(owner_count):
        start = start_ref[owner]
        first = pl.ds(jnp.right_shift(start, 7), span)
        shift = jnp.bitwise_and(start, LANES - 1)
        slots = held[first, :]
        mine = (slots >= owner * per_owner) & (slots < (owner + 1) * per_owner)
        for kind in range(2):
            for block in range(blocks):
                lines[block : block + 1, :] = back_ref[owner, kind : kind + 1, block * LANES : (block + 1) * LANES]
            turned = pltpu.roll(lines[...], shift, 1)
            earlier = pltpu.roll(turned, 1, 0)
            moved = jnp.where(lane >= shift, turned, earlier)
            result[kind, first, :] = jnp.where(mine, moved, result[kind, first, :])
    near_ref[...] = result[0, :rows, :]
    cosine_ref[...] = result[1, :rows, :]


def place_rows(starts, slots, back, per_owner):
    padded = back.shape[2]
    span = round_up(padded // LANES + 1, SUBLANES)
    rows = slots.shape[0]
    return pl.pallas_call(
        functools.partial(place_kernel, per_owner),
        out_shape=(jax.ShapeDtypeStruct(slots.shape, jnp.float32),) * 2,
        in_specs=[in_smem, in_vmem, in_vmem],
        out_specs=(in_vmem, in_vmem),
        scratch_shapes=[
            pltpu.VMEM((rows + span, LANES), jnp.int32),
            pltpu.VMEM((span, LANES), jnp.float32),
            pltpu.VMEM((2, rows + span, LANES), jnp.float32),
        ],
        compiler_params=params(),
        name="place",
    )(starts, slots, back)


def turns(count):
    order = sorted(range(count), key=lambda turn: (min(turn, count - turn), turn))
    return order[:2] + order[3:4] + order[2:3] + order[4:]


IN_FLIGHT = 3


def per_device(embeddings, assign, cluster_slot):
    row_count, width = embeddings.shape
    owner_count = lax.axis_size("docs")
    per_owner = cluster_slot.shape[0] // owner_count
    capacity = row_count // owner_count + row_count // (4 * owner_count)
    padded = round_up(capacity, LANES)
    me = lax.axis_index("docs").astype(jnp.int32)
    order_of = turns(owner_count)
    order = jnp.stack([lax.rem(me + owner_count - turn, owner_count) for turn in order_of])

    pieces = [(place, 0, capacity) for place in range(owner_count - 1)]
    cut = round_up(capacity // 2, LANES) if capacity == padded else capacity
    pieces.append((owner_count - 1, 0, cut))
    if cut < capacity:
        pieces.append((owner_count - 1, cut, capacity - cut))

    slots, starts = make_plan(
        assign.reshape(-1, LANES), cluster_slot.reshape(-1, LANES), owner_count, per_owner, row_count - capacity
    )
    sum_labels, wire_labels = sent_labels(starts, slots, owner_count, per_owner, capacity, padded)
    got_labels = lax.all_to_all(wire_labels, "docs", split_axis=0, concat_axis=0, tiled=True)
    rows, columns, group_tally = arrived_labels(order, got_labels, width)

    chunks, sent = [], []
    bests = [jnp.full((owner_count, padded), -2.0, jnp.float32)]
    group_share = None

    def multiply(count):
        after = [group_share] if count == len(pieces) // 2 else []
        bests.append(gram_step(rows, columns, bests[-1], pieces[:count], chunks[:count], after))

    for index, (place, offset, length) in enumerate(pieces):
        turn = order_of[place]
        owner = lax.rem(me + turn, owner_count).reshape(1)
        after = []
        if index > IN_FLIGHT + 1:
            multiply(index - IN_FLIGHT - 1)
            after = [chunks[index - IN_FLIGHT], bests[-1]]
        piece = unit_piece(starts, owner, embeddings, offset, length, after)
        sent.append(piece)
        if turn:
            pairs = [(i, (i + turn) % owner_count) for i in range(owner_count)]
            piece = lax.ppermute(piece, "docs", pairs)
        chunks.append(piece)
        if index == IN_FLIGHT + 1:
            partial_sums = slot_sums(starts, sum_labels, embeddings, per_owner, capacity, sent)
            partial_sums = hold_until(partial_sums, chunks[1:IN_FLIGHT])
            group_share = lax.psum_scatter(partial_sums, "grp", scatter_dimension=1, tiled=True)
            share = lax.psum_scatter(group_share, "docs", scatter_dimension=0, tiled=True)[0]
    for count in range(max(len(pieces) - IN_FLIGHT - 1, 1), len(pieces)):
        multiply(count)
    packed = pack_share(share, group_tally, bests[max(len(pieces) - 3, 0)])
    centroids, centroid_unit = make_centroids(lax.all_gather(packed, "grp"), per_owner)
    cosines = make_cosines(rows, centroid_unit, pieces[:-1], chunks[:-1])
    results = gram_step(
        rows, columns, bests[-1], pieces, chunks, final=(order, cosines, centroid_unit)
    )
    back = lax.all_to_all(results, "docs", split_axis=0, concat_axis=0, tiled=True)
    near, cosine = place_rows(starts, slots, back, per_owner)
    return (centroids, near.reshape(-1), cosine.reshape(-1))


def solution(mesh):
    placed = (P(("grp", "docs"), None), P(("grp", "docs")), P())
    return jax.shard_map(
        per_device,
        mesh=mesh,
        in_specs=placed,
        out_specs=(P("docs", None), P(("grp", "docs")), P(("grp", "docs"))),
        check_vma=False,
    )
```

```python
import functools

import jax
import jax.numpy as jnp
from jax import lax
from jax.experimental import pallas as pl
from jax.experimental.pallas import tpu as pltpu
from jax.sharding import PartitionSpec as P

epsilon = 1e-06
LANES = 128
SUBLANES = 8
MIB = 1024 * 1024
TILE = 256
in_vmem = pl.BlockSpec(memory_space=pltpu.VMEM)
in_smem = pl.BlockSpec(memory_space=pltpu.SMEM)
anywhere = pl.BlockSpec(memory_space=pl.ANY)
brief = pl.CostEstimate(flops=1000, bytes_accessed=1000, transcendentals=0)


def round_up(value, step):
    return -(-value // step) * step


def params(mib=46):
    return pltpu.CompilerParams(vmem_limit_bytes=mib * MIB)


def look_up(table_ref, index):
    lane = jnp.bitwise_and(index, LANES - 1)
    row = jnp.right_shift(index, 7)
    found = jnp.zeros(index.shape, jnp.int32)
    for part in range(table_ref.shape[0]):
        entries = jnp.broadcast_to(table_ref[part : part + 1, :], index.shape)
        found = jnp.where(row == part, jnp.take_along_axis(entries, lane, axis=1), found)
    return found


def rows_below(slots, bound):
    return jnp.sum((slots < bound).astype(jnp.float32)).astype(jnp.int32)


def plan_kernel(per_owner, limit, assign_ref, table_ref, slot_ref, start_ref):
    slots = look_up(table_ref, assign_ref[...])
    slot_ref[...] = slots
    for owner in range(start_ref.shape[0]):
        start_ref[owner] = jnp.minimum(rows_below(slots, owner * per_owner), limit)


def make_plan(assign_rows, table, owner_count, per_owner, limit):
    return pl.pallas_call(
        functools.partial(plan_kernel, per_owner, limit),
        out_shape=(
            jax.ShapeDtypeStruct(assign_rows.shape, jnp.int32),
            jax.ShapeDtypeStruct((owner_count,), jnp.int32),
        ),
        in_specs=[in_vmem, in_vmem],
        out_specs=(in_vmem, in_smem),
        compiler_params=params(),
        name="plan",
    )(assign_rows, table)


def unit_kernel(steps, offset, turn, start_ref, me_ref, rows_ref, *refs):
    unit_ref, held, sem = refs[-3:]
    part = unit_ref.shape[0] // steps
    window = part + SUBLANES
    start = start_ref[lax.rem(me_ref[0] + turn, start_ref.shape[0])] + offset

    def first(step):
        return aligned_start(start + step * part, rows_ref.shape[0], window)

    copies = [
        pltpu.make_async_copy(rows_ref.at[pl.ds(first(step), window), :], held.at[step], sem.at[step])
        for step in range(steps)
    ]
    for copy in copies:
        copy.start()
    for step in range(steps):
        copies[step].wait()
        shift = start + step * part - first(step)
        groups = held[step].reshape(window // SUBLANES, SUBLANES, -1)
        turned = pltpu.roll(groups, SUBLANES - shift, 1)
        line = lax.broadcasted_iota(jnp.int32, (part // SUBLANES, SUBLANES, groups.shape[2]), 1)
        values = jnp.where(line < SUBLANES - shift, turned[:-1], turned[1:]).reshape(part, -1)
        scale = lax.rsqrt(jnp.sum(values * values, -1, keepdims=True) + epsilon)
        unit_ref[step * part : (step + 1) * part, :] = (values * scale).astype(jnp.bfloat16)


def unit_piece(starts, me, embeddings, turn, offset, rows, after):
    width = embeddings.shape[1]
    steps = rows // LANES if rows % LANES == 0 else 1
    return pl.pallas_call(
        functools.partial(unit_kernel, steps, offset, turn),
        out_shape=jax.ShapeDtypeStruct((rows, width), jnp.bfloat16),
        in_specs=[in_smem, in_smem, anywhere] + [anywhere] * len(after),
        out_specs=in_vmem,
        scratch_shapes=[
            pltpu.VMEM((steps, rows // steps + SUBLANES, width), jnp.float32),
            pltpu.SemaphoreType.DMA((steps,)),
        ],
        compiler_params=params(),
        cost_estimate=brief,
        name="unit",
    )(starts, me, embeddings, *after)


def hold_until(values, arrived):
    def nothing(*refs):
        pass

    return pl.pallas_call(
        nothing,
        out_shape=jax.ShapeDtypeStruct(values.shape, values.dtype),
        in_specs=[anywhere] * (1 + len(arrived)),
        out_specs=anywhere,
        input_output_aliases={0: 0},
        compiler_params=params(),
        name="hold",
    )(values, *arrived)


def aligned_start(start, row_count, window):
    begin = jnp.minimum(jnp.left_shift(jnp.right_shift(start, 3), 3), row_count - window)
    return pl.multiple_of(begin, SUBLANES)


def flat_window(held, start, rows):
    span = round_up(rows + 1, SUBLANES)
    shift = jnp.bitwise_and(start, LANES - 1)
    block = held[pl.ds(jnp.right_shift(start, 7), span), :]
    turned = pltpu.roll(block, jnp.bitwise_and(LANES - shift, LANES - 1), 1)
    following = pltpu.roll(turned, span - 1, 0)
    lane = lax.broadcasted_iota(jnp.int32, block.shape, 1)
    return jnp.where(lane < LANES - shift, turned, following)


def window_labels(held, slots, owner, start, per_owner, capacity, blocks):
    low = owner * per_owner
    mine = (slots >= low) & (slots < low + per_owner)
    held[: slots.shape[0], :] = jnp.where(mine, slots - low, -1)
    labels = flat_window(held, start, blocks)
    place = lax.broadcasted_iota(jnp.int32, labels.shape, 0) * LANES + lax.broadcasted_iota(
        jnp.int32, labels.shape, 1
    )
    return jnp.where(place < capacity, labels, -1)


def sent_kernel(per_owner, capacity, start_ref, slot_ref, sum_ref, sent_ref, held):
    owner_count, span, _ = sent_ref.shape
    held[...] = jnp.full(held.shape, -1, jnp.int32)
    slots = slot_ref[...]
    window = capacity + SUBLANES
    wide = sum_ref.shape[1] // LANES
    for owner in range(owner_count):
        labels = window_labels(held, slots, owner, start_ref[owner], per_owner, capacity, span - 1)
        sent_ref[owner] = labels[:span, :]
        aligned = aligned_start(start_ref[owner], slots.size, window)
        labels = window_labels(held, slots, owner, aligned, per_owner, window, wide)
        for block in range(wide):
            sum_ref[owner : owner + 1, block * LANES : (block + 1) * LANES] = labels[block : block + 1, :]


def sent_labels(starts, slots, owner_count, per_owner, capacity):
    span = round_up(-(-capacity // LANES) + 1, SUBLANES)
    return pl.pallas_call(
        functools.partial(sent_kernel, per_owner, capacity),
        out_shape=(
            jax.ShapeDtypeStruct((owner_count, round_up(capacity + SUBLANES, LANES)), jnp.int32),
            jax.ShapeDtypeStruct((owner_count, span, LANES), jnp.int32),
        ),
        in_specs=[in_smem, in_vmem],
        out_specs=(in_vmem, in_vmem),
        scratch_shapes=[pltpu.VMEM((slots.shape[0] + 2 * SUBLANES, LANES), jnp.int32)],
        compiler_params=params(),
        name="sent",
    )(starts, slots)


def arrived_kernel(blocks, turns_of, me_ref, got_ref, row_ref, column_ref, tally_ref):
    tally = jnp.zeros((LANES, LANES), jnp.float32)
    cluster = lax.broadcasted_iota(jnp.int32, tally.shape, 0)
    for place, turn in enumerate(turns_of):
        source = lax.rem(me_ref[0] + len(turns_of) - turn, len(turns_of))
        for block in range(blocks):
            line = place * blocks + block
            spread = jnp.broadcast_to(got_ref[source, block : block + 1, :], tally.shape)
            row_ref[line : line + 1, :] = spread[:1, :]
            column_ref[line * LANES : (line + 1) * LANES, :] = spread.T
            tally += (spread == cluster).astype(jnp.float32)
    total = jnp.broadcast_to(jnp.sum(tally, 1, keepdims=True), tally.shape)
    tally_ref[...] = jnp.zeros(tally_ref.shape, jnp.float32)
    tally_ref[:, :LANES] = total.T[:SUBLANES, :]


def arrived_labels(me, got, turns_of, blocks, width):
    lines = len(turns_of) * blocks
    return pl.pallas_call(
        functools.partial(arrived_kernel, blocks, turns_of),
        out_shape=(
            jax.ShapeDtypeStruct((lines, LANES), jnp.int32),
            jax.ShapeDtypeStruct((lines * LANES, LANES), jnp.int32),
            jax.ShapeDtypeStruct((SUBLANES, width), jnp.float32),
        ),
        in_specs=[in_smem, in_vmem],
        out_specs=(in_vmem, in_vmem, in_vmem),
        compiler_params=params(),
        name="arrived",
    )(me, got)


def sum_kernel(start_ref, label_ref, rows_ref, *refs):
    sum_ref, held, sem = refs[-3:]
    owner_count, per_owner, _ = sum_ref.shape
    window = held.shape[1]

    def copy(owner, slot):
        first = aligned_start(start_ref[owner], rows_ref.shape[0], window)
        return pltpu.make_async_copy(rows_ref.at[pl.ds(first, window), :], held.at[slot], sem.at[slot])

    copy(0, 0).start()

    def body(owner, carry):
        slot = lax.rem(owner, 2)

        @pl.when(owner + 1 < owner_count)
        def _():
            copy(owner + 1, 1 - slot).start()

        copy(owner, slot).wait()
        labels = label_ref[pl.ds(owner, 1), :][:, :window]
        cluster = lax.broadcasted_iota(jnp.int32, (per_owner, window), 0)
        member = (labels == cluster).astype(jnp.float32).astype(jnp.bfloat16)
        values = held[slot]
        high = values.astype(jnp.bfloat16)
        rest = values - high.astype(jnp.float32)
        middle = rest.astype(jnp.bfloat16)
        low = (rest - middle.astype(jnp.float32)).astype(jnp.bfloat16)
        total = jnp.dot(member, high, preferred_element_type=jnp.float32)
        total += jnp.dot(member, middle, preferred_element_type=jnp.float32)
        total += jnp.dot(member, low, preferred_element_type=jnp.float32)
        sum_ref[pl.ds(owner, 1)] = total[None]
        return carry

    lax.fori_loop(0, owner_count, body, 0)


def slot_sums(starts, labels, embeddings, per_owner, capacity, after):
    owner_count = labels.shape[0]
    width = embeddings.shape[1]
    return pl.pallas_call(
        sum_kernel,
        out_shape=jax.ShapeDtypeStruct((owner_count, per_owner, width), jnp.float32),
        in_specs=[in_smem, in_vmem, anywhere] + [anywhere] * len(after),
        out_specs=in_vmem,
        scratch_shapes=[
            pltpu.VMEM((2, capacity + SUBLANES, width), jnp.float32),
            pltpu.SemaphoreType.DMA((2,)),
        ],
        compiler_params=params(),
        cost_estimate=pl.CostEstimate(
            flops=6 * owner_count * per_owner * capacity * width,
            bytes_accessed=4 * embeddings.size,
            transcendentals=0,
        ),
        name="sums",
    )(starts, labels, embeddings, *after)


def gram_kernel(begin, rows, wide, after_count, turns_of, *refs):
    chunk_ref, row_ref, column_ref, best_ref, *refs = refs
    flat_ref = centroid_ref = result_ref = None
    if begin:
        flat_ref, *refs = refs
    refs = refs[after_count:]
    if turns_of:
        centroid_ref, me_ref, result_ref, *refs, out_ref, cosine_ref = refs
    else:
        out_ref, flat_ref, *refs = refs
    mine, labels, tiles, even, odd, best, sem, tile_sem = refs
    first = begin // LANES
    count = round_up(-(-begin // TILE), 2)

    def line_of(tile):
        return jnp.minimum(tile * (TILE // LANES), first - TILE // LANES)

    def fetch(tile):
        start = pl.multiple_of(line_of(tile) * LANES, LANES)
        slot = lax.rem(tile, 4)
        return pltpu.make_async_copy(flat_ref.at[pl.ds(start, TILE), :], tiles.at[slot], tile_sem.at[slot])

    chunk_copy = pltpu.make_async_copy(chunk_ref, mine.at[pl.ds(0, rows), :], sem.at[0])
    label_copy = pltpu.make_async_copy(column_ref.at[pl.ds(begin, wide), :], labels, sem.at[1])
    chunk_copy.start()
    label_copy.start()
    for tile in range(min(count, 3)):
        fetch(jnp.int32(tile)).start()
    if rows < wide:
        mine[rows:wide, :] = jnp.zeros((wide - rows, mine.shape[1]), mine.dtype)
    if turns_of:
        mine[wide:, :] = centroid_ref[...]
        cosine_ref[...] = jnp.zeros(cosine_ref.shape, jnp.float32)
    out_ref[...] = best_ref[...]
    best[...] = jnp.full(best.shape, -2.0, jnp.float32)
    chunk_copy.wait()
    label_copy.wait()
    if not turns_of:
        flat_copy = pltpu.make_async_copy(
            mine.at[pl.ds(0, wide), :], flat_ref.at[pl.ds(begin, wide), :], sem.at[2]
        )
        flat_copy.start()

    def products(right):
        return lax.dot_general(mine[...], right, (((1,), (1,)), ((), ())), preferred_element_type=jnp.float32)

    def cosines(values, line):
        cluster = lax.broadcasted_iota(jnp.int32, values.shape, 0)
        own = jnp.where(row_ref[pl.ds(line, 1), :] == cluster, values, 0.0)
        cosine_ref[pl.ds(line, 1), :] = jnp.sum(own, 0, keepdims=True)

    def reduce_tile(held, tile):
        for part in range(TILE // LANES):
            line = line_of(tile) + part
            here = slice(part * LANES, (part + 1) * LANES)
            near = jnp.where(labels[...] == row_ref[pl.ds(line, 1), :], held[:wide, here], -2.0)
            out_ref[pl.ds(line, 1), :] = jnp.maximum(
                out_ref[pl.ds(line, 1), :], jnp.max(near, 0, keepdims=True)
            )
            best[...] = jnp.maximum(best[...], near)
            if turns_of:
                cosines(held[wide:, here], line)

    if begin:
        fetch(jnp.int32(0)).wait()
        even[...] = products(tiles[0])

        def body(pair, carry):
            tile = pair * 2
            fetch(tile + 1).wait()
            fetch(tile + 3).start()
            odd[...] = products(tiles[lax.rem(tile + 1, 4)])
            reduce_tile(even, tile)
            fetch(tile + 2).wait()

            @pl.when(tile + 4 < count)
            def _():
                fetch(tile + 4).start()

            even[...] = products(tiles[lax.rem(tile + 2, 4)])
            reduce_tile(odd, tile + 1)
            return carry

        lax.fori_loop(0, count // 2 - 1, body, 0)
        fetch(jnp.int32(count - 1)).wait()
        odd[...] = products(tiles[(count - 1) % 4])
        reduce_tile(even, jnp.int32(count - 2))
        reduce_tile(odd, jnp.int32(count - 1))
    own = products(mine[:wide, :])
    row = lax.broadcasted_iota(jnp.int32, (wide, LANES), 0)
    column = lax.broadcasted_iota(jnp.int32, (wide, LANES), 1)
    for block in range(wide // LANES):
        line = first + block
        here = slice(block * LANES, (block + 1) * LANES)
        allowed = (labels[...] == row_ref[line : line + 1, :]) & (row != column + block * LANES)
        near = jnp.max(jnp.where(allowed, own[:wide, here], -2.0), 0, keepdims=True)
        other = jnp.max(best[here, :].T, 0, keepdims=True)
        out_ref[line : line + 1, :] = jnp.maximum(near, other)
        if turns_of:
            cosines(own[wide:, here], line)
    if turns_of:
        blocks = row_ref.shape[0] // len(turns_of)
        half = result_ref.shape[1] // 2
        result_ref[...] = jnp.zeros(result_ref.shape, jnp.float32)
        for place, turn in enumerate(turns_of):
            source = lax.rem(me_ref[0] + len(turns_of) - turn, len(turns_of))
            lines = slice(place * blocks, (place + 1) * blocks)
            result_ref[source, :blocks, :] = out_ref[lines, :]
            result_ref[source, half : half + blocks, :] = cosine_ref[lines, :]
    else:
        flat_copy.wait()


def gram_step(rows, columns, best, flat, chunk, begin, after=(), final=None):
    length, width = chunk.shape
    wide = round_up(length, LANES)
    tall = wide
    flat_shape = jax.ShapeDtypeStruct((columns.shape[0], width), jnp.bfloat16)
    inputs = [chunk, rows, columns, best]
    in_specs = [anywhere, in_vmem, anywhere, in_vmem]
    aliases = {}
    if begin:
        if not final:
            aliases = {len(inputs): 1}
        inputs.append(flat)
        in_specs.append(anywhere)
    inputs += after
    in_specs += [anywhere] * len(after)
    out_shape = (jax.ShapeDtypeStruct(best.shape, jnp.float32), flat_shape)
    out_specs = (in_vmem, anywhere)
    turns_of = ()
    extra = []
    if final:
        centroid_unit, me, turns_of = final
        tall += centroid_unit.shape[0]
        inputs += [centroid_unit, me]
        in_specs += [in_vmem, in_smem]
        half = round_up(rows.shape[0] // len(turns_of) + 1, SUBLANES)
        out_shape = jax.ShapeDtypeStruct((len(turns_of), 2 * half, LANES), jnp.float32)
        out_specs = in_vmem
        extra = [pltpu.VMEM(best.shape, jnp.float32)] * 2
    return pl.pallas_call(
        functools.partial(gram_kernel, begin, length, wide, len(after), turns_of),
        out_shape=out_shape,
        in_specs=in_specs,
        out_specs=out_specs,
        scratch_shapes=[
            pltpu.VMEM((tall, width), jnp.bfloat16),
            pltpu.VMEM((wide, LANES), jnp.int32),
            pltpu.VMEM((4, TILE, width), jnp.bfloat16),
            pltpu.VMEM((tall, TILE), jnp.float32),
            pltpu.VMEM((tall, TILE), jnp.float32),
            pltpu.VMEM((wide, LANES), jnp.float32),
            pltpu.SemaphoreType.DMA((3,)),
            pltpu.SemaphoreType.DMA((4,)),
        ]
        + extra,
        input_output_aliases=aliases,
        compiler_params=params(),
        cost_estimate=brief,
        name="gram",
    )(*inputs)


def pack_kernel(share_ref, tally_ref, *refs):
    packed_ref = refs[-1]
    packed_ref[: share_ref.shape[0], :] = share_ref[...]
    packed_ref[share_ref.shape[0] :, :] = tally_ref[...]


def pack_share(share, tally, after):
    length = share.shape[0] + tally.shape[0]
    return pl.pallas_call(
        pack_kernel,
        out_shape=jax.ShapeDtypeStruct((length, share.shape[1]), jnp.float32),
        in_specs=[in_vmem, in_vmem] + [anywhere] * len(after),
        out_specs=in_vmem,
        compiler_params=params(),
        name="pack",
    )(share, tally, *after)


def centroid_kernel(gathered_ref, centroid_ref, unit_ref):
    groups, length, width = gathered_ref.shape
    share = length - SUBLANES
    per_owner = centroid_ref.shape[0]
    tally = jnp.sum(gathered_ref[:, share, :LANES], 0, keepdims=True)
    column = jnp.broadcast_to(tally, (LANES, LANES)).T[:per_owner, :]
    sums = jnp.concatenate([gathered_ref[group, :share, :] for group in range(groups)], 0)
    centroids = sums / jnp.concatenate([column] * (width // LANES), 1)
    centroid_ref[...] = centroids
    scale = lax.rsqrt(jnp.sum(centroids * centroids, -1, keepdims=True) + epsilon)
    unit_ref[...] = (centroids * scale).astype(jnp.bfloat16)


def make_centroids(gathered, per_owner):
    shape = (per_owner, gathered.shape[2])
    return pl.pallas_call(
        centroid_kernel,
        out_shape=(
            jax.ShapeDtypeStruct(shape, jnp.float32),
            jax.ShapeDtypeStruct(shape, jnp.bfloat16),
        ),
        in_specs=[in_vmem],
        out_specs=(in_vmem, in_vmem),
        compiler_params=params(),
        name="centroids",
    )(gathered)


def place_kernel(per_owner, start_ref, slot_ref, back_ref, near_ref, cosine_ref, held, result):
    owner_count, double, _ = back_ref.shape
    span = double // 2
    rows = slot_ref.shape[0]
    held[...] = jnp.full(held.shape, -1, jnp.int32)
    held[:rows, :] = slot_ref[...]
    result[...] = jnp.zeros(result.shape, jnp.float32)
    lane = lax.broadcasted_iota(jnp.int32, (span, LANES), 1)
    for owner in range(owner_count):
        start = start_ref[owner]
        first = pl.ds(jnp.right_shift(start, 7), span)
        shift = jnp.bitwise_and(start, LANES - 1)
        slots = held[first, :]
        mine = (slots >= owner * per_owner) & (slots < (owner + 1) * per_owner)
        for kind in range(2):
            turned = pltpu.roll(back_ref[owner, kind * span : (kind + 1) * span, :], shift, 1)
            earlier = pltpu.roll(turned, 1, 0)
            moved = jnp.where(lane >= shift, turned, earlier)
            result[kind, first, :] = jnp.where(mine, moved, result[kind, first, :])
    near_ref[...] = result[0, :rows, :]
    cosine_ref[...] = result[1, :rows, :]


def place_rows(starts, slots, back, per_owner):
    span = back.shape[1] // 2
    rows = slots.shape[0]
    return pl.pallas_call(
        functools.partial(place_kernel, per_owner),
        out_shape=(jax.ShapeDtypeStruct(slots.shape, jnp.float32),) * 2,
        in_specs=[in_smem, in_vmem, in_vmem],
        out_specs=(in_vmem, in_vmem),
        scratch_shapes=[
            pltpu.VMEM((rows + span, LANES), jnp.int32),
            pltpu.VMEM((2, rows + span, LANES), jnp.float32),
        ],
        compiler_params=params(),
        name="place",
    )(starts, slots, back)


def turns(count):
    order = sorted(range(count), key=lambda turn: (min(turn, count - turn), turn))
    return order[:1] + order[3:4] + order[1:3] + order[4:]


IN_FLIGHT = 2


def per_device(embeddings, assign, cluster_slot):
    row_count, width = embeddings.shape
    owner_count = lax.axis_size("docs")
    per_owner = cluster_slot.shape[0] // owner_count
    capacity = row_count // owner_count + row_count // (4 * owner_count)
    padded = round_up(capacity, LANES)
    blocks = padded // LANES
    me = lax.axis_index("docs").astype(jnp.int32).reshape(1)
    turns_of = turns(owner_count)

    pieces = []
    for place, turn in enumerate(turns_of):
        if capacity < padded or blocks < 5 or place < owner_count - 3:
            cuts = [0, capacity]
        elif place < owner_count - 1:
            cuts = [0, 3 * LANES, capacity]
        else:
            cuts = [0, 2 * LANES, 4 * LANES, capacity]
        for low, high in zip(cuts, cuts[1:]):
            pieces.append((turn, low, high - low, place * padded + low))

    slots, starts = make_plan(
        assign.reshape(-1, LANES), cluster_slot.reshape(-1, LANES), owner_count, per_owner, row_count - capacity
    )
    sum_labels, wire_labels = sent_labels(starts, slots, owner_count, per_owner, capacity)
    got_labels = lax.all_to_all(wire_labels, "docs", split_axis=0, concat_axis=0, tiled=True)
    rows, columns, group_tally = arrived_labels(me, got_labels, turns_of, blocks, width)

    chunks, sent = [], []
    bests = [jnp.full((owner_count * blocks, LANES), -2.0, jnp.float32)]
    flat = group_share = share = None

    def multiply(index):
        after = [group_share] if index == len(pieces) // 4 else []
        best, held = gram_step(rows, columns, bests[-1], flat, chunks[index], pieces[index][3], after)
        bests.append(best)
        return held

    for index, (turn, offset, length, _) in enumerate(pieces):
        after = [got_labels] if index == IN_FLIGHT else []
        if index > IN_FLIGHT:
            after += [chunks[index - IN_FLIGHT - (index == len(pieces) - 1)], sent[-1]]
        if index > IN_FLIGHT + 2:
            flat = multiply(index - IN_FLIGHT - 3)
            after.append(bests[-1])
        piece = unit_piece(starts, me, embeddings, turn, offset, length, after)
        sent.append(piece)
        if turn:
            piece = lax.ppermute(piece, "docs", [(i, (i + turn) % owner_count) for i in range(owner_count)])
        chunks.append(piece)
        if index == IN_FLIGHT + 1:
            partial_sums = slot_sums(starts, sum_labels, embeddings, per_owner, capacity, sent[: IN_FLIGHT + 1])
            partial_sums = hold_until(partial_sums, chunks[1 : IN_FLIGHT + 1] + sent[IN_FLIGHT + 1 :])
            group_share = lax.psum_scatter(partial_sums, "grp", scatter_dimension=1, tiled=True)
            share = lax.psum_scatter(group_share, "docs", scatter_dimension=0, tiled=True)[0]
    for index in range(len(bests) - 1, len(pieces) - 1):
        flat = multiply(index)
    packed = pack_share(share, group_tally, [bests[-2], sent[-1]])
    centroids, centroid_unit = make_centroids(lax.all_gather(packed, "grp"), per_owner)
    results = gram_step(
        rows, columns, bests[-1], flat, chunks[-1], pieces[-1][3], final=(centroid_unit, me, turns_of)
    )
    back = lax.all_to_all(results, "docs", split_axis=0, concat_axis=0, tiled=True)
    near, cosine = place_rows(starts, slots, back, per_owner)
    return (centroids, near.reshape(-1), cosine.reshape(-1))


def solution(mesh):
    placed = (P(("grp", "docs"), None), P(("grp", "docs")), P())
    return jax.shard_map(
        per_device,
        mesh=mesh,
        in_specs=placed,
        out_specs=(P("docs", None), P(("grp", "docs")), P(("grp", "docs"))),
        check_vma=False,
    )
```

```python
import functools

import jax
import jax.numpy as jnp
from jax import lax
from jax.experimental import pallas as pl
from jax.experimental.pallas import tpu as pltpu
from jax.sharding import PartitionSpec as P

epsilon = 1e-06
LANES = 128
SUBLANES = 8
MIB = 1024 * 1024
TILE = 512
in_vmem = pl.BlockSpec(memory_space=pltpu.VMEM)
in_smem = pl.BlockSpec(memory_space=pltpu.SMEM)
anywhere = pl.BlockSpec(memory_space=pl.ANY)
brief = pl.CostEstimate(flops=1000, bytes_accessed=1000, transcendentals=0)


def round_up(value, step):
    return -(-value // step) * step


def params(mib=46):
    return pltpu.CompilerParams(vmem_limit_bytes=mib * MIB)


def look_up(table_ref, index):
    lane = jnp.bitwise_and(index, LANES - 1)
    row = jnp.right_shift(index, 7)
    found = jnp.zeros(index.shape, jnp.int32)
    for part in range(table_ref.shape[0]):
        entries = jnp.broadcast_to(table_ref[part : part + 1, :], index.shape)
        found = jnp.where(row == part, jnp.take_along_axis(entries, lane, axis=1), found)
    return found


def rows_below(slots, bound):
    return jnp.sum((slots < bound).astype(jnp.float32)).astype(jnp.int32)


def plan_kernel(per_owner, limit, assign_ref, table_ref, slot_ref, start_ref):
    slots = look_up(table_ref, assign_ref[...])
    slot_ref[...] = slots
    for owner in range(start_ref.shape[0]):
        start_ref[owner] = jnp.minimum(rows_below(slots, owner * per_owner), limit)


def make_plan(assign_rows, table, owner_count, per_owner, limit):
    return pl.pallas_call(
        functools.partial(plan_kernel, per_owner, limit),
        out_shape=(
            jax.ShapeDtypeStruct(assign_rows.shape, jnp.int32),
            jax.ShapeDtypeStruct((owner_count,), jnp.int32),
        ),
        in_specs=[in_vmem, in_vmem],
        out_specs=(in_vmem, in_smem),
        compiler_params=params(),
        name="plan",
    )(assign_rows, table)


def unit_kernel(steps, offset, turn, start_ref, me_ref, rows_ref, *refs):
    unit_ref, held, sem = refs[-3:]
    part = unit_ref.shape[0] // steps
    window = part + SUBLANES
    start = start_ref[lax.rem(me_ref[0] + turn, start_ref.shape[0])] + offset

    def first(step):
        return aligned_start(start + step * part, rows_ref.shape[0], window)

    copies = [
        pltpu.make_async_copy(rows_ref.at[pl.ds(first(step), window), :], held.at[step], sem.at[step])
        for step in range(steps)
    ]
    for copy in copies:
        copy.start()
    for step in range(steps):
        copies[step].wait()
        shift = start + step * part - first(step)
        groups = held[step].reshape(window // SUBLANES, SUBLANES, -1)
        turned = pltpu.roll(groups, SUBLANES - shift, 1)
        line = lax.broadcasted_iota(jnp.int32, (part // SUBLANES, SUBLANES, groups.shape[2]), 1)
        values = jnp.where(line < SUBLANES - shift, turned[:-1], turned[1:]).reshape(part, -1)
        scale = lax.rsqrt(jnp.sum(values * values, -1, keepdims=True) + epsilon)
        unit_ref[step * part : (step + 1) * part, :] = (values * scale).astype(jnp.bfloat16)


def unit_piece(starts, me, embeddings, turn, offset, rows, after):
    width = embeddings.shape[1]
    steps = rows // LANES if rows % LANES == 0 else 1
    return pl.pallas_call(
        functools.partial(unit_kernel, steps, offset, turn),
        out_shape=jax.ShapeDtypeStruct((rows, width), jnp.bfloat16),
        in_specs=[in_smem, in_smem, anywhere] + [anywhere] * len(after),
        out_specs=in_vmem,
        scratch_shapes=[
            pltpu.VMEM((steps, rows // steps + SUBLANES, width), jnp.float32),
            pltpu.SemaphoreType.DMA((steps,)),
        ],
        compiler_params=params(),
        cost_estimate=brief,
        name="unit",
    )(starts, me, embeddings, *after)


def hold_until(values, arrived):
    def nothing(*refs):
        pass

    return pl.pallas_call(
        nothing,
        out_shape=jax.ShapeDtypeStruct(values.shape, values.dtype),
        in_specs=[anywhere] * (1 + len(arrived)),
        out_specs=anywhere,
        input_output_aliases={0: 0},
        compiler_params=params(),
        name="hold",
    )(values, *arrived)


def aligned_start(start, row_count, window):
    begin = jnp.minimum(jnp.left_shift(jnp.right_shift(start, 3), 3), row_count - window)
    return pl.multiple_of(begin, SUBLANES)


def flat_window(held, start, rows):
    span = round_up(rows + 1, SUBLANES)
    shift = jnp.bitwise_and(start, LANES - 1)
    block = held[pl.ds(jnp.right_shift(start, 7), span), :]
    turned = pltpu.roll(block, jnp.bitwise_and(LANES - shift, LANES - 1), 1)
    following = pltpu.roll(turned, span - 1, 0)
    lane = lax.broadcasted_iota(jnp.int32, block.shape, 1)
    return jnp.where(lane < LANES - shift, turned, following)


def window_labels(held, slots, owner, start, per_owner, capacity, blocks):
    low = owner * per_owner
    mine = (slots >= low) & (slots < low + per_owner)
    held[: slots.shape[0], :] = jnp.where(mine, slots - low, -1)
    labels = flat_window(held, start, blocks)
    place = lax.broadcasted_iota(jnp.int32, labels.shape, 0) * LANES + lax.broadcasted_iota(
        jnp.int32, labels.shape, 1
    )
    return jnp.where(place < capacity, labels, -1)


def sent_kernel(per_owner, capacity, start_ref, slot_ref, after_ref, sum_ref, sent_ref, held):
    owner_count, span, _ = sent_ref.shape
    held[...] = jnp.full(held.shape, -1, jnp.int32)
    slots = slot_ref[...]
    window = capacity + SUBLANES
    wide = sum_ref.shape[1] // LANES
    for owner in range(owner_count):
        labels = window_labels(held, slots, owner, start_ref[owner], per_owner, capacity, span - 1)
        sent_ref[owner] = labels[:span, :]
        aligned = aligned_start(start_ref[owner], slots.size, window)
        labels = window_labels(held, slots, owner, aligned, per_owner, window, wide)
        for block in range(wide):
            sum_ref[owner : owner + 1, block * LANES : (block + 1) * LANES] = labels[block : block + 1, :]


def sent_labels(starts, slots, owner_count, per_owner, capacity, after):
    span = round_up(-(-capacity // LANES) + 1, SUBLANES)
    return pl.pallas_call(
        functools.partial(sent_kernel, per_owner, capacity),
        out_shape=(
            jax.ShapeDtypeStruct((owner_count, round_up(capacity + SUBLANES, LANES)), jnp.int32),
            jax.ShapeDtypeStruct((owner_count, span, LANES), jnp.int32),
        ),
        in_specs=[in_smem, in_vmem, anywhere],
        out_specs=(in_vmem, in_vmem),
        scratch_shapes=[pltpu.VMEM((slots.shape[0] + 2 * SUBLANES, LANES), jnp.int32)],
        compiler_params=params(),
        name="sent",
    )(starts, slots, after)


def arrived_kernel(blocks, turns_of, me_ref, got_ref, row_ref, column_ref, tally_ref):
    tally = jnp.zeros((LANES, LANES), jnp.float32)
    cluster = lax.broadcasted_iota(jnp.int32, tally.shape, 0)
    for place, turn in enumerate(turns_of):
        source = lax.rem(me_ref[0] + len(turns_of) - turn, len(turns_of))
        for block in range(blocks):
            line = place * blocks + block
            spread = jnp.broadcast_to(got_ref[source, block : block + 1, :], tally.shape)
            row_ref[line : line + 1, :] = spread[:1, :]
            column_ref[line * LANES : (line + 1) * LANES, :] = spread.T
            tally += (spread == cluster).astype(jnp.float32)
    total = jnp.broadcast_to(jnp.sum(tally, 1, keepdims=True), tally.shape)
    tally_ref[...] = jnp.zeros(tally_ref.shape, jnp.float32)
    tally_ref[:, :LANES] = total.T[:SUBLANES, :]


def arrived_labels(me, got, turns_of, blocks, width):
    lines = len(turns_of) * blocks
    return pl.pallas_call(
        functools.partial(arrived_kernel, blocks, turns_of),
        out_shape=(
            jax.ShapeDtypeStruct((lines, LANES), jnp.int32),
            jax.ShapeDtypeStruct((lines * LANES, LANES), jnp.int32),
            jax.ShapeDtypeStruct((SUBLANES, width), jnp.float32),
        ),
        in_specs=[in_smem, in_vmem],
        out_specs=(in_vmem, in_vmem, in_vmem),
        compiler_params=params(),
        name="arrived",
    )(me, got)


def sum_kernel(start_ref, label_ref, rows_ref, *refs):
    sum_ref, held, sem = refs[-3:]
    owner_count, per_owner, _ = sum_ref.shape
    window = held.shape[1]

    def copy(owner, slot):
        first = aligned_start(start_ref[owner], rows_ref.shape[0], window)
        return pltpu.make_async_copy(rows_ref.at[pl.ds(first, window), :], held.at[slot], sem.at[slot])

    copy(0, 0).start()

    def body(owner, carry):
        slot = lax.rem(owner, 2)

        @pl.when(owner + 1 < owner_count)
        def _():
            copy(owner + 1, 1 - slot).start()

        copy(owner, slot).wait()
        labels = label_ref[pl.ds(owner, 1), :][:, :window]
        cluster = lax.broadcasted_iota(jnp.int32, (per_owner, window), 0)
        member = (labels == cluster).astype(jnp.float32).astype(jnp.bfloat16)
        values = held[slot]
        high = values.astype(jnp.bfloat16)
        rest = values - high.astype(jnp.float32)
        middle = rest.astype(jnp.bfloat16)
        low = (rest - middle.astype(jnp.float32)).astype(jnp.bfloat16)
        total = jnp.dot(member, high, preferred_element_type=jnp.float32)
        total += jnp.dot(member, middle, preferred_element_type=jnp.float32)
        total += jnp.dot(member, low, preferred_element_type=jnp.float32)
        sum_ref[pl.ds(owner, 1)] = total[None]
        return carry

    lax.fori_loop(0, owner_count, body, 0)


def slot_sums(starts, labels, embeddings, per_owner, capacity, after):
    owner_count = labels.shape[0]
    width = embeddings.shape[1]
    return pl.pallas_call(
        sum_kernel,
        out_shape=jax.ShapeDtypeStruct((owner_count, per_owner, width), jnp.float32),
        in_specs=[in_smem, in_vmem, anywhere] + [anywhere] * len(after),
        out_specs=in_vmem,
        scratch_shapes=[
            pltpu.VMEM((2, capacity + SUBLANES, width), jnp.float32),
            pltpu.SemaphoreType.DMA((2,)),
        ],
        compiler_params=params(),
        cost_estimate=pl.CostEstimate(
            flops=6 * owner_count * per_owner * capacity * width,
            bytes_accessed=4 * embeddings.size,
            transcendentals=0,
        ),
        name="sums",
    )(starts, labels, embeddings, *after)


def gram_kernel(begin, rows, wide, after_count, turns_of, *refs):
    chunk_ref, row_ref, column_ref, best_ref, *refs = refs
    flat_ref = centroid_ref = result_ref = None
    if begin:
        flat_ref, *refs = refs
    refs = refs[after_count:]
    if turns_of:
        centroid_ref, me_ref, result_ref, *refs, out_ref, cosine_ref = refs
    else:
        out_ref, flat_ref, *refs = refs
    mine, turned, labels, tiles, even, odd, best, sem, tile_sem = refs
    first = begin // LANES
    size = tiles.shape[2]
    count = round_up(-(-begin // size), 2)

    def line_of(tile):
        return jnp.minimum(tile * (size // LANES), first - size // LANES)

    def fetch(tile):
        start = pl.multiple_of(line_of(tile) * LANES, LANES)
        slot = lax.rem(tile, 4)
        return pltpu.make_async_copy(flat_ref.at[:, pl.ds(start, size)], tiles.at[slot], tile_sem.at[slot])

    chunk_copy = pltpu.make_async_copy(chunk_ref, mine.at[pl.ds(0, rows), :], sem.at[0])
    label_copy = pltpu.make_async_copy(column_ref.at[pl.ds(begin, wide), :], labels, sem.at[1])
    chunk_copy.start()
    label_copy.start()
    for tile in range(min(count, 3)):
        fetch(jnp.int32(tile)).start()
    if rows < wide:
        mine[rows:wide, :] = jnp.zeros((wide - rows, mine.shape[1]), mine.dtype)
    if turns_of:
        mine[wide:, :] = centroid_ref[...]
        cosine_ref[...] = jnp.zeros(cosine_ref.shape, jnp.float32)
    out_ref[...] = best_ref[...]
    best[...] = jnp.full(best.shape, -2.0, jnp.float32)
    chunk_copy.wait()
    label_copy.wait()
    turned[...] = mine[:wide, :].T
    if not turns_of:
        flat_copy = pltpu.make_async_copy(turned, flat_ref.at[:, pl.ds(begin, wide)], sem.at[2])
        flat_copy.start()

    def products(right):
        return jnp.dot(mine[...], right, preferred_element_type=jnp.float32)

    def cosines(values, line):
        cluster = lax.broadcasted_iota(jnp.int32, values.shape, 0)
        own = jnp.where(row_ref[pl.ds(line, 1), :] == cluster, values, 0.0)
        cosine_ref[pl.ds(line, 1), :] = jnp.sum(own, 0, keepdims=True)

    def reduce_tile(held, tile):
        for part in range(size // LANES):
            line = line_of(tile) + part
            here = slice(part * LANES, (part + 1) * LANES)
            near = jnp.where(labels[...] == row_ref[pl.ds(line, 1), :], held[:wide, here], -2.0)
            out_ref[pl.ds(line, 1), :] = jnp.maximum(
                out_ref[pl.ds(line, 1), :], jnp.max(near, 0, keepdims=True)
            )
            best[...] = jnp.maximum(best[...], near)
            if turns_of:
                cosines(held[wide:, here], line)

    if begin:
        fetch(jnp.int32(0)).wait()
        even[...] = products(tiles[0])

        def body(pair, carry):
            tile = pair * 2
            fetch(tile + 1).wait()
            fetch(tile + 3).start()
            odd[...] = products(tiles[lax.rem(tile + 1, 4)])
            reduce_tile(even, tile)
            fetch(tile + 2).wait()

            @pl.when(tile + 4 < count)
            def _():
                fetch(tile + 4).start()

            even[...] = products(tiles[lax.rem(tile + 2, 4)])
            reduce_tile(odd, tile + 1)
            return carry

        lax.fori_loop(0, count // 2 - 1, body, 0)
        fetch(jnp.int32(count - 1)).wait()
        odd[...] = products(tiles[(count - 1) % 4])
        reduce_tile(even, jnp.int32(count - 2))
        reduce_tile(odd, jnp.int32(count - 1))
    own = products(turned[...])
    row = lax.broadcasted_iota(jnp.int32, (wide, LANES), 0)
    column = lax.broadcasted_iota(jnp.int32, (wide, LANES), 1)
    for block in range(wide // LANES):
        line = first + block
        here = slice(block * LANES, (block + 1) * LANES)
        allowed = (labels[...] == row_ref[line : line + 1, :]) & (row != column + block * LANES)
        near = jnp.max(jnp.where(allowed, own[:wide, here], -2.0), 0, keepdims=True)
        other = jnp.max(best[here, :].T, 0, keepdims=True)
        out_ref[line : line + 1, :] = jnp.maximum(near, other)
        if turns_of:
            cosines(own[wide:, here], line)
    if turns_of:
        blocks = row_ref.shape[0] // len(turns_of)
        half = result_ref.shape[1] // 2
        result_ref[...] = jnp.zeros(result_ref.shape, jnp.float32)
        for place, turn in enumerate(turns_of):
            source = lax.rem(me_ref[0] + len(turns_of) - turn, len(turns_of))
            lines = slice(place * blocks, (place + 1) * blocks)
            result_ref[source, :blocks, :] = out_ref[lines, :]
            result_ref[source, half : half + blocks, :] = cosine_ref[lines, :]
    else:
        flat_copy.wait()


def gram_step(rows, columns, best, flat, chunk, begin, after=(), final=None):
    length, width = chunk.shape
    wide = round_up(length, LANES)
    tall = wide
    size = min(TILE, begin) if begin else LANES
    flat_shape = jax.ShapeDtypeStruct((width, columns.shape[0]), jnp.bfloat16)
    inputs = [chunk, rows, columns, best]
    in_specs = [anywhere, in_vmem, anywhere, in_vmem]
    aliases = {}
    if begin:
        if not final:
            aliases = {len(inputs): 1}
        inputs.append(flat)
        in_specs.append(anywhere)
    inputs += after
    in_specs += [anywhere] * len(after)
    out_shape = (jax.ShapeDtypeStruct(best.shape, jnp.float32), flat_shape)
    out_specs = (in_vmem, anywhere)
    turns_of = ()
    extra = []
    if final:
        centroid_unit, me, turns_of = final
        tall += centroid_unit.shape[0]
        inputs += [centroid_unit, me]
        in_specs += [in_vmem, in_smem]
        half = round_up(rows.shape[0] // len(turns_of) + 1, SUBLANES)
        out_shape = jax.ShapeDtypeStruct((len(turns_of), 2 * half, LANES), jnp.float32)
        out_specs = in_vmem
        extra = [pltpu.VMEM(best.shape, jnp.float32)] * 2
    return pl.pallas_call(
        functools.partial(gram_kernel, begin, length, wide, len(after), turns_of),
        out_shape=out_shape,
        in_specs=in_specs,
        out_specs=out_specs,
        scratch_shapes=[
            pltpu.VMEM((tall, width), jnp.bfloat16),
            pltpu.VMEM((width, wide), jnp.bfloat16),
            pltpu.VMEM((wide, LANES), jnp.int32),
            pltpu.VMEM((4, width, size), jnp.bfloat16),
            pltpu.VMEM((tall, size), jnp.float32),
            pltpu.VMEM((tall, size), jnp.float32),
            pltpu.VMEM((wide, LANES), jnp.float32),
            pltpu.SemaphoreType.DMA((3,)),
            pltpu.SemaphoreType.DMA((4,)),
        ]
        + extra,
        input_output_aliases=aliases,
        compiler_params=params(),
        cost_estimate=brief,
        name="gram",
    )(*inputs)


def pack_kernel(share_ref, tally_ref, *refs):
    packed_ref = refs[-1]
    packed_ref[: share_ref.shape[0], :] = share_ref[...]
    packed_ref[share_ref.shape[0] :, :] = tally_ref[...]


def pack_share(share, tally, after):
    length = share.shape[0] + tally.shape[0]
    return pl.pallas_call(
        pack_kernel,
        out_shape=jax.ShapeDtypeStruct((length, share.shape[1]), jnp.float32),
        in_specs=[in_vmem, in_vmem] + [anywhere] * len(after),
        out_specs=in_vmem,
        compiler_params=params(),
        name="pack",
    )(share, tally, *after)


def centroid_kernel(gathered_ref, centroid_ref, unit_ref):
    groups, length, width = gathered_ref.shape
    share = length - SUBLANES
    per_owner = centroid_ref.shape[0]
    tally = jnp.sum(gathered_ref[:, share, :LANES], 0, keepdims=True)
    column = jnp.broadcast_to(tally, (LANES, LANES)).T[:per_owner, :]
    sums = jnp.concatenate([gathered_ref[group, :share, :] for group in range(groups)], 0)
    centroids = sums / jnp.concatenate([column] * (width // LANES), 1)
    centroid_ref[...] = centroids
    scale = lax.rsqrt(jnp.sum(centroids * centroids, -1, keepdims=True) + epsilon)
    unit_ref[...] = (centroids * scale).astype(jnp.bfloat16)


def make_centroids(gathered, per_owner):
    shape = (per_owner, gathered.shape[2])
    return pl.pallas_call(
        centroid_kernel,
        out_shape=(
            jax.ShapeDtypeStruct(shape, jnp.float32),
            jax.ShapeDtypeStruct(shape, jnp.bfloat16),
        ),
        in_specs=[in_vmem],
        out_specs=(in_vmem, in_vmem),
        compiler_params=params(),
        name="centroids",
    )(gathered)


def place_kernel(per_owner, start_ref, slot_ref, back_ref, near_ref, cosine_ref, held, result):
    owner_count, double, _ = back_ref.shape
    span = double // 2
    rows = slot_ref.shape[0]
    held[...] = jnp.full(held.shape, -1, jnp.int32)
    held[:rows, :] = slot_ref[...]
    result[...] = jnp.zeros(result.shape, jnp.float32)
    lane = lax.broadcasted_iota(jnp.int32, (span, LANES), 1)
    for owner in range(owner_count):
        start = start_ref[owner]
        first = pl.ds(jnp.right_shift(start, 7), span)
        shift = jnp.bitwise_and(start, LANES - 1)
        slots = held[first, :]
        mine = (slots >= owner * per_owner) & (slots < (owner + 1) * per_owner)
        for kind in range(2):
            turned = pltpu.roll(back_ref[owner, kind * span : (kind + 1) * span, :], shift, 1)
            earlier = pltpu.roll(turned, 1, 0)
            moved = jnp.where(lane >= shift, turned, earlier)
            result[kind, first, :] = jnp.where(mine, moved, result[kind, first, :])
    near_ref[...] = result[0, :rows, :]
    cosine_ref[...] = result[1, :rows, :]


def place_rows(starts, slots, back, per_owner):
    span = back.shape[1] // 2
    rows = slots.shape[0]
    return pl.pallas_call(
        functools.partial(place_kernel, per_owner),
        out_shape=(jax.ShapeDtypeStruct(slots.shape, jnp.float32),) * 2,
        in_specs=[in_smem, in_vmem, in_vmem],
        out_specs=(in_vmem, in_vmem),
        scratch_shapes=[
            pltpu.VMEM((rows + span, LANES), jnp.int32),
            pltpu.VMEM((2, rows + span, LANES), jnp.float32),
        ],
        compiler_params=params(),
        name="place",
    )(starts, slots, back)


def turns(count):
    order = sorted(range(count), key=lambda turn: (min(turn, count - turn), turn))
    return order[:1] + order[3:4] + order[1:3] + order[4:]


def per_device(embeddings, assign, cluster_slot):
    row_count, width = embeddings.shape
    owner_count = lax.axis_size("docs")
    per_owner = cluster_slot.shape[0] // owner_count
    capacity = row_count // owner_count + row_count // (4 * owner_count)
    padded = round_up(capacity, LANES)
    blocks = padded // LANES
    me = lax.axis_index("docs").astype(jnp.int32).reshape(1)
    turns_of = turns(owner_count)

    slots, starts = make_plan(
        assign.reshape(-1, LANES), cluster_slot.reshape(-1, LANES), owner_count, per_owner, row_count - capacity
    )

    sent, chunks = [], []
    for place, turn in enumerate(turns_of):
        piece = unit_piece(starts, me, embeddings, turn, 0, capacity, sent[-1:] if place > 1 else [])
        if place == 2:
            sum_labels, wire_labels = sent_labels(starts, slots, owner_count, per_owner, capacity, sent[1])
            got_labels = lax.all_to_all(wire_labels, "docs", split_axis=0, concat_axis=0, tiled=True)
            piece = hold_until(piece, [got_labels])
        sent.append(piece)
        if turn:
            piece = lax.ppermute(piece, "docs", [(i, (i + turn) % owner_count) for i in range(owner_count)])
        chunks.append(piece)
    rows, columns, group_tally = arrived_labels(me, got_labels, turns_of, blocks, width)
    partial_sums = slot_sums(starts, sum_labels, embeddings, per_owner, capacity, sent[1:5])
    partial_sums = hold_until(partial_sums, chunks[1:3])
    group_share = lax.psum_scatter(partial_sums, "grp", scatter_dimension=1, tiled=True)
    share = lax.psum_scatter(group_share, "docs", scatter_dimension=0, tiled=True)[0]

    bests = [jnp.full((owner_count * blocks, LANES), -2.0, jnp.float32)]
    flat = None
    for place in range(owner_count - 1):
        after = [group_share] if place == 2 else []
        best, flat = gram_step(rows, columns, bests[-1], flat, chunks[place], place * padded, after)
        bests.append(best)
    packed = pack_share(share, group_tally, bests[-3:-2])
    centroids, centroid_unit = make_centroids(lax.all_gather(packed, "grp"), per_owner)
    results = gram_step(
        rows, columns, bests[-1], flat, chunks[-1], (owner_count - 1) * padded, final=(centroid_unit, me, turns_of)
    )
    back = lax.all_to_all(results, "docs", split_axis=0, concat_axis=0, tiled=True)
    near, cosine = place_rows(starts, slots, back, per_owner)
    return (centroids, near.reshape(-1), cosine.reshape(-1))


def solution(mesh):
    placed = (P(("grp", "docs"), None), P(("grp", "docs")), P())
    return jax.shard_map(
        per_device,
        mesh=mesh,
        in_specs=placed,
        out_specs=(P("docs", None), P(("grp", "docs")), P(("grp", "docs"))),
        check_vma=False,
    )
```

```python
import functools

import jax
import jax.numpy as jnp
from jax import lax
from jax.experimental import pallas as pl
from jax.experimental.pallas import tpu as pltpu
from jax.sharding import PartitionSpec as P

epsilon = 1e-06
LANES = 128
SUBLANES = 8
MIB = 1024 * 1024
TILE = 512
in_vmem = pl.BlockSpec(memory_space=pltpu.VMEM)
in_smem = pl.BlockSpec(memory_space=pltpu.SMEM)
anywhere = pl.BlockSpec(memory_space=pl.ANY)
brief = pl.CostEstimate(flops=1000, bytes_accessed=1000, transcendentals=0)


def round_up(value, step):
    return -(-value // step) * step


def params(mib=46):
    return pltpu.CompilerParams(vmem_limit_bytes=mib * MIB)


def look_up(table_ref, index):
    lane = jnp.bitwise_and(index, LANES - 1)
    row = jnp.right_shift(index, 7)
    found = jnp.zeros(index.shape, jnp.int32)
    for part in range(table_ref.shape[0]):
        entries = jnp.broadcast_to(table_ref[part : part + 1, :], index.shape)
        found = jnp.where(row == part, jnp.take_along_axis(entries, lane, axis=1), found)
    return found


def rows_below(slots, bound):
    return jnp.sum((slots < bound).astype(jnp.float32)).astype(jnp.int32)


def plan_kernel(per_owner, limit, assign_ref, table_ref, slot_ref, start_ref):
    slots = look_up(table_ref, assign_ref[...])
    slot_ref[...] = slots
    for owner in range(start_ref.shape[0]):
        start_ref[owner] = jnp.minimum(rows_below(slots, owner * per_owner), limit)


def make_plan(assign_rows, table, owner_count, per_owner, limit):
    return pl.pallas_call(
        functools.partial(plan_kernel, per_owner, limit),
        out_shape=(
            jax.ShapeDtypeStruct(assign_rows.shape, jnp.int32),
            jax.ShapeDtypeStruct((owner_count,), jnp.int32),
        ),
        in_specs=[in_vmem, in_vmem],
        out_specs=(in_vmem, in_smem),
        compiler_params=params(),
        name="plan",
    )(assign_rows, table)


def unit_kernel(steps, offset, turn, start_ref, me_ref, rows_ref, *refs):
    unit_ref, held, sem = refs[-3:]
    part = unit_ref.shape[0] // steps
    window = part + SUBLANES
    start = start_ref[lax.rem(me_ref[0] + turn, start_ref.shape[0])] + offset

    def first(step):
        return aligned_start(start + step * part, rows_ref.shape[0], window)

    copies = [
        pltpu.make_async_copy(rows_ref.at[pl.ds(first(step), window), :], held.at[step], sem.at[step])
        for step in range(steps)
    ]
    for copy in copies:
        copy.start()
    for step in range(steps):
        copies[step].wait()
        shift = start + step * part - first(step)
        groups = held[step].reshape(window // SUBLANES, SUBLANES, -1)
        turned = pltpu.roll(groups, SUBLANES - shift, 1)
        line = lax.broadcasted_iota(jnp.int32, (part // SUBLANES, SUBLANES, groups.shape[2]), 1)
        values = jnp.where(line < SUBLANES - shift, turned[:-1], turned[1:]).reshape(part, -1)
        scale = lax.rsqrt(jnp.sum(values * values, -1, keepdims=True) + epsilon)
        unit_ref[step * part : (step + 1) * part, :] = (values * scale).astype(jnp.bfloat16)


def unit_piece(starts, me, embeddings, turn, offset, rows, after):
    width = embeddings.shape[1]
    steps = rows // LANES if rows % LANES == 0 else 1
    return pl.pallas_call(
        functools.partial(unit_kernel, steps, offset, turn),
        out_shape=jax.ShapeDtypeStruct((rows, width), jnp.bfloat16),
        in_specs=[in_smem, in_smem, anywhere] + [anywhere] * len(after),
        out_specs=in_vmem,
        scratch_shapes=[
            pltpu.VMEM((steps, rows // steps + SUBLANES, width), jnp.float32),
            pltpu.SemaphoreType.DMA((steps,)),
        ],
        compiler_params=params(),
        cost_estimate=brief,
        name="unit",
    )(starts, me, embeddings, *after)


def hold_until(values, arrived):
    def nothing(*refs):
        pass

    return pl.pallas_call(
        nothing,
        out_shape=jax.ShapeDtypeStruct(values.shape, values.dtype),
        in_specs=[anywhere] * (1 + len(arrived)),
        out_specs=anywhere,
        input_output_aliases={0: 0},
        compiler_params=params(),
        name="hold",
    )(values, *arrived)


def aligned_start(start, row_count, window):
    begin = jnp.minimum(jnp.left_shift(jnp.right_shift(start, 3), 3), row_count - window)
    return pl.multiple_of(begin, SUBLANES)


def flat_window(held, start, rows):
    span = round_up(rows + 1, SUBLANES)
    shift = jnp.bitwise_and(start, LANES - 1)
    block = held[pl.ds(jnp.right_shift(start, 7), span), :]
    turned = pltpu.roll(block, jnp.bitwise_and(LANES - shift, LANES - 1), 1)
    following = pltpu.roll(turned, span - 1, 0)
    lane = lax.broadcasted_iota(jnp.int32, block.shape, 1)
    return jnp.where(lane < LANES - shift, turned, following)


def window_labels(held, slots, owner, start, per_owner, capacity, blocks):
    low = owner * per_owner
    mine = (slots >= low) & (slots < low + per_owner)
    held[: slots.shape[0], :] = jnp.where(mine, slots - low, -1)
    labels = flat_window(held, start, blocks)
    place = lax.broadcasted_iota(jnp.int32, labels.shape, 0) * LANES + lax.broadcasted_iota(
        jnp.int32, labels.shape, 1
    )
    return jnp.where(place < capacity, labels, -1)


def summed_kernel(per_owner, capacity, start_ref, slot_ref, sum_ref, held):
    owner_count = sum_ref.shape[0]
    held[...] = jnp.full(held.shape, -1, jnp.int32)
    slots = slot_ref[...]
    window = capacity + SUBLANES
    wide = sum_ref.shape[1] // LANES
    for owner in range(owner_count):
        aligned = aligned_start(start_ref[owner], slots.size, window)
        labels = window_labels(held, slots, owner, aligned, per_owner, window, wide)
        for block in range(wide):
            sum_ref[owner : owner + 1, block * LANES : (block + 1) * LANES] = labels[block : block + 1, :]


def summed_labels(starts, slots, owner_count, per_owner, capacity):
    return pl.pallas_call(
        functools.partial(summed_kernel, per_owner, capacity),
        out_shape=jax.ShapeDtypeStruct((owner_count, round_up(capacity + SUBLANES, LANES)), jnp.int32),
        in_specs=[in_smem, in_vmem],
        out_specs=in_vmem,
        scratch_shapes=[pltpu.VMEM((slots.shape[0] + 2 * SUBLANES, LANES), jnp.int32)],
        compiler_params=params(),
        name="summed",
    )(starts, slots)


def sent_kernel(per_owner, capacity, start_ref, slot_ref, after_ref, sent_ref, held):
    owner_count, span, _ = sent_ref.shape
    held[...] = jnp.full(held.shape, -1, jnp.int32)
    slots = slot_ref[...]
    for owner in range(owner_count):
        labels = window_labels(held, slots, owner, start_ref[owner], per_owner, capacity, span - 1)
        sent_ref[owner] = labels[:span, :]


def sent_labels(starts, slots, owner_count, per_owner, capacity, after):
    span = round_up(-(-capacity // LANES) + 1, SUBLANES)
    return pl.pallas_call(
        functools.partial(sent_kernel, per_owner, capacity),
        out_shape=jax.ShapeDtypeStruct((owner_count, span, LANES), jnp.int32),
        in_specs=[in_smem, in_vmem, anywhere],
        out_specs=in_vmem,
        scratch_shapes=[pltpu.VMEM((slots.shape[0] + 2 * SUBLANES, LANES), jnp.int32)],
        compiler_params=params(),
        name="sent",
    )(starts, slots, after)


def arrived_kernel(blocks, turns_of, me_ref, got_ref, row_ref, column_ref, tally_ref):
    tally = jnp.zeros((LANES, LANES), jnp.float32)
    cluster = lax.broadcasted_iota(jnp.int32, tally.shape, 0)
    for place, turn in enumerate(turns_of):
        source = lax.rem(me_ref[0] + len(turns_of) - turn, len(turns_of))
        for block in range(blocks):
            line = place * blocks + block
            spread = jnp.broadcast_to(got_ref[source, block : block + 1, :], tally.shape)
            row_ref[line : line + 1, :] = spread[:1, :]
            column_ref[line * LANES : (line + 1) * LANES, :] = spread.T
            tally += (spread == cluster).astype(jnp.float32)
    total = jnp.broadcast_to(jnp.sum(tally, 1, keepdims=True), tally.shape)
    tally_ref[...] = jnp.zeros(tally_ref.shape, jnp.float32)
    tally_ref[:, :LANES] = total.T[:SUBLANES, :]


def arrived_labels(me, got, turns_of, blocks, width):
    lines = len(turns_of) * blocks
    return pl.pallas_call(
        functools.partial(arrived_kernel, blocks, turns_of),
        out_shape=(
            jax.ShapeDtypeStruct((lines, LANES), jnp.int32),
            jax.ShapeDtypeStruct((lines * LANES, LANES), jnp.int32),
            jax.ShapeDtypeStruct((SUBLANES, width), jnp.float32),
        ),
        in_specs=[in_smem, in_vmem],
        out_specs=(in_vmem, in_vmem, in_vmem),
        compiler_params=params(),
        name="arrived",
    )(me, got)


def sum_kernel(start_ref, label_ref, rows_ref, *refs):
    sum_ref, held, sem = refs[-3:]
    owner_count, per_owner, _ = sum_ref.shape
    window = held.shape[1]

    def copy(owner, slot):
        first = aligned_start(start_ref[owner], rows_ref.shape[0], window)
        return pltpu.make_async_copy(rows_ref.at[pl.ds(first, window), :], held.at[slot], sem.at[slot])

    copy(0, 0).start()

    def body(owner, carry):
        slot = lax.rem(owner, 2)

        @pl.when(owner + 1 < owner_count)
        def _():
            copy(owner + 1, 1 - slot).start()

        copy(owner, slot).wait()
        labels = label_ref[pl.ds(owner, 1), :][:, :window]
        cluster = lax.broadcasted_iota(jnp.int32, (per_owner, window), 0)
        member = (labels == cluster).astype(jnp.float32).astype(jnp.bfloat16)
        values = held[slot]
        high = values.astype(jnp.bfloat16)
        rest = values - high.astype(jnp.float32)
        middle = rest.astype(jnp.bfloat16)
        low = (rest - middle.astype(jnp.float32)).astype(jnp.bfloat16)
        total = jnp.dot(member, high, preferred_element_type=jnp.float32)
        total += jnp.dot(member, middle, preferred_element_type=jnp.float32)
        total += jnp.dot(member, low, preferred_element_type=jnp.float32)
        sum_ref[pl.ds(owner, 1)] = total[None]
        return carry

    lax.fori_loop(0, owner_count, body, 0)


def slot_sums(starts, labels, embeddings, per_owner, capacity, after):
    owner_count = labels.shape[0]
    width = embeddings.shape[1]
    return pl.pallas_call(
        sum_kernel,
        out_shape=jax.ShapeDtypeStruct((owner_count, per_owner, width), jnp.float32),
        in_specs=[in_smem, in_vmem, anywhere] + [anywhere] * len(after),
        out_specs=in_vmem,
        scratch_shapes=[
            pltpu.VMEM((2, capacity + SUBLANES, width), jnp.float32),
            pltpu.SemaphoreType.DMA((2,)),
        ],
        compiler_params=params(),
        cost_estimate=pl.CostEstimate(
            flops=6 * owner_count * per_owner * capacity * width,
            bytes_accessed=4 * embeddings.size,
            transcendentals=0,
        ),
        name="sums",
    )(starts, labels, embeddings, *after)


def gram_kernel(begin, rows, wide, after_count, turns_of, *refs):
    chunk_ref, row_ref, column_ref, best_ref, *refs = refs
    flat_ref = centroid_ref = result_ref = None
    if begin:
        flat_ref, *refs = refs
    refs = refs[after_count:]
    if turns_of:
        centroid_ref, me_ref, result_ref, *refs, out_ref, cosine_ref = refs
    else:
        out_ref, flat_ref, *refs = refs
    mine, turned, labels, tiles, even, odd, best, sem, tile_sem = refs
    first = begin // LANES
    size = tiles.shape[2]
    count = round_up(-(-begin // size), 2)

    def line_of(tile):
        return jnp.minimum(tile * (size // LANES), first - size // LANES)

    def fetch(tile):
        start = pl.multiple_of(line_of(tile) * LANES, LANES)
        slot = lax.rem(tile, 4)
        return pltpu.make_async_copy(flat_ref.at[:, pl.ds(start, size)], tiles.at[slot], tile_sem.at[slot])

    chunk_copy = pltpu.make_async_copy(chunk_ref, mine.at[pl.ds(0, rows), :], sem.at[0])
    label_copy = pltpu.make_async_copy(column_ref.at[pl.ds(begin, wide), :], labels, sem.at[1])
    chunk_copy.start()
    label_copy.start()
    for tile in range(min(count, 3)):
        fetch(jnp.int32(tile)).start()
    if rows < wide:
        mine[rows:wide, :] = jnp.zeros((wide - rows, mine.shape[1]), mine.dtype)
    if turns_of:
        mine[wide:, :] = centroid_ref[...]
        cosine_ref[...] = jnp.zeros(cosine_ref.shape, jnp.float32)
    out_ref[...] = best_ref[...]
    best[...] = jnp.full(best.shape, -2.0, jnp.float32)
    chunk_copy.wait()
    label_copy.wait()
    turned[...] = mine[:wide, :].T
    if not turns_of:
        flat_copy = pltpu.make_async_copy(turned, flat_ref.at[:, pl.ds(begin, wide)], sem.at[2])
        flat_copy.start()

    def products(right):
        return jnp.dot(mine[...], right, preferred_element_type=jnp.float32)

    def cosines(values, line):
        cluster = lax.broadcasted_iota(jnp.int32, values.shape, 0)
        own = jnp.where(row_ref[pl.ds(line, 1), :] == cluster, values, 0.0)
        cosine_ref[pl.ds(line, 1), :] = jnp.sum(own, 0, keepdims=True)

    def reduce_tile(held, tile):
        parts = range(size // LANES)
        lines = [line_of(tile) + part for part in parts]
        tops = [jnp.full((SUBLANES, LANES), -2.0, jnp.float32) for _ in parts]
        against = [jnp.broadcast_to(row_ref[pl.ds(line, 1), :], (LANES, LANES)) for line in lines]
        for begin_row in range(0, wide, LANES):
            span = slice(begin_row, begin_row + LANES)
            own = labels[span, :]
            fold = best[span, :]
            for part in parts:
                near = jnp.where(own == against[part], held[span, part * LANES : (part + 1) * LANES], -2.0)
                fold = jnp.maximum(fold, near)
                tops[part] = jnp.maximum(tops[part], jnp.max(near.reshape(-1, SUBLANES, LANES), 0))
            best[span, :] = fold
        for part in parts:
            out_ref[pl.ds(lines[part], 1), :] = jnp.maximum(
                out_ref[pl.ds(lines[part], 1), :], jnp.max(tops[part], 0, keepdims=True)
            )
            if turns_of:
                cosines(held[wide:, part * LANES : (part + 1) * LANES], lines[part])

    if begin:
        fetch(jnp.int32(0)).wait()
        even[...] = products(tiles[0])

        def body(pair, carry):
            tile = pair * 2
            fetch(tile + 1).wait()
            fetch(tile + 3).start()
            odd[...] = products(tiles[lax.rem(tile + 1, 4)])
            reduce_tile(even, tile)
            fetch(tile + 2).wait()

            @pl.when(tile + 4 < count)
            def _():
                fetch(tile + 4).start()

            even[...] = products(tiles[lax.rem(tile + 2, 4)])
            reduce_tile(odd, tile + 1)
            return carry

        lax.fori_loop(0, count // 2 - 1, body, 0)
        fetch(jnp.int32(count - 1)).wait()
        odd[...] = products(tiles[(count - 1) % 4])
        reduce_tile(even, jnp.int32(count - 2))
        reduce_tile(odd, jnp.int32(count - 1))
    own = products(turned[...])
    row = lax.broadcasted_iota(jnp.int32, (wide, LANES), 0)
    column = lax.broadcasted_iota(jnp.int32, (wide, LANES), 1)
    for block in range(wide // LANES):
        line = first + block
        here = slice(block * LANES, (block + 1) * LANES)
        allowed = (labels[...] == row_ref[line : line + 1, :]) & (row != column + block * LANES)
        near = jnp.max(jnp.where(allowed, own[:wide, here], -2.0), 0, keepdims=True)
        other = jnp.max(best[here, :].T, 0, keepdims=True)
        out_ref[line : line + 1, :] = jnp.maximum(near, other)
        if turns_of:
            cosines(own[wide:, here], line)
    if turns_of:
        blocks = row_ref.shape[0] // len(turns_of)
        half = result_ref.shape[1] // 2
        result_ref[...] = jnp.zeros(result_ref.shape, jnp.float32)
        for place, turn in enumerate(turns_of):
            source = lax.rem(me_ref[0] + len(turns_of) - turn, len(turns_of))
            lines = slice(place * blocks, (place + 1) * blocks)
            result_ref[source, :blocks, :] = out_ref[lines, :]
            result_ref[source, half : half + blocks, :] = cosine_ref[lines, :]
    else:
        flat_copy.wait()


def gram_step(rows, columns, best, flat, chunk, begin, after=(), final=None):
    length, width = chunk.shape
    wide = round_up(length, LANES)
    tall = wide
    size = min(TILE, begin) if begin else LANES
    flat_shape = jax.ShapeDtypeStruct((width, columns.shape[0]), jnp.bfloat16)
    inputs = [chunk, rows, columns, best]
    in_specs = [anywhere, in_vmem, anywhere, in_vmem]
    aliases = {}
    if begin:
        if not final:
            aliases = {len(inputs): 1}
        inputs.append(flat)
        in_specs.append(anywhere)
    inputs += after
    in_specs += [anywhere] * len(after)
    out_shape = (jax.ShapeDtypeStruct(best.shape, jnp.float32), flat_shape)
    out_specs = (in_vmem, anywhere)
    turns_of = ()
    extra = []
    if final:
        centroid_unit, me, turns_of = final
        tall += centroid_unit.shape[0]
        inputs += [centroid_unit, me]
        in_specs += [in_vmem, in_smem]
        half = round_up(rows.shape[0] // len(turns_of) + 1, SUBLANES)
        out_shape = jax.ShapeDtypeStruct((len(turns_of), 2 * half, LANES), jnp.float32)
        out_specs = in_vmem
        extra = [pltpu.VMEM(best.shape, jnp.float32)] * 2
    return pl.pallas_call(
        functools.partial(gram_kernel, begin, length, wide, len(after), turns_of),
        out_shape=out_shape,
        in_specs=in_specs,
        out_specs=out_specs,
        scratch_shapes=[
            pltpu.VMEM((tall, width), jnp.bfloat16),
            pltpu.VMEM((width, wide), jnp.bfloat16),
            pltpu.VMEM((wide, LANES), jnp.int32),
            pltpu.VMEM((4, width, size), jnp.bfloat16),
            pltpu.VMEM((tall, size), jnp.float32),
            pltpu.VMEM((tall, size), jnp.float32),
            pltpu.VMEM((wide, LANES), jnp.float32),
            pltpu.SemaphoreType.DMA((3,)),
            pltpu.SemaphoreType.DMA((4,)),
        ]
        + extra,
        input_output_aliases=aliases,
        compiler_params=params(),
        cost_estimate=brief,
        name="gram",
    )(*inputs)


def pack_kernel(share_ref, tally_ref, *refs):
    packed_ref = refs[-1]
    packed_ref[: share_ref.shape[0], :] = share_ref[...]
    packed_ref[share_ref.shape[0] :, :] = tally_ref[...]


def pack_share(share, tally, after):
    length = share.shape[0] + tally.shape[0]
    return pl.pallas_call(
        pack_kernel,
        out_shape=jax.ShapeDtypeStruct((length, share.shape[1]), jnp.float32),
        in_specs=[in_vmem, in_vmem] + [anywhere] * len(after),
        out_specs=in_vmem,
        compiler_params=params(),
        name="pack",
    )(share, tally, *after)


def centroid_kernel(gathered_ref, centroid_ref, unit_ref):
    groups, length, width = gathered_ref.shape
    share = length - SUBLANES
    per_owner = centroid_ref.shape[0]
    tally = jnp.sum(gathered_ref[:, share, :LANES], 0, keepdims=True)
    column = jnp.broadcast_to(tally, (LANES, LANES)).T[:per_owner, :]
    sums = jnp.concatenate([gathered_ref[group, :share, :] for group in range(groups)], 0)
    centroids = sums / jnp.concatenate([column] * (width // LANES), 1)
    centroid_ref[...] = centroids
    scale = lax.rsqrt(jnp.sum(centroids * centroids, -1, keepdims=True) + epsilon)
    unit_ref[...] = (centroids * scale).astype(jnp.bfloat16)


def make_centroids(gathered, per_owner):
    shape = (per_owner, gathered.shape[2])
    return pl.pallas_call(
        centroid_kernel,
        out_shape=(
            jax.ShapeDtypeStruct(shape, jnp.float32),
            jax.ShapeDtypeStruct(shape, jnp.bfloat16),
        ),
        in_specs=[in_vmem],
        out_specs=(in_vmem, in_vmem),
        compiler_params=params(),
        name="centroids",
    )(gathered)


def place_kernel(per_owner, start_ref, slot_ref, back_ref, near_ref, cosine_ref, held, result):
    owner_count, double, _ = back_ref.shape
    span = double // 2
    rows = slot_ref.shape[0]
    held[...] = jnp.full(held.shape, -1, jnp.int32)
    held[:rows, :] = slot_ref[...]
    result[...] = jnp.zeros(result.shape, jnp.float32)
    lane = lax.broadcasted_iota(jnp.int32, (span, LANES), 1)
    for owner in range(owner_count):
        start = start_ref[owner]
        first = pl.ds(jnp.right_shift(start, 7), span)
        shift = jnp.bitwise_and(start, LANES - 1)
        slots = held[first, :]
        mine = (slots >= owner * per_owner) & (slots < (owner + 1) * per_owner)
        for kind in range(2):
            turned = pltpu.roll(back_ref[owner, kind * span : (kind + 1) * span, :], shift, 1)
            earlier = pltpu.roll(turned, 1, 0)
            moved = jnp.where(lane >= shift, turned, earlier)
            result[kind, first, :] = jnp.where(mine, moved, result[kind, first, :])
    near_ref[...] = result[0, :rows, :]
    cosine_ref[...] = result[1, :rows, :]


def place_rows(starts, slots, back, per_owner):
    span = back.shape[1] // 2
    rows = slots.shape[0]
    return pl.pallas_call(
        functools.partial(place_kernel, per_owner),
        out_shape=(jax.ShapeDtypeStruct(slots.shape, jnp.float32),) * 2,
        in_specs=[in_smem, in_vmem, in_vmem],
        out_specs=(in_vmem, in_vmem),
        scratch_shapes=[
            pltpu.VMEM((rows + span, LANES), jnp.int32),
            pltpu.VMEM((2, rows + span, LANES), jnp.float32),
        ],
        compiler_params=params(),
        name="place",
    )(starts, slots, back)


def turns(count):
    order = sorted(range(count), key=lambda turn: (min(turn, count - turn), turn))
    if count == 8:
        order = [0, 1, 2, 3, 6, 7, 5, 4]
    return order


def per_device(embeddings, assign, cluster_slot):
    row_count, width = embeddings.shape
    owner_count = lax.axis_size("docs")
    per_owner = cluster_slot.shape[0] // owner_count
    capacity = row_count // owner_count + row_count // (4 * owner_count)
    padded = round_up(capacity, LANES)
    blocks = padded // LANES
    me = lax.axis_index("docs").astype(jnp.int32).reshape(1)
    turns_of = turns(owner_count)

    slots, starts = make_plan(
        assign.reshape(-1, LANES), cluster_slot.reshape(-1, LANES), owner_count, per_owner, row_count - capacity
    )

    sent, chunks = [], []
    for place, turn in enumerate(turns_of):
        piece = unit_piece(starts, me, embeddings, turn, 0, capacity, sent[-1:] if place > 1 else [])
        if place == 5:
            sum_labels = summed_labels(starts, slots, owner_count, per_owner, capacity)
            partial_sums = slot_sums(starts, sum_labels, embeddings, per_owner, capacity, sent[1:])
            partial_sums = hold_until(partial_sums, chunks[1:3])
            wire_labels = sent_labels(starts, slots, owner_count, per_owner, capacity, partial_sums)
            got_labels = lax.all_to_all(wire_labels, "docs", split_axis=0, concat_axis=0, tiled=True)
            piece = hold_until(piece, [got_labels])
        sent.append(piece)
        if turn:
            piece = lax.ppermute(piece, "docs", [(i, (i + turn) % owner_count) for i in range(owner_count)])
        chunks.append(piece)
    rows, columns, group_tally = arrived_labels(me, got_labels, turns_of, blocks, width)
    group_share = lax.psum_scatter(partial_sums, "grp", scatter_dimension=1, tiled=True)
    group_share = hold_until(group_share, chunks[3:5])
    share = lax.psum_scatter(group_share, "docs", scatter_dimension=0, tiled=True)[0]

    bests = [jnp.full((owner_count * blocks, LANES), -2.0, jnp.float32)]
    flat = None
    for place in range(owner_count - 1):
        best, flat = gram_step(rows, columns, bests[-1], flat, chunks[place], place * padded)
        bests.append(best)
    packed = pack_share(share, group_tally, bests[-3:-2])
    centroids, centroid_unit = make_centroids(lax.all_gather(packed, "grp"), per_owner)
    results = gram_step(
        rows, columns, bests[-1], flat, chunks[-1], (owner_count - 1) * padded, final=(centroid_unit, me, turns_of)
    )
    back = lax.all_to_all(results, "docs", split_axis=0, concat_axis=0, tiled=True)
    near, cosine = place_rows(starts, slots, back, per_owner)
    return (centroids, near.reshape(-1), cosine.reshape(-1))


def solution(mesh):
    placed = (P(("grp", "docs"), None), P(("grp", "docs")), P())
    return jax.shard_map(
        per_device,
        mesh=mesh,
        in_specs=placed,
        out_specs=(P("docs", None), P(("grp", "docs")), P(("grp", "docs"))),
        check_vma=False,
    )
```

```python
import functools

import jax
import jax.numpy as jnp
from jax import lax
from jax.experimental import pallas as pl
from jax.experimental.pallas import tpu as pltpu
from jax.sharding import PartitionSpec as P

epsilon = 1e-06
LANES = 128
SUBLANES = 8
MIB = 1024 * 1024
TILE = 512
in_vmem = pl.BlockSpec(memory_space=pltpu.VMEM)
in_smem = pl.BlockSpec(memory_space=pltpu.SMEM)
anywhere = pl.BlockSpec(memory_space=pl.ANY)
brief = pl.CostEstimate(flops=1000, bytes_accessed=1000, transcendentals=0)


def round_up(value, step):
    return -(-value // step) * step


def params(mib=44):
    return pltpu.CompilerParams(vmem_limit_bytes=mib * MIB)


def look_up(table_ref, index):
    lane = jnp.bitwise_and(index, LANES - 1)
    row = jnp.right_shift(index, 7)
    found = jnp.zeros(index.shape, jnp.int32)
    for part in range(table_ref.shape[0]):
        entries = jnp.broadcast_to(table_ref[part : part + 1, :], index.shape)
        found = jnp.where(row == part, jnp.take_along_axis(entries, lane, axis=1), found)
    return found


def rows_below(slots, bound):
    return jnp.sum((slots < bound).astype(jnp.float32)).astype(jnp.int32)


def plan_kernel(per_owner, limit, assign_ref, table_ref, slot_ref, start_ref):
    slots = look_up(table_ref, assign_ref[...])
    slot_ref[...] = slots
    for owner in range(start_ref.shape[0]):
        start_ref[owner] = jnp.minimum(rows_below(slots, owner * per_owner), limit)


def make_plan(assign_rows, table, owner_count, per_owner, limit):
    return pl.pallas_call(
        functools.partial(plan_kernel, per_owner, limit),
        out_shape=(
            jax.ShapeDtypeStruct(assign_rows.shape, jnp.int32),
            jax.ShapeDtypeStruct((owner_count,), jnp.int32),
        ),
        in_specs=[in_vmem, in_vmem],
        out_specs=(in_vmem, in_smem),
        compiler_params=params(8),
        name="plan",
    )(assign_rows, table)


def unit_kernel(steps, offset, turn, start_ref, me_ref, rows_ref, *refs):
    unit_ref, held, sem = refs[-3:]
    part = unit_ref.shape[0] // steps
    window = part + SUBLANES
    start = start_ref[lax.rem(me_ref[0] + turn, start_ref.shape[0])] + offset

    def first(step):
        return aligned_start(start + step * part, rows_ref.shape[0], window)

    copies = [
        pltpu.make_async_copy(rows_ref.at[pl.ds(first(step), window), :], held.at[step], sem.at[step])
        for step in range(steps)
    ]
    for copy in copies:
        copy.start()
    for step in range(steps):
        copies[step].wait()
        shift = start + step * part - first(step)
        groups = held[step].reshape(window // SUBLANES, SUBLANES, -1)
        turned = pltpu.roll(groups, SUBLANES - shift, 1)
        line = lax.broadcasted_iota(jnp.int32, (part // SUBLANES, SUBLANES, groups.shape[2]), 1)
        values = jnp.where(line < SUBLANES - shift, turned[:-1], turned[1:]).reshape(part, -1)
        scale = lax.rsqrt(jnp.sum(values * values, -1, keepdims=True) + epsilon)
        unit_ref[step * part : (step + 1) * part, :] = (values * scale).astype(jnp.bfloat16)


def unit_piece(starts, me, embeddings, turn, offset, rows, after):
    width = embeddings.shape[1]
    steps = rows // LANES if rows % LANES == 0 else 1
    return pl.pallas_call(
        functools.partial(unit_kernel, steps, offset, turn),
        out_shape=jax.ShapeDtypeStruct((rows, width), jnp.bfloat16),
        in_specs=[in_smem, in_smem, anywhere] + [anywhere] * len(after),
        out_specs=in_vmem,
        scratch_shapes=[
            pltpu.VMEM((steps, rows // steps + SUBLANES, width), jnp.float32),
            pltpu.SemaphoreType.DMA((steps,)),
        ],
        compiler_params=params(),
        cost_estimate=brief,
        name="unit",
    )(starts, me, embeddings, *after)


def hold_until(values, arrived):
    def nothing(*refs):
        pass

    return pl.pallas_call(
        nothing,
        out_shape=jax.ShapeDtypeStruct(values.shape, values.dtype),
        in_specs=[anywhere] * (1 + len(arrived)),
        out_specs=anywhere,
        input_output_aliases={0: 0},
        compiler_params=params(8),
        name="hold",
    )(values, *arrived)


def aligned_start(start, row_count, window):
    begin = jnp.minimum(jnp.left_shift(jnp.right_shift(start, 3), 3), row_count - window)
    return pl.multiple_of(begin, SUBLANES)


def flat_window(held, start, rows):
    span = round_up(rows + 1, SUBLANES)
    shift = jnp.bitwise_and(start, LANES - 1)
    block = held[pl.ds(jnp.right_shift(start, 7), span), :]
    turned = pltpu.roll(block, jnp.bitwise_and(LANES - shift, LANES - 1), 1)
    following = pltpu.roll(turned, span - 1, 0)
    lane = lax.broadcasted_iota(jnp.int32, block.shape, 1)
    return jnp.where(lane < LANES - shift, turned, following)


def window_labels(held, slots, owner, start, per_owner, capacity, blocks):
    low = owner * per_owner
    mine = (slots >= low) & (slots < low + per_owner)
    held[: slots.shape[0], :] = jnp.where(mine, slots - low, -1)
    labels = flat_window(held, start, blocks)
    place = lax.broadcasted_iota(jnp.int32, labels.shape, 0) * LANES + lax.broadcasted_iota(
        jnp.int32, labels.shape, 1
    )
    return jnp.where(place < capacity, labels, -1)


def summed_kernel(per_owner, capacity, start_ref, slot_ref, sum_ref, held):
    owner_count = sum_ref.shape[0]
    held[...] = jnp.full(held.shape, -1, jnp.int32)
    slots = slot_ref[...]
    window = capacity + SUBLANES
    wide = sum_ref.shape[1] // LANES
    for owner in range(owner_count):
        aligned = aligned_start(start_ref[owner], slots.size, window)
        labels = window_labels(held, slots, owner, aligned, per_owner, window, wide)
        for block in range(wide):
            sum_ref[owner : owner + 1, block * LANES : (block + 1) * LANES] = labels[block : block + 1, :]


def summed_labels(starts, slots, owner_count, per_owner, capacity):
    return pl.pallas_call(
        functools.partial(summed_kernel, per_owner, capacity),
        out_shape=jax.ShapeDtypeStruct((owner_count, round_up(capacity + SUBLANES, LANES)), jnp.int32),
        in_specs=[in_smem, in_vmem],
        out_specs=in_vmem,
        scratch_shapes=[pltpu.VMEM((slots.shape[0] + 2 * SUBLANES, LANES), jnp.int32)],
        compiler_params=params(8),
        name="summed",
    )(starts, slots)


def sent_kernel(per_owner, capacity, start_ref, slot_ref, after_ref, sent_ref, held):
    owner_count, span, _ = sent_ref.shape
    held[...] = jnp.full(held.shape, -1, jnp.int32)
    slots = slot_ref[...]
    for owner in range(owner_count):
        labels = window_labels(held, slots, owner, start_ref[owner], per_owner, capacity, span - 1)
        sent_ref[owner] = labels[:span, :]


def sent_labels(starts, slots, owner_count, per_owner, capacity, after):
    span = round_up(-(-capacity // LANES) + 1, SUBLANES)
    return pl.pallas_call(
        functools.partial(sent_kernel, per_owner, capacity),
        out_shape=jax.ShapeDtypeStruct((owner_count, span, LANES), jnp.int32),
        in_specs=[in_smem, in_vmem, anywhere],
        out_specs=in_vmem,
        scratch_shapes=[pltpu.VMEM((slots.shape[0] + 2 * SUBLANES, LANES), jnp.int32)],
        compiler_params=params(8),
        name="sent",
    )(starts, slots, after)


def arrived_kernel(blocks, turns_of, me_ref, got_ref, row_ref, column_ref, tally_ref):
    tally = jnp.zeros((LANES, LANES), jnp.float32)
    cluster = lax.broadcasted_iota(jnp.int32, tally.shape, 0)
    for place, turn in enumerate(turns_of):
        source = lax.rem(me_ref[0] + len(turns_of) - turn, len(turns_of))
        for block in range(blocks):
            line = place * blocks + block
            spread = jnp.broadcast_to(got_ref[source, block : block + 1, :], tally.shape)
            row_ref[line : line + 1, :] = spread[:1, :]
            column_ref[line * LANES : (line + 1) * LANES, :] = spread.T
            tally += (spread == cluster).astype(jnp.float32)
    total = jnp.broadcast_to(jnp.sum(tally, 1, keepdims=True), tally.shape)
    tally_ref[...] = jnp.zeros(tally_ref.shape, jnp.float32)
    tally_ref[:, :LANES] = total.T[:SUBLANES, :]


def arrived_labels(me, got, turns_of, blocks, width):
    lines = len(turns_of) * blocks
    return pl.pallas_call(
        functools.partial(arrived_kernel, blocks, turns_of),
        out_shape=(
            jax.ShapeDtypeStruct((lines, LANES), jnp.int32),
            jax.ShapeDtypeStruct((lines * LANES, LANES), jnp.int32),
            jax.ShapeDtypeStruct((SUBLANES, width), jnp.float32),
        ),
        in_specs=[in_smem, in_vmem],
        out_specs=(in_vmem, in_vmem, in_vmem),
        compiler_params=params(8),
        name="arrived",
    )(me, got)


def sum_kernel(start_ref, label_ref, rows_ref, *refs):
    sum_ref, held, sem = refs[-3:]
    owner_count, per_owner, _ = sum_ref.shape
    window = held.shape[1]

    def copy(owner, slot):
        first = aligned_start(start_ref[owner], rows_ref.shape[0], window)
        return pltpu.make_async_copy(rows_ref.at[pl.ds(first, window), :], held.at[slot], sem.at[slot])

    copy(0, 0).start()

    def body(owner, carry):
        slot = lax.rem(owner, 2)

        @pl.when(owner + 1 < owner_count)
        def _():
            copy(owner + 1, 1 - slot).start()

        copy(owner, slot).wait()
        labels = label_ref[pl.ds(owner, 1), :][:, :window]
        cluster = lax.broadcasted_iota(jnp.int32, (per_owner, window), 0)
        member = (labels == cluster).astype(jnp.float32).astype(jnp.bfloat16)
        values = held[slot]
        high = values.astype(jnp.bfloat16)
        rest = values - high.astype(jnp.float32)
        middle = rest.astype(jnp.bfloat16)
        low = (rest - middle.astype(jnp.float32)).astype(jnp.bfloat16)
        total = jnp.dot(member, high, preferred_element_type=jnp.float32)
        total += jnp.dot(member, middle, preferred_element_type=jnp.float32)
        total += jnp.dot(member, low, preferred_element_type=jnp.float32)
        sum_ref[pl.ds(owner, 1)] = total[None]
        return carry

    lax.fori_loop(0, owner_count, body, 0)


def slot_sums(starts, labels, embeddings, per_owner, capacity, after):
    owner_count = labels.shape[0]
    width = embeddings.shape[1]
    return pl.pallas_call(
        sum_kernel,
        out_shape=jax.ShapeDtypeStruct((owner_count, per_owner, width), jnp.float32),
        in_specs=[in_smem, in_vmem, anywhere] + [anywhere] * len(after),
        out_specs=in_vmem,
        scratch_shapes=[
            pltpu.VMEM((2, capacity + SUBLANES, width), jnp.float32),
            pltpu.SemaphoreType.DMA((2,)),
        ],
        compiler_params=params(),
        cost_estimate=pl.CostEstimate(
            flops=6 * owner_count * per_owner * capacity * width,
            bytes_accessed=4 * embeddings.size,
            transcendentals=0,
        ),
        name="sums",
    )(starts, labels, embeddings, *after)


def gram_kernel(begin, rows, wide, after_count, turns_of, *refs):
    chunk_ref, row_ref, column_ref, best_ref, *refs = refs
    flat_ref = centroid_ref = result_ref = None
    if begin:
        flat_ref, *refs = refs
    refs = refs[after_count:]
    if turns_of:
        centroid_ref, me_ref, result_ref, *refs, out_ref, cosine_ref = refs
    else:
        out_ref, flat_ref, *refs = refs
    mine, turned, labels, tiles, even, odd, best, sem, tile_sem = refs
    first = begin // LANES
    size = tiles.shape[2]
    count = round_up(-(-begin // size), 2)

    def line_of(tile):
        return jnp.minimum(tile * (size // LANES), first - size // LANES)

    def fetch(tile):
        start = pl.multiple_of(line_of(tile) * LANES, LANES)
        slot = lax.rem(tile, 4)
        return pltpu.make_async_copy(flat_ref.at[:, pl.ds(start, size)], tiles.at[slot], tile_sem.at[slot])

    chunk_copy = pltpu.make_async_copy(chunk_ref, mine.at[pl.ds(0, rows), :], sem.at[0])
    label_copy = pltpu.make_async_copy(column_ref.at[pl.ds(begin, wide), :], labels, sem.at[1])
    chunk_copy.start()
    label_copy.start()
    for tile in range(min(count, 3)):
        fetch(jnp.int32(tile)).start()
    if rows < wide:
        mine[rows:wide, :] = jnp.zeros((wide - rows, mine.shape[1]), mine.dtype)
    if turns_of:
        mine[wide:, :] = centroid_ref[...]
        cosine_ref[...] = jnp.zeros(cosine_ref.shape, jnp.float32)
    out_ref[...] = best_ref[...]
    best[...] = jnp.full(best.shape, -2.0, jnp.float32)
    chunk_copy.wait()
    label_copy.wait()
    turned[...] = mine[:wide, :].T
    if not turns_of:
        flat_copy = pltpu.make_async_copy(turned, flat_ref.at[:, pl.ds(begin, wide)], sem.at[2])
        flat_copy.start()

    def products(right):
        return jnp.dot(mine[...], right, preferred_element_type=jnp.float32)

    def cosines(values, line):
        cluster = lax.broadcasted_iota(jnp.int32, values.shape, 0)
        own = jnp.where(row_ref[pl.ds(line, 1), :] == cluster, values, 0.0)
        cosine_ref[pl.ds(line, 1), :] = jnp.sum(own, 0, keepdims=True)

    def reduce_tile(held, tile):
        parts = range(size // LANES)
        lines = [line_of(tile) + part for part in parts]
        tops = [jnp.full((SUBLANES, LANES), -2.0, jnp.float32) for _ in parts]
        against = [jnp.broadcast_to(row_ref[pl.ds(line, 1), :], (LANES, LANES)) for line in lines]
        for begin_row in range(0, wide, LANES):
            span = slice(begin_row, begin_row + LANES)
            own = labels[span, :]
            fold = best[span, :]
            for part in parts:
                near = jnp.where(own == against[part], held[span, part * LANES : (part + 1) * LANES], -2.0)
                fold = jnp.maximum(fold, near)
                tops[part] = jnp.maximum(tops[part], jnp.max(near.reshape(-1, SUBLANES, LANES), 0))
            best[span, :] = fold
        for part in parts:
            out_ref[pl.ds(lines[part], 1), :] = jnp.maximum(
                out_ref[pl.ds(lines[part], 1), :], jnp.max(tops[part], 0, keepdims=True)
            )
            if turns_of:
                cosines(held[wide:, part * LANES : (part + 1) * LANES], lines[part])

    if begin:
        fetch(jnp.int32(0)).wait()
        even[...] = products(tiles[0])

        def body(pair, carry):
            tile = pair * 2
            fetch(tile + 1).wait()
            fetch(tile + 3).start()
            odd[...] = products(tiles[lax.rem(tile + 1, 4)])
            reduce_tile(even, tile)
            fetch(tile + 2).wait()

            @pl.when(tile + 4 < count)
            def _():
                fetch(tile + 4).start()

            even[...] = products(tiles[lax.rem(tile + 2, 4)])
            reduce_tile(odd, tile + 1)
            return carry

        lax.fori_loop(0, count // 2 - 1, body, 0)
        fetch(jnp.int32(count - 1)).wait()
        odd[...] = products(tiles[(count - 1) % 4])
        reduce_tile(even, jnp.int32(count - 2))
        reduce_tile(odd, jnp.int32(count - 1))
    own = products(turned[...])
    row = lax.broadcasted_iota(jnp.int32, (wide, LANES), 0)
    column = lax.broadcasted_iota(jnp.int32, (wide, LANES), 1)
    for block in range(wide // LANES):
        line = first + block
        here = slice(block * LANES, (block + 1) * LANES)
        allowed = (labels[...] == row_ref[line : line + 1, :]) & (row != column + block * LANES)
        near = jnp.max(jnp.where(allowed, own[:wide, here], -2.0), 0, keepdims=True)
        other = jnp.max(best[here, :].T, 0, keepdims=True)
        out_ref[line : line + 1, :] = jnp.maximum(near, other)
        if turns_of:
            cosines(own[wide:, here], line)
    if turns_of:
        blocks = row_ref.shape[0] // len(turns_of)
        half = result_ref.shape[1] // 2
        result_ref[...] = jnp.zeros(result_ref.shape, jnp.float32)
        for place, turn in enumerate(turns_of):
            source = lax.rem(me_ref[0] + len(turns_of) - turn, len(turns_of))
            lines = slice(place * blocks, (place + 1) * blocks)
            result_ref[source, :blocks, :] = out_ref[lines, :]
            result_ref[source, half : half + blocks, :] = cosine_ref[lines, :]
    else:
        flat_copy.wait()


def gram_step(rows, columns, best, flat, chunk, begin, after=(), final=None):
    length, width = chunk.shape
    wide = round_up(length, LANES)
    tall = wide
    size = min(TILE, begin) if begin else LANES
    flat_shape = jax.ShapeDtypeStruct((width, columns.shape[0]), jnp.bfloat16)
    inputs = [chunk, rows, columns, best]
    in_specs = [anywhere, in_vmem, anywhere, in_vmem]
    aliases = {}
    if begin:
        if not final:
            aliases = {len(inputs): 1}
        inputs.append(flat)
        in_specs.append(anywhere)
    inputs += after
    in_specs += [anywhere] * len(after)
    out_shape = (jax.ShapeDtypeStruct(best.shape, jnp.float32), flat_shape)
    out_specs = (in_vmem, anywhere)
    turns_of = ()
    extra = []
    if final:
        centroid_unit, me, turns_of = final
        tall += centroid_unit.shape[0]
        inputs += [centroid_unit, me]
        in_specs += [in_vmem, in_smem]
        half = round_up(rows.shape[0] // len(turns_of) + 1, SUBLANES)
        out_shape = jax.ShapeDtypeStruct((len(turns_of), 2 * half, LANES), jnp.float32)
        out_specs = in_vmem
        extra = [pltpu.VMEM(best.shape, jnp.float32)] * 2
    return pl.pallas_call(
        functools.partial(gram_kernel, begin, length, wide, len(after), turns_of),
        out_shape=out_shape,
        in_specs=in_specs,
        out_specs=out_specs,
        scratch_shapes=[
            pltpu.VMEM((tall, width), jnp.bfloat16),
            pltpu.VMEM((width, wide), jnp.bfloat16),
            pltpu.VMEM((wide, LANES), jnp.int32),
            pltpu.VMEM((4, width, size), jnp.bfloat16),
            pltpu.VMEM((tall, size), jnp.float32),
            pltpu.VMEM((tall, size), jnp.float32),
            pltpu.VMEM((wide, LANES), jnp.float32),
            pltpu.SemaphoreType.DMA((3,)),
            pltpu.SemaphoreType.DMA((4,)),
        ]
        + extra,
        input_output_aliases=aliases,
        compiler_params=params(),
        cost_estimate=brief,
        name="gram",
    )(*inputs)


def pack_kernel(share_ref, tally_ref, *refs):
    packed_ref = refs[-1]
    packed_ref[: share_ref.shape[0], :] = share_ref[...]
    packed_ref[share_ref.shape[0] :, :] = tally_ref[...]


def pack_share(share, tally, after):
    length = share.shape[0] + tally.shape[0]
    return pl.pallas_call(
        pack_kernel,
        out_shape=jax.ShapeDtypeStruct((length, share.shape[1]), jnp.float32),
        in_specs=[in_vmem, in_vmem] + [anywhere] * len(after),
        out_specs=in_vmem,
        compiler_params=params(8),
        name="pack",
    )(share, tally, *after)


def centroid_kernel(gathered_ref, centroid_ref, unit_ref):
    groups, length, width = gathered_ref.shape
    share = length - SUBLANES
    per_owner = centroid_ref.shape[0]
    tally = jnp.sum(gathered_ref[:, share, :LANES], 0, keepdims=True)
    column = jnp.broadcast_to(tally, (LANES, LANES)).T[:per_owner, :]
    sums = jnp.concatenate([gathered_ref[group, :share, :] for group in range(groups)], 0)
    centroids = sums / jnp.concatenate([column] * (width // LANES), 1)
    centroid_ref[...] = centroids
    scale = lax.rsqrt(jnp.sum(centroids * centroids, -1, keepdims=True) + epsilon)
    unit_ref[...] = (centroids * scale).astype(jnp.bfloat16)


def make_centroids(gathered, per_owner):
    shape = (per_owner, gathered.shape[2])
    return pl.pallas_call(
        centroid_kernel,
        out_shape=(
            jax.ShapeDtypeStruct(shape, jnp.float32),
            jax.ShapeDtypeStruct(shape, jnp.bfloat16),
        ),
        in_specs=[in_vmem],
        out_specs=(in_vmem, in_vmem),
        compiler_params=params(8),
        name="centroids",
    )(gathered)


def place_kernel(per_owner, start_ref, slot_ref, back_ref, near_ref, cosine_ref, held, result):
    owner_count, double, _ = back_ref.shape
    span = double // 2
    rows = slot_ref.shape[0]
    held[...] = jnp.full(held.shape, -1, jnp.int32)
    held[:rows, :] = slot_ref[...]
    result[...] = jnp.zeros(result.shape, jnp.float32)
    lane = lax.broadcasted_iota(jnp.int32, (span, LANES), 1)
    for owner in range(owner_count):
        start = start_ref[owner]
        first = pl.ds(jnp.right_shift(start, 7), span)
        shift = jnp.bitwise_and(start, LANES - 1)
        slots = held[first, :]
        mine = (slots >= owner * per_owner) & (slots < (owner + 1) * per_owner)
        for kind in range(2):
            turned = pltpu.roll(back_ref[owner, kind * span : (kind + 1) * span, :], shift, 1)
            earlier = pltpu.roll(turned, 1, 0)
            moved = jnp.where(lane >= shift, turned, earlier)
            result[kind, first, :] = jnp.where(mine, moved, result[kind, first, :])
    near_ref[...] = result[0, :rows, :]
    cosine_ref[...] = result[1, :rows, :]


def place_rows(starts, slots, back, per_owner):
    span = back.shape[1] // 2
    rows = slots.shape[0]
    return pl.pallas_call(
        functools.partial(place_kernel, per_owner),
        out_shape=(jax.ShapeDtypeStruct(slots.shape, jnp.float32),) * 2,
        in_specs=[in_smem, in_vmem, in_vmem],
        out_specs=(in_vmem, in_vmem),
        scratch_shapes=[
            pltpu.VMEM((rows + span, LANES), jnp.int32),
            pltpu.VMEM((2, rows + span, LANES), jnp.float32),
        ],
        compiler_params=params(8),
        name="place",
    )(starts, slots, back)


def turns(count):
    order = sorted(range(count), key=lambda turn: (min(turn, count - turn), turn))
    if count == 8:
        order = [0, 1, 2, 3, 6, 7, 5, 4]
    return order


def per_device(embeddings, assign, cluster_slot):
    row_count, width = embeddings.shape
    owner_count = lax.axis_size("docs")
    per_owner = cluster_slot.shape[0] // owner_count
    capacity = row_count // owner_count + row_count // (4 * owner_count)
    padded = round_up(capacity, LANES)
    blocks = padded // LANES
    me = lax.axis_index("docs").astype(jnp.int32).reshape(1)
    turns_of = turns(owner_count)

    slots, starts = make_plan(
        assign.reshape(-1, LANES), cluster_slot.reshape(-1, LANES), owner_count, per_owner, row_count - capacity
    )

    sent, chunks = [], []
    for place, turn in enumerate(turns_of):
        piece = unit_piece(starts, me, embeddings, turn, 0, capacity, sent[-1:] if place > 1 else [])
        if place == 2:
            wire_labels = sent_labels(starts, slots, owner_count, per_owner, capacity, sent[1])
            got_labels = lax.all_to_all(wire_labels, "docs", split_axis=0, concat_axis=0, tiled=True)
            piece = hold_until(piece, [got_labels])
        sent.append(piece)
        if turn:
            piece = lax.ppermute(piece, "docs", [(i, (i + turn) % owner_count) for i in range(owner_count)])
        chunks.append(piece)
    rows, columns, group_tally = arrived_labels(me, got_labels, turns_of, blocks, width)
    sum_labels = summed_labels(starts, slots, owner_count, per_owner, capacity)
    partial_sums = slot_sums(starts, sum_labels, embeddings, per_owner, capacity, sent[1:8])
    partial_sums = hold_until(partial_sums, chunks[1:3])
    group_share = lax.psum_scatter(partial_sums, "grp", scatter_dimension=1, tiled=True)
    group_share = hold_until(group_share, chunks[3:6])
    share = lax.psum_scatter(group_share, "docs", scatter_dimension=0, tiled=True)[0]

    bests = [jnp.full((owner_count * blocks, LANES), -2.0, jnp.float32)]
    flat = None
    for place in range(owner_count - 1):
        best, flat = gram_step(rows, columns, bests[-1], flat, chunks[place], place * padded)
        bests.append(best)
    packed = pack_share(share, group_tally, bests[-3:-2])
    centroids, centroid_unit = make_centroids(lax.all_gather(packed, "grp"), per_owner)
    results = gram_step(
        rows, columns, bests[-1], flat, chunks[-1], (owner_count - 1) * padded, final=(centroid_unit, me, turns_of)
    )
    back = lax.all_to_all(results, "docs", split_axis=0, concat_axis=0, tiled=True)
    near, cosine = place_rows(starts, slots, back, per_owner)
    return (centroids, near.reshape(-1), cosine.reshape(-1))


def solution(mesh):
    placed = (P(("grp", "docs"), None), P(("grp", "docs")), P())
    return jax.shard_map(
        per_device,
        mesh=mesh,
        in_specs=placed,
        out_specs=(P("docs", None), P(("grp", "docs")), P(("grp", "docs"))),
        check_vma=False,
    )
```

```python
import functools

import jax
import jax.numpy as jnp
from jax import lax
from jax.experimental import pallas as pl
from jax.experimental.pallas import tpu as pltpu
from jax.sharding import PartitionSpec as P

epsilon = 1e-06
LANES = 128
SUBLANES = 8
MIB = 1024 * 1024
TILE = 512
in_vmem = pl.BlockSpec(memory_space=pltpu.VMEM)
in_smem = pl.BlockSpec(memory_space=pltpu.SMEM)
anywhere = pl.BlockSpec(memory_space=pl.ANY)
brief = pl.CostEstimate(flops=1000, bytes_accessed=1000, transcendentals=0)


def round_up(value, step):
    return -(-value // step) * step


def params(mib=44):
    return pltpu.CompilerParams(vmem_limit_bytes=mib * MIB)


def look_up(table_ref, index):
    lane = jnp.bitwise_and(index, LANES - 1)
    row = jnp.right_shift(index, 7)
    found = jnp.zeros(index.shape, jnp.int32)
    for part in range(table_ref.shape[0]):
        entries = jnp.broadcast_to(table_ref[part : part + 1, :], index.shape)
        found = jnp.where(row == part, jnp.take_along_axis(entries, lane, axis=1), found)
    return found


def rows_below(slots, bound):
    return jnp.sum((slots < bound).astype(jnp.float32)).astype(jnp.int32)


def plan_kernel(per_owner, limit, assign_ref, table_ref, slot_ref, start_ref):
    slots = look_up(table_ref, assign_ref[...])
    slot_ref[...] = slots
    for owner in range(start_ref.shape[0]):
        start_ref[owner] = jnp.minimum(rows_below(slots, owner * per_owner), limit)


def make_plan(assign_rows, table, owner_count, per_owner, limit):
    return pl.pallas_call(
        functools.partial(plan_kernel, per_owner, limit),
        out_shape=(
            jax.ShapeDtypeStruct(assign_rows.shape, jnp.int32),
            jax.ShapeDtypeStruct((owner_count,), jnp.int32),
        ),
        in_specs=[in_vmem, in_vmem],
        out_specs=(in_vmem, in_smem),
        compiler_params=params(8),
        name="plan",
    )(assign_rows, table)


def unit_kernel(steps, offset, turn, start_ref, me_ref, rows_ref, *refs):
    unit_ref, held, sem = refs[-3:]
    part = unit_ref.shape[0] // steps
    window = part + SUBLANES
    start = start_ref[lax.rem(me_ref[0] + turn, start_ref.shape[0])] + offset

    def first(step):
        return aligned_start(start + step * part, rows_ref.shape[0], window)

    copies = [
        pltpu.make_async_copy(rows_ref.at[pl.ds(first(step), window), :], held.at[step], sem.at[step])
        for step in range(steps)
    ]
    for copy in copies:
        copy.start()
    for step in range(steps):
        copies[step].wait()
        shift = start + step * part - first(step)
        groups = held[step].reshape(window // SUBLANES, SUBLANES, -1)
        turned = pltpu.roll(groups, SUBLANES - shift, 1)
        line = lax.broadcasted_iota(jnp.int32, (part // SUBLANES, SUBLANES, groups.shape[2]), 1)
        values = jnp.where(line < SUBLANES - shift, turned[:-1], turned[1:]).reshape(part, -1)
        scale = lax.rsqrt(jnp.sum(values * values, -1, keepdims=True) + epsilon)
        unit_ref[step * part : (step + 1) * part, :] = (values * scale).astype(jnp.bfloat16)


def unit_piece(starts, me, embeddings, turn, offset, rows, after):
    width = embeddings.shape[1]
    steps = rows // LANES if rows % LANES == 0 else 1
    return pl.pallas_call(
        functools.partial(unit_kernel, steps, offset, turn),
        out_shape=jax.ShapeDtypeStruct((rows, width), jnp.bfloat16),
        in_specs=[in_smem, in_smem, anywhere] + [anywhere] * len(after),
        out_specs=in_vmem,
        scratch_shapes=[
            pltpu.VMEM((steps, rows // steps + SUBLANES, width), jnp.float32),
            pltpu.SemaphoreType.DMA((steps,)),
        ],
        compiler_params=params(),
        cost_estimate=brief,
        name="unit",
    )(starts, me, embeddings, *after)


def hold_until(values, arrived):
    def nothing(*refs):
        pass

    return pl.pallas_call(
        nothing,
        out_shape=jax.ShapeDtypeStruct(values.shape, values.dtype),
        in_specs=[anywhere] * (1 + len(arrived)),
        out_specs=anywhere,
        input_output_aliases={0: 0},
        compiler_params=params(8),
        cost_estimate=brief,
        name="hold",
    )(values, *arrived)


def aligned_start(start, row_count, window):
    begin = jnp.minimum(jnp.left_shift(jnp.right_shift(start, 3), 3), row_count - window)
    return pl.multiple_of(begin, SUBLANES)


def flat_window(held, start, rows):
    span = round_up(rows + 1, SUBLANES)
    shift = jnp.bitwise_and(start, LANES - 1)
    block = held[pl.ds(jnp.right_shift(start, 7), span), :]
    turned = pltpu.roll(block, jnp.bitwise_and(LANES - shift, LANES - 1), 1)
    following = pltpu.roll(turned, span - 1, 0)
    lane = lax.broadcasted_iota(jnp.int32, block.shape, 1)
    return jnp.where(lane < LANES - shift, turned, following)


def window_labels(held, slots, owner, start, per_owner, capacity, blocks):
    low = owner * per_owner
    mine = (slots >= low) & (slots < low + per_owner)
    held[: slots.shape[0], :] = jnp.where(mine, slots - low, -1)
    labels = flat_window(held, start, blocks)
    place = lax.broadcasted_iota(jnp.int32, labels.shape, 0) * LANES + lax.broadcasted_iota(
        jnp.int32, labels.shape, 1
    )
    return jnp.where(place < capacity, labels, -1)


def summed_kernel(per_owner, capacity, start_ref, slot_ref, sum_ref, held):
    owner_count = sum_ref.shape[0]
    held[...] = jnp.full(held.shape, -1, jnp.int32)
    slots = slot_ref[...]
    window = capacity + SUBLANES
    wide = sum_ref.shape[1] // LANES
    for owner in range(owner_count):
        aligned = aligned_start(start_ref[owner], slots.size, window)
        labels = window_labels(held, slots, owner, aligned, per_owner, window, wide)
        for block in range(wide):
            sum_ref[owner : owner + 1, block * LANES : (block + 1) * LANES] = labels[block : block + 1, :]


def summed_labels(starts, slots, owner_count, per_owner, capacity):
    return pl.pallas_call(
        functools.partial(summed_kernel, per_owner, capacity),
        out_shape=jax.ShapeDtypeStruct((owner_count, round_up(capacity + SUBLANES, LANES)), jnp.int32),
        in_specs=[in_smem, in_vmem],
        out_specs=in_vmem,
        scratch_shapes=[pltpu.VMEM((slots.shape[0] + 2 * SUBLANES, LANES), jnp.int32)],
        compiler_params=params(8),
        name="summed",
    )(starts, slots)


def sent_kernel(per_owner, capacity, start_ref, slot_ref, after_ref, sent_ref, held):
    owner_count, span, _ = sent_ref.shape
    held[...] = jnp.full(held.shape, -1, jnp.int32)
    slots = slot_ref[...]
    for owner in range(owner_count):
        labels = window_labels(held, slots, owner, start_ref[owner], per_owner, capacity, span - 1)
        sent_ref[owner] = labels[:span, :]


def sent_labels(starts, slots, owner_count, per_owner, capacity, after):
    span = round_up(-(-capacity // LANES) + 1, SUBLANES)
    return pl.pallas_call(
        functools.partial(sent_kernel, per_owner, capacity),
        out_shape=jax.ShapeDtypeStruct((owner_count, span, LANES), jnp.int32),
        in_specs=[in_smem, in_vmem, anywhere],
        out_specs=in_vmem,
        scratch_shapes=[pltpu.VMEM((slots.shape[0] + 2 * SUBLANES, LANES), jnp.int32)],
        compiler_params=params(8),
        name="sent",
    )(starts, slots, after)


def arrived_kernel(blocks, turns_of, me_ref, got_ref, row_ref, column_ref, tally_ref):
    tally = jnp.zeros((LANES, LANES), jnp.float32)
    cluster = lax.broadcasted_iota(jnp.int32, tally.shape, 0)
    for place, turn in enumerate(turns_of):
        source = lax.rem(me_ref[0] + len(turns_of) - turn, len(turns_of))
        for block in range(blocks):
            line = place * blocks + block
            spread = jnp.broadcast_to(got_ref[source, block : block + 1, :], tally.shape)
            row_ref[line : line + 1, :] = spread[:1, :]
            column_ref[line * LANES : (line + 1) * LANES, :] = spread.T
            tally += (spread == cluster).astype(jnp.float32)
    total = jnp.broadcast_to(jnp.sum(tally, 1, keepdims=True), tally.shape)
    tally_ref[...] = jnp.zeros(tally_ref.shape, jnp.float32)
    tally_ref[:, :LANES] = total.T[:SUBLANES, :]


def arrived_labels(me, got, turns_of, blocks, width):
    lines = len(turns_of) * blocks
    return pl.pallas_call(
        functools.partial(arrived_kernel, blocks, turns_of),
        out_shape=(
            jax.ShapeDtypeStruct((lines, LANES), jnp.int32),
            jax.ShapeDtypeStruct((lines * LANES, LANES), jnp.int32),
            jax.ShapeDtypeStruct((SUBLANES, width), jnp.float32),
        ),
        in_specs=[in_smem, in_vmem],
        out_specs=(in_vmem, in_vmem, in_vmem),
        compiler_params=params(8),
        name="arrived",
    )(me, got)


def sum_kernel(start_ref, label_ref, rows_ref, *refs):
    sum_ref, held, sem = refs[-3:]
    owner_count, per_owner, _ = sum_ref.shape
    window = held.shape[1]

    def copy(owner, slot):
        first = aligned_start(start_ref[owner], rows_ref.shape[0], window)
        return pltpu.make_async_copy(rows_ref.at[pl.ds(first, window), :], held.at[slot], sem.at[slot])

    copy(0, 0).start()

    def body(owner, carry):
        slot = lax.rem(owner, 2)

        @pl.when(owner + 1 < owner_count)
        def _():
            copy(owner + 1, 1 - slot).start()

        copy(owner, slot).wait()
        labels = label_ref[pl.ds(owner, 1), :][:, :window]
        cluster = lax.broadcasted_iota(jnp.int32, (per_owner, window), 0)
        member = (labels == cluster).astype(jnp.float32).astype(jnp.bfloat16)
        values = held[slot]
        high = values.astype(jnp.bfloat16)
        rest = values - high.astype(jnp.float32)
        middle = rest.astype(jnp.bfloat16)
        low = (rest - middle.astype(jnp.float32)).astype(jnp.bfloat16)
        total = jnp.dot(member, high, preferred_element_type=jnp.float32)
        total += jnp.dot(member, middle, preferred_element_type=jnp.float32)
        total += jnp.dot(member, low, preferred_element_type=jnp.float32)
        sum_ref[pl.ds(owner, 1)] = total[None]
        return carry

    lax.fori_loop(0, owner_count, body, 0)


def slot_sums(starts, labels, embeddings, per_owner, capacity, after):
    owner_count = labels.shape[0]
    width = embeddings.shape[1]
    return pl.pallas_call(
        sum_kernel,
        out_shape=jax.ShapeDtypeStruct((owner_count, per_owner, width), jnp.float32),
        in_specs=[in_smem, in_vmem, anywhere] + [anywhere] * len(after),
        out_specs=in_vmem,
        scratch_shapes=[
            pltpu.VMEM((2, capacity + SUBLANES, width), jnp.float32),
            pltpu.SemaphoreType.DMA((2,)),
        ],
        compiler_params=params(),
        cost_estimate=pl.CostEstimate(
            flops=6 * owner_count * per_owner * capacity * width,
            bytes_accessed=4 * embeddings.size,
            transcendentals=0,
        ),
        name="sums",
    )(starts, labels, embeddings, *after)


def gram_kernel(begin, rows, wide, after_count, turns_of, *refs):
    chunk_ref, row_ref, column_ref, best_ref, *refs = refs
    flat_ref = centroid_ref = result_ref = None
    if begin:
        flat_ref, *refs = refs
    refs = refs[after_count:]
    if turns_of:
        centroid_ref, me_ref, result_ref, *refs, out_ref, cosine_ref = refs
    else:
        out_ref, flat_ref, *refs = refs
    mine, turned, labels, tiles, even, odd, best, sem, tile_sem = refs
    first = begin // LANES
    size = tiles.shape[2]
    count = round_up(-(-begin // size), 2)

    def line_of(tile):
        return jnp.minimum(tile * (size // LANES), first - size // LANES)

    def fetch(tile):
        start = pl.multiple_of(line_of(tile) * LANES, LANES)
        slot = lax.rem(tile, 4)
        return pltpu.make_async_copy(flat_ref.at[:, pl.ds(start, size)], tiles.at[slot], tile_sem.at[slot])

    chunk_copy = pltpu.make_async_copy(chunk_ref, mine.at[pl.ds(0, rows), :], sem.at[0])
    label_copy = pltpu.make_async_copy(column_ref.at[pl.ds(begin, wide), :], labels, sem.at[1])
    chunk_copy.start()
    label_copy.start()
    for tile in range(min(count, 3)):
        fetch(jnp.int32(tile)).start()
    if rows < wide:
        mine[rows:wide, :] = jnp.zeros((wide - rows, mine.shape[1]), mine.dtype)
    if turns_of:
        mine[wide:, :] = centroid_ref[...]
        cosine_ref[...] = jnp.zeros(cosine_ref.shape, jnp.float32)
    out_ref[...] = best_ref[...]
    best[...] = jnp.full(best.shape, -2.0, jnp.float32)
    chunk_copy.wait()
    label_copy.wait()
    turned[...] = mine[:wide, :].T
    if not turns_of:
        flat_copy = pltpu.make_async_copy(turned, flat_ref.at[:, pl.ds(begin, wide)], sem.at[2])
        flat_copy.start()

    def products(right):
        return jnp.dot(mine[...], right, preferred_element_type=jnp.float32)

    halves = 2 if size % (4 * LANES) == 0 else 1

    def multiply(held, slot, half):
        here = slice(half * (size // halves), (half + 1) * (size // halves))
        held[:, here] = products(tiles[slot, :, here])

    def cosines(values, line):
        cluster = lax.broadcasted_iota(jnp.int32, values.shape, 0)
        own = jnp.where(row_ref[pl.ds(line, 1), :] == cluster, values, 0.0)
        cosine_ref[pl.ds(line, 1), :] = jnp.sum(own, 0, keepdims=True)

    def reduce_tile(held, tile, half):
        parts = range(half * (size // halves) // LANES, (half + 1) * (size // halves) // LANES)
        lines = {part: line_of(tile) + part for part in parts}
        tops = {part: jnp.full((SUBLANES, LANES), -2.0, jnp.float32) for part in parts}
        against = {
            part: jnp.broadcast_to(row_ref[pl.ds(lines[part], 1), :], (LANES, LANES)) for part in parts
        }
        for begin_row in range(0, wide, LANES):
            span = slice(begin_row, begin_row + LANES)
            own = labels[span, :]
            fold = best[span, :]
            for part in parts:
                near = jnp.where(own == against[part], held[span, part * LANES : (part + 1) * LANES], -2.0)
                fold = jnp.maximum(fold, near)
                tops[part] = jnp.maximum(tops[part], jnp.max(near.reshape(-1, SUBLANES, LANES), 0))
            best[span, :] = fold
        for part in parts:
            out_ref[pl.ds(lines[part], 1), :] = jnp.maximum(
                out_ref[pl.ds(lines[part], 1), :], jnp.max(tops[part], 0, keepdims=True)
            )
            if turns_of:
                cosines(held[wide:, part * LANES : (part + 1) * LANES], lines[part])

    if begin:
        fetch(jnp.int32(0)).wait()
        for half in range(halves):
            multiply(even, 0, half)

        def body(pair, carry):
            tile = pair * 2
            fetch(tile + 1).wait()
            fetch(tile + 3).start()
            for half in range(halves):
                multiply(odd, lax.rem(tile + 1, 4), half)
                reduce_tile(even, tile, half)
            fetch(tile + 2).wait()

            @pl.when(tile + 4 < count)
            def _():
                fetch(tile + 4).start()

            for half in range(halves):
                multiply(even, lax.rem(tile + 2, 4), half)
                reduce_tile(odd, tile + 1, half)
            return carry

        lax.fori_loop(0, count // 2 - 1, body, 0)
        fetch(jnp.int32(count - 1)).wait()
        for half in range(halves):
            multiply(odd, (count - 1) % 4, half)
            reduce_tile(even, jnp.int32(count - 2), half)
        for half in range(halves):
            reduce_tile(odd, jnp.int32(count - 1), half)
    own = products(turned[...])
    row = lax.broadcasted_iota(jnp.int32, (wide, LANES), 0)
    column = lax.broadcasted_iota(jnp.int32, (wide, LANES), 1)
    for block in range(wide // LANES):
        line = first + block
        here = slice(block * LANES, (block + 1) * LANES)
        allowed = (labels[...] == row_ref[line : line + 1, :]) & (row != column + block * LANES)
        near = jnp.max(jnp.where(allowed, own[:wide, here], -2.0), 0, keepdims=True)
        other = jnp.max(best[here, :].T, 0, keepdims=True)
        out_ref[line : line + 1, :] = jnp.maximum(near, other)
        if turns_of:
            cosines(own[wide:, here], line)
    if turns_of:
        blocks = row_ref.shape[0] // len(turns_of)
        half = result_ref.shape[1] // 2
        result_ref[...] = jnp.zeros(result_ref.shape, jnp.float32)
        for place, turn in enumerate(turns_of):
            source = lax.rem(me_ref[0] + len(turns_of) - turn, len(turns_of))
            lines = slice(place * blocks, (place + 1) * blocks)
            result_ref[source, :blocks, :] = out_ref[lines, :]
            result_ref[source, half : half + blocks, :] = cosine_ref[lines, :]
    else:
        flat_copy.wait()


def gram_step(rows, columns, best, flat, chunk, begin, after=(), final=None):
    length, width = chunk.shape
    wide = round_up(length, LANES)
    tall = wide
    size = min(TILE, begin) if begin else LANES
    flat_shape = jax.ShapeDtypeStruct((width, columns.shape[0]), jnp.bfloat16)
    inputs = [chunk, rows, columns, best]
    in_specs = [anywhere, in_vmem, anywhere, in_vmem]
    aliases = {}
    if begin:
        if not final:
            aliases = {len(inputs): 1}
        inputs.append(flat)
        in_specs.append(anywhere)
    inputs += after
    in_specs += [anywhere] * len(after)
    out_shape = (jax.ShapeDtypeStruct(best.shape, jnp.float32), flat_shape)
    out_specs = (in_vmem, anywhere)
    turns_of = ()
    extra = []
    if final:
        centroid_unit, me, turns_of = final
        tall += centroid_unit.shape[0]
        inputs += [centroid_unit, me]
        in_specs += [in_vmem, in_smem]
        half = round_up(rows.shape[0] // len(turns_of) + 1, SUBLANES)
        out_shape = jax.ShapeDtypeStruct((len(turns_of), 2 * half, LANES), jnp.float32)
        out_specs = in_vmem
        extra = [pltpu.VMEM(best.shape, jnp.float32)] * 2
    return pl.pallas_call(
        functools.partial(gram_kernel, begin, length, wide, len(after), turns_of),
        out_shape=out_shape,
        in_specs=in_specs,
        out_specs=out_specs,
        scratch_shapes=[
            pltpu.VMEM((tall, width), jnp.bfloat16),
            pltpu.VMEM((width, wide), jnp.bfloat16),
            pltpu.VMEM((wide, LANES), jnp.int32),
            pltpu.VMEM((4, width, size), jnp.bfloat16),
            pltpu.VMEM((tall, size), jnp.float32),
            pltpu.VMEM((tall, size), jnp.float32),
            pltpu.VMEM((wide, LANES), jnp.float32),
            pltpu.SemaphoreType.DMA((3,)),
            pltpu.SemaphoreType.DMA((4,)),
        ]
        + extra,
        input_output_aliases=aliases,
        compiler_params=params(),
        cost_estimate=brief,
        name="gram",
    )(*inputs)


def pack_kernel(share_ref, tally_ref, *refs):
    packed_ref = refs[-1]
    packed_ref[: share_ref.shape[0], :] = share_ref[...]
    packed_ref[share_ref.shape[0] :, :] = tally_ref[...]


def pack_share(share, tally, after):
    length = share.shape[0] + tally.shape[0]
    return pl.pallas_call(
        pack_kernel,
        out_shape=jax.ShapeDtypeStruct((length, share.shape[1]), jnp.float32),
        in_specs=[in_vmem, in_vmem] + [anywhere] * len(after),
        out_specs=in_vmem,
        compiler_params=params(8),
        name="pack",
    )(share, tally, *after)


def centroid_kernel(gathered_ref, centroid_ref, unit_ref):
    groups, length, width = gathered_ref.shape
    share = length - SUBLANES
    per_owner = centroid_ref.shape[0]
    tally = jnp.sum(gathered_ref[:, share, :LANES], 0, keepdims=True)
    column = jnp.broadcast_to(tally, (LANES, LANES)).T[:per_owner, :]
    sums = jnp.concatenate([gathered_ref[group, :share, :] for group in range(groups)], 0)
    centroids = sums / jnp.concatenate([column] * (width // LANES), 1)
    centroid_ref[...] = centroids
    scale = lax.rsqrt(jnp.sum(centroids * centroids, -1, keepdims=True) + epsilon)
    unit_ref[...] = (centroids * scale).astype(jnp.bfloat16)


def make_centroids(gathered, per_owner):
    shape = (per_owner, gathered.shape[2])
    return pl.pallas_call(
        centroid_kernel,
        out_shape=(
            jax.ShapeDtypeStruct(shape, jnp.float32),
            jax.ShapeDtypeStruct(shape, jnp.bfloat16),
        ),
        in_specs=[in_vmem],
        out_specs=(in_vmem, in_vmem),
        compiler_params=params(8),
        name="centroids",
    )(gathered)


def place_kernel(per_owner, start_ref, slot_ref, back_ref, near_ref, cosine_ref, held, result):
    owner_count, double, _ = back_ref.shape
    span = double // 2
    rows = slot_ref.shape[0]
    held[...] = jnp.full(held.shape, -1, jnp.int32)
    held[:rows, :] = slot_ref[...]
    result[...] = jnp.zeros(result.shape, jnp.float32)
    lane = lax.broadcasted_iota(jnp.int32, (span, LANES), 1)
    for owner in range(owner_count):
        start = start_ref[owner]
        first = pl.ds(jnp.right_shift(start, 7), span)
        shift = jnp.bitwise_and(start, LANES - 1)
        slots = held[first, :]
        mine = (slots >= owner * per_owner) & (slots < (owner + 1) * per_owner)
        for kind in range(2):
            turned = pltpu.roll(back_ref[owner, kind * span : (kind + 1) * span, :], shift, 1)
            earlier = pltpu.roll(turned, 1, 0)
            moved = jnp.where(lane >= shift, turned, earlier)
            result[kind, first, :] = jnp.where(mine, moved, result[kind, first, :])
    near_ref[...] = result[0, :rows, :]
    cosine_ref[...] = result[1, :rows, :]


def place_rows(starts, slots, back, per_owner):
    span = back.shape[1] // 2
    rows = slots.shape[0]
    return pl.pallas_call(
        functools.partial(place_kernel, per_owner),
        out_shape=(jax.ShapeDtypeStruct(slots.shape, jnp.float32),) * 2,
        in_specs=[in_smem, in_vmem, in_vmem],
        out_specs=(in_vmem, in_vmem),
        scratch_shapes=[
            pltpu.VMEM((rows + span, LANES), jnp.int32),
            pltpu.VMEM((2, rows + span, LANES), jnp.float32),
        ],
        compiler_params=params(8),
        name="place",
    )(starts, slots, back)


def turns(count):
    order = sorted(range(count), key=lambda turn: (min(turn, count - turn), turn))
    if count == 8:
        order = [0, 1, 2, 3, 7, 6, 5, 4]
    return order


def per_device(embeddings, assign, cluster_slot):
    row_count, width = embeddings.shape
    owner_count = lax.axis_size("docs")
    per_owner = cluster_slot.shape[0] // owner_count
    capacity = row_count // owner_count + row_count // (4 * owner_count)
    padded = round_up(capacity, LANES)
    blocks = padded // LANES
    me = lax.axis_index("docs").astype(jnp.int32).reshape(1)
    turns_of = turns(owner_count)

    slots, starts = make_plan(
        assign.reshape(-1, LANES), cluster_slot.reshape(-1, LANES), owner_count, per_owner, row_count - capacity
    )

    sent, chunks = [], []
    for place, turn in enumerate(turns_of):
        piece = unit_piece(starts, me, embeddings, turn, 0, capacity, sent[-1:] if place > 1 else [])
        if place == 2:
            wire_labels = sent_labels(starts, slots, owner_count, per_owner, capacity, sent[1])
            got_labels = lax.all_to_all(wire_labels, "docs", split_axis=0, concat_axis=0, tiled=True)
            piece = hold_until(piece, [got_labels])
        sent.append(piece)
        if turn:
            piece = lax.ppermute(piece, "docs", [(i, (i + turn) % owner_count) for i in range(owner_count)])
        chunks.append(piece)
    rows, columns, group_tally = arrived_labels(me, got_labels, turns_of, blocks, width)
    sum_labels = summed_labels(starts, slots, owner_count, per_owner, capacity)
    partial_sums = slot_sums(starts, sum_labels, embeddings, per_owner, capacity, sent[1:8])
    partial_sums = hold_until(partial_sums, chunks[1:3])
    group_share = lax.psum_scatter(partial_sums, "grp", scatter_dimension=1, tiled=True)
    group_share = hold_until(group_share, chunks[3:4])
    share = lax.psum_scatter(group_share, "docs", scatter_dimension=0, tiled=True)[0]

    bests = [jnp.full((owner_count * blocks, LANES), -2.0, jnp.float32)]
    flat = None
    for place in range(owner_count - 1):
        best, flat = gram_step(rows, columns, bests[-1], flat, chunks[place], place * padded)
        bests.append(best)
    packed = pack_share(share, group_tally, bests[-3:-2])
    centroids, centroid_unit = make_centroids(lax.all_gather(packed, "grp"), per_owner)
    results = gram_step(
        rows, columns, bests[-1], flat, chunks[-1], (owner_count - 1) * padded, final=(centroid_unit, me, turns_of)
    )
    back = lax.all_to_all(results, "docs", split_axis=0, concat_axis=0, tiled=True)
    near, cosine = place_rows(starts, slots, back, per_owner)
    return (centroids, near.reshape(-1), cosine.reshape(-1))


def solution(mesh):
    placed = (P(("grp", "docs"), None), P(("grp", "docs")), P())
    return jax.shard_map(
        per_device,
        mesh=mesh,
        in_specs=placed,
        out_specs=(P("docs", None), P(("grp", "docs")), P(("grp", "docs"))),
        check_vma=False,
    )
```

```python
import functools

import jax
import jax.numpy as jnp
from jax import lax
from jax.experimental import pallas as pl
from jax.experimental.pallas import tpu as pltpu
from jax.sharding import PartitionSpec as P

epsilon = 1e-06
LANES = 128
SUBLANES = 8
MIB = 1024 * 1024
TILE = 512
in_vmem = pl.BlockSpec(memory_space=pltpu.VMEM)
in_smem = pl.BlockSpec(memory_space=pltpu.SMEM)
anywhere = pl.BlockSpec(memory_space=pl.ANY)
brief = pl.CostEstimate(flops=1000, bytes_accessed=1000, transcendentals=0)


def round_up(value, step):
    return -(-value // step) * step


def params(mib=44):
    return pltpu.CompilerParams(vmem_limit_bytes=mib * MIB)


def look_up(table_ref, index):
    lane = jnp.bitwise_and(index, LANES - 1)
    row = jnp.right_shift(index, 7)
    found = jnp.zeros(index.shape, jnp.int32)
    for part in range(table_ref.shape[0]):
        entries = jnp.broadcast_to(table_ref[part : part + 1, :], index.shape)
        found = jnp.where(row == part, jnp.take_along_axis(entries, lane, axis=1), found)
    return found


def rows_below(slots, bound):
    return jnp.sum((slots < bound).astype(jnp.float32)).astype(jnp.int32)


def plan_kernel(per_owner, limit, assign_ref, table_ref, slot_ref, start_ref):
    slots = look_up(table_ref, assign_ref[...])
    slot_ref[...] = slots
    for owner in range(start_ref.shape[0]):
        start_ref[owner] = jnp.minimum(rows_below(slots, owner * per_owner), limit)


def make_plan(assign_rows, table, owner_count, per_owner, limit):
    return pl.pallas_call(
        functools.partial(plan_kernel, per_owner, limit),
        out_shape=(
            jax.ShapeDtypeStruct(assign_rows.shape, jnp.int32),
            jax.ShapeDtypeStruct((owner_count,), jnp.int32),
        ),
        in_specs=[in_vmem, in_vmem],
        out_specs=(in_vmem, in_smem),
        compiler_params=params(8),
        name="plan",
    )(assign_rows, table)


def unit_kernel(steps, offset, turn, start_ref, me_ref, rows_ref, *refs):
    unit_ref, held, sem = refs[-3:]
    part = unit_ref.shape[0] // steps
    window = part + SUBLANES
    start = start_ref[lax.rem(me_ref[0] + turn, start_ref.shape[0])] + offset

    def first(step):
        return aligned_start(start + step * part, rows_ref.shape[0], window)

    copies = [
        pltpu.make_async_copy(rows_ref.at[pl.ds(first(step), window), :], held.at[step], sem.at[step])
        for step in range(steps)
    ]
    for copy in copies:
        copy.start()
    for step in range(steps):
        copies[step].wait()
        shift = start + step * part - first(step)
        groups = held[step].reshape(window // SUBLANES, SUBLANES, -1)
        turned = pltpu.roll(groups, SUBLANES - shift, 1)
        line = lax.broadcasted_iota(jnp.int32, (part // SUBLANES, SUBLANES, groups.shape[2]), 1)
        values = jnp.where(line < SUBLANES - shift, turned[:-1], turned[1:]).reshape(part, -1)
        scale = lax.rsqrt(jnp.sum(values * values, -1, keepdims=True) + epsilon)
        unit_ref[step * part : (step + 1) * part, :] = (values * scale).astype(jnp.bfloat16)


def unit_piece(starts, me, embeddings, turn, offset, rows, after):
    width = embeddings.shape[1]
    steps = rows // LANES if rows % LANES == 0 else 1
    return pl.pallas_call(
        functools.partial(unit_kernel, steps, offset, turn),
        out_shape=jax.ShapeDtypeStruct((rows, width), jnp.bfloat16),
        in_specs=[in_smem, in_smem, anywhere] + [anywhere] * len(after),
        out_specs=in_vmem,
        scratch_shapes=[
            pltpu.VMEM((steps, rows // steps + SUBLANES, width), jnp.float32),
            pltpu.SemaphoreType.DMA((steps,)),
        ],
        compiler_params=params(),
        cost_estimate=brief,
        name="unit",
    )(starts, me, embeddings, *after)


def hold_until(values, arrived):
    def nothing(*refs):
        pass

    return pl.pallas_call(
        nothing,
        out_shape=jax.ShapeDtypeStruct(values.shape, values.dtype),
        in_specs=[anywhere] * (1 + len(arrived)),
        out_specs=anywhere,
        input_output_aliases={0: 0},
        compiler_params=params(8),
        cost_estimate=brief,
        name="hold",
    )(values, *arrived)


def aligned_start(start, row_count, window):
    begin = jnp.minimum(jnp.left_shift(jnp.right_shift(start, 3), 3), row_count - window)
    return pl.multiple_of(begin, SUBLANES)


def flat_window(held, start, rows):
    span = round_up(rows + 1, SUBLANES)
    shift = jnp.bitwise_and(start, LANES - 1)
    block = held[pl.ds(jnp.right_shift(start, 7), span), :]
    turned = pltpu.roll(block, jnp.bitwise_and(LANES - shift, LANES - 1), 1)
    following = pltpu.roll(turned, span - 1, 0)
    lane = lax.broadcasted_iota(jnp.int32, block.shape, 1)
    return jnp.where(lane < LANES - shift, turned, following)


def window_labels(held, slots, owner, start, per_owner, capacity, blocks):
    low = owner * per_owner
    mine = (slots >= low) & (slots < low + per_owner)
    held[: slots.shape[0], :] = jnp.where(mine, slots - low, -1)
    labels = flat_window(held, start, blocks)
    place = lax.broadcasted_iota(jnp.int32, labels.shape, 0) * LANES + lax.broadcasted_iota(
        jnp.int32, labels.shape, 1
    )
    return jnp.where(place < capacity, labels, -1)


def summed_kernel(per_owner, capacity, start_ref, slot_ref, sum_ref, held):
    owner_count = sum_ref.shape[0]
    held[...] = jnp.full(held.shape, -1, jnp.int32)
    slots = slot_ref[...]
    window = capacity + SUBLANES
    wide = sum_ref.shape[1] // LANES
    for owner in range(owner_count):
        aligned = aligned_start(start_ref[owner], slots.size, window)
        labels = window_labels(held, slots, owner, aligned, per_owner, window, wide)
        for block in range(wide):
            sum_ref[owner : owner + 1, block * LANES : (block + 1) * LANES] = labels[block : block + 1, :]


def summed_labels(starts, slots, owner_count, per_owner, capacity):
    return pl.pallas_call(
        functools.partial(summed_kernel, per_owner, capacity),
        out_shape=jax.ShapeDtypeStruct((owner_count, round_up(capacity + SUBLANES, LANES)), jnp.int32),
        in_specs=[in_smem, in_vmem],
        out_specs=in_vmem,
        scratch_shapes=[pltpu.VMEM((slots.shape[0] + 2 * SUBLANES, LANES), jnp.int32)],
        compiler_params=params(8),
        name="summed",
    )(starts, slots)


def sent_kernel(per_owner, capacity, start_ref, slot_ref, after_ref, sent_ref, held):
    owner_count, span, _ = sent_ref.shape
    held[...] = jnp.full(held.shape, -1, jnp.int32)
    slots = slot_ref[...]
    for owner in range(owner_count):
        labels = window_labels(held, slots, owner, start_ref[owner], per_owner, capacity, span - 1)
        sent_ref[owner] = labels[:span, :]


def sent_labels(starts, slots, owner_count, per_owner, capacity, after):
    span = round_up(-(-capacity // LANES) + 1, SUBLANES)
    return pl.pallas_call(
        functools.partial(sent_kernel, per_owner, capacity),
        out_shape=jax.ShapeDtypeStruct((owner_count, span, LANES), jnp.int32),
        in_specs=[in_smem, in_vmem, anywhere],
        out_specs=in_vmem,
        scratch_shapes=[pltpu.VMEM((slots.shape[0] + 2 * SUBLANES, LANES), jnp.int32)],
        compiler_params=params(8),
        name="sent",
    )(starts, slots, after)


def arrived_kernel(blocks, turns_of, me_ref, got_ref, row_ref, column_ref, tally_ref):
    tally = jnp.zeros((LANES, LANES), jnp.float32)
    cluster = lax.broadcasted_iota(jnp.int32, tally.shape, 0)
    for place, turn in enumerate(turns_of):
        source = lax.rem(me_ref[0] + len(turns_of) - turn, len(turns_of))
        for block in range(blocks):
            line = place * blocks + block
            spread = jnp.broadcast_to(got_ref[source, block : block + 1, :], tally.shape)
            row_ref[line : line + 1, :] = spread[:1, :]
            column_ref[line * LANES : (line + 1) * LANES, :] = spread.T
            tally += (spread == cluster).astype(jnp.float32)
    total = jnp.broadcast_to(jnp.sum(tally, 1, keepdims=True), tally.shape)
    tally_ref[...] = jnp.zeros(tally_ref.shape, jnp.float32)
    tally_ref[:, :LANES] = total.T[:SUBLANES, :]


def arrived_labels(me, got, turns_of, blocks, width):
    lines = len(turns_of) * blocks
    return pl.pallas_call(
        functools.partial(arrived_kernel, blocks, turns_of),
        out_shape=(
            jax.ShapeDtypeStruct((lines, LANES), jnp.int32),
            jax.ShapeDtypeStruct((lines * LANES, LANES), jnp.int32),
            jax.ShapeDtypeStruct((SUBLANES, width), jnp.float32),
        ),
        in_specs=[in_smem, in_vmem],
        out_specs=(in_vmem, in_vmem, in_vmem),
        compiler_params=params(8),
        name="arrived",
    )(me, got)


def sum_kernel(start_ref, label_ref, rows_ref, *refs):
    sum_ref, held, sem = refs[-3:]
    owner_count, per_owner, _ = sum_ref.shape
    window = held.shape[1]

    def copy(owner, slot):
        first = aligned_start(start_ref[owner], rows_ref.shape[0], window)
        return pltpu.make_async_copy(rows_ref.at[pl.ds(first, window), :], held.at[slot], sem.at[slot])

    copy(0, 0).start()

    def body(owner, carry):
        slot = lax.rem(owner, 2)

        @pl.when(owner + 1 < owner_count)
        def _():
            copy(owner + 1, 1 - slot).start()

        copy(owner, slot).wait()
        labels = label_ref[pl.ds(owner, 1), :][:, :window]
        cluster = lax.broadcasted_iota(jnp.int32, (per_owner, window), 0)
        member = (labels == cluster).astype(jnp.float32).astype(jnp.bfloat16)
        values = held[slot]
        high = values.astype(jnp.bfloat16)
        rest = values - high.astype(jnp.float32)
        middle = rest.astype(jnp.bfloat16)
        low = (rest - middle.astype(jnp.float32)).astype(jnp.bfloat16)
        total = jnp.dot(member, high, preferred_element_type=jnp.float32)
        total += jnp.dot(member, middle, preferred_element_type=jnp.float32)
        total += jnp.dot(member, low, preferred_element_type=jnp.float32)
        sum_ref[pl.ds(owner, 1)] = total[None]
        return carry

    lax.fori_loop(0, owner_count, body, 0)


def slot_sums(starts, labels, embeddings, per_owner, capacity, after):
    owner_count = labels.shape[0]
    width = embeddings.shape[1]
    return pl.pallas_call(
        sum_kernel,
        out_shape=jax.ShapeDtypeStruct((owner_count, per_owner, width), jnp.float32),
        in_specs=[in_smem, in_vmem, anywhere] + [anywhere] * len(after),
        out_specs=in_vmem,
        scratch_shapes=[
            pltpu.VMEM((2, capacity + SUBLANES, width), jnp.float32),
            pltpu.SemaphoreType.DMA((2,)),
        ],
        compiler_params=params(),
        cost_estimate=pl.CostEstimate(
            flops=6 * owner_count * per_owner * capacity * width,
            bytes_accessed=4 * embeddings.size,
            transcendentals=0,
        ),
        name="sums",
    )(starts, labels, embeddings, *after)


def gram_kernel(begin, rows, wide, after_count, turns_of, *refs):
    chunk_ref, row_ref, column_ref, best_ref, *refs = refs
    flat_ref = centroid_ref = result_ref = None
    if begin:
        flat_ref, *refs = refs
    refs = refs[after_count:]
    if turns_of:
        centroid_ref, me_ref, result_ref, *refs, out_ref, cosine_ref = refs
    else:
        out_ref, flat_ref, *refs = refs
    mine, turned, labels, tiles, even, odd, best, sem, tile_sem = refs
    first = begin // LANES
    size = tiles.shape[2]
    count = round_up(-(-begin // size), 2)

    def line_of(tile):
        return jnp.minimum(tile * (size // LANES), first - size // LANES)

    def fetch(tile):
        start = pl.multiple_of(line_of(tile) * LANES, LANES)
        slot = lax.rem(tile, 4)
        return pltpu.make_async_copy(flat_ref.at[:, pl.ds(start, size)], tiles.at[slot], tile_sem.at[slot])

    chunk_copy = pltpu.make_async_copy(chunk_ref, mine.at[pl.ds(0, rows), :], sem.at[0])
    label_copy = pltpu.make_async_copy(column_ref.at[pl.ds(begin, wide), :], labels, sem.at[1])
    chunk_copy.start()
    label_copy.start()
    for tile in range(min(count, 3)):
        fetch(jnp.int32(tile)).start()
    if rows < wide:
        mine[rows:wide, :] = jnp.zeros((wide - rows, mine.shape[1]), mine.dtype)
    if turns_of:
        mine[wide:, :] = centroid_ref[...]
        cosine_ref[...] = jnp.zeros(cosine_ref.shape, jnp.float32)
    out_ref[...] = best_ref[...]
    best[...] = jnp.full(best.shape, -2.0, jnp.float32)
    chunk_copy.wait()
    label_copy.wait()
    turned[...] = mine[:wide, :].T
    if not turns_of:
        flat_copy = pltpu.make_async_copy(turned, flat_ref.at[:, pl.ds(begin, wide)], sem.at[2])
        flat_copy.start()

    def products(right):
        return jnp.dot(mine[...], right, preferred_element_type=jnp.float32)

    halves = 2 if size % (4 * LANES) == 0 else 1

    def multiply(held, slot, half):
        here = slice(half * (size // halves), (half + 1) * (size // halves))
        held[:, here] = products(tiles[slot, :, here])

    def cosines(values, line):
        cluster = lax.broadcasted_iota(jnp.int32, values.shape, 0)
        own = jnp.where(row_ref[pl.ds(line, 1), :] == cluster, values, 0.0)
        cosine_ref[pl.ds(line, 1), :] = jnp.sum(own, 0, keepdims=True)

    def reduce_tile(held, tile, half):
        parts = range(half * (size // halves) // LANES, (half + 1) * (size // halves) // LANES)
        lines = {part: line_of(tile) + part for part in parts}
        tops = {part: jnp.full((SUBLANES, LANES), -2.0, jnp.float32) for part in parts}
        against = {
            part: jnp.broadcast_to(row_ref[pl.ds(lines[part], 1), :], (LANES, LANES)) for part in parts
        }
        for begin_row in range(0, wide, LANES):
            span = slice(begin_row, begin_row + LANES)
            own = labels[span, :]
            fold = best[span, :]
            for part in parts:
                near = jnp.where(own == against[part], held[span, part * LANES : (part + 1) * LANES], -2.0)
                fold = jnp.maximum(fold, near)
                tops[part] = jnp.maximum(tops[part], jnp.max(near.reshape(-1, SUBLANES, LANES), 0))
            best[span, :] = fold
        for part in parts:
            out_ref[pl.ds(lines[part], 1), :] = jnp.maximum(
                out_ref[pl.ds(lines[part], 1), :], jnp.max(tops[part], 0, keepdims=True)
            )
            if turns_of:
                cosines(held[wide:, part * LANES : (part + 1) * LANES], lines[part])

    if begin:
        fetch(jnp.int32(0)).wait()
        for half in range(halves):
            multiply(even, 0, half)

        def body(pair, carry):
            tile = pair * 2
            fetch(tile + 1).wait()
            fetch(tile + 3).start()
            for half in range(halves):
                multiply(odd, lax.rem(tile + 1, 4), half)
                reduce_tile(even, tile, half)
            fetch(tile + 2).wait()

            @pl.when(tile + 4 < count)
            def _():
                fetch(tile + 4).start()

            for half in range(halves):
                multiply(even, lax.rem(tile + 2, 4), half)
                reduce_tile(odd, tile + 1, half)
            return carry

        lax.fori_loop(0, count // 2 - 1, body, 0)
        fetch(jnp.int32(count - 1)).wait()
        for half in range(halves):
            multiply(odd, (count - 1) % 4, half)
            reduce_tile(even, jnp.int32(count - 2), half)
        for half in range(halves):
            reduce_tile(odd, jnp.int32(count - 1), half)
    own = products(turned[...])
    row = lax.broadcasted_iota(jnp.int32, (wide, LANES), 0)
    column = lax.broadcasted_iota(jnp.int32, (wide, LANES), 1)
    for block in range(wide // LANES):
        line = first + block
        here = slice(block * LANES, (block + 1) * LANES)
        allowed = (labels[...] == row_ref[line : line + 1, :]) & (row != column + block * LANES)
        near = jnp.max(jnp.where(allowed, own[:wide, here], -2.0), 0, keepdims=True)
        other = jnp.max(best[here, :].T, 0, keepdims=True)
        out_ref[line : line + 1, :] = jnp.maximum(near, other)
        if turns_of:
            cosines(own[wide:, here], line)
    if turns_of:
        blocks = row_ref.shape[0] // len(turns_of)
        half = result_ref.shape[1] // 2
        result_ref[...] = jnp.zeros(result_ref.shape, jnp.float32)
        for place, turn in enumerate(turns_of):
            source = lax.rem(me_ref[0] + len(turns_of) - turn, len(turns_of))
            lines = slice(place * blocks, (place + 1) * blocks)
            result_ref[source, :blocks, :] = out_ref[lines, :]
            result_ref[source, half : half + blocks, :] = cosine_ref[lines, :]
    else:
        flat_copy.wait()


def gram_step(rows, columns, best, flat, chunk, begin, after=(), final=None):
    length, width = chunk.shape
    wide = round_up(length, LANES)
    tall = wide
    size = min(TILE, begin) if begin else LANES
    flat_shape = jax.ShapeDtypeStruct((width, columns.shape[0]), jnp.bfloat16)
    inputs = [chunk, rows, columns, best]
    in_specs = [anywhere, in_vmem, anywhere, in_vmem]
    aliases = {}
    if begin:
        if not final:
            aliases = {len(inputs): 1}
        inputs.append(flat)
        in_specs.append(anywhere)
    inputs += after
    in_specs += [anywhere] * len(after)
    out_shape = (jax.ShapeDtypeStruct(best.shape, jnp.float32), flat_shape)
    out_specs = (in_vmem, anywhere)
    turns_of = ()
    extra = []
    if final:
        centroid_unit, me, turns_of = final
        tall += centroid_unit.shape[0]
        inputs += [centroid_unit, me]
        in_specs += [in_vmem, in_smem]
        half = round_up(rows.shape[0] // len(turns_of) + 1, SUBLANES)
        out_shape = jax.ShapeDtypeStruct((len(turns_of), 2 * half, LANES), jnp.float32)
        out_specs = in_vmem
        extra = [pltpu.VMEM(best.shape, jnp.float32)] * 2
    return pl.pallas_call(
        functools.partial(gram_kernel, begin, length, wide, len(after), turns_of),
        out_shape=out_shape,
        in_specs=in_specs,
        out_specs=out_specs,
        scratch_shapes=[
            pltpu.VMEM((tall, width), jnp.bfloat16),
            pltpu.VMEM((width, wide), jnp.bfloat16),
            pltpu.VMEM((wide, LANES), jnp.int32),
            pltpu.VMEM((4, width, size), jnp.bfloat16),
            pltpu.VMEM((tall, size), jnp.float32),
            pltpu.VMEM((tall, size), jnp.float32),
            pltpu.VMEM((wide, LANES), jnp.float32),
            pltpu.SemaphoreType.DMA((3,)),
            pltpu.SemaphoreType.DMA((4,)),
        ]
        + extra,
        input_output_aliases=aliases,
        compiler_params=params(),
        cost_estimate=brief,
        name="gram",
    )(*inputs)


def pack_kernel(share_ref, tally_ref, *refs):
    packed_ref = refs[-1]
    packed_ref[: share_ref.shape[0], :] = share_ref[...]
    packed_ref[share_ref.shape[0] :, :] = tally_ref[...]


def pack_share(share, tally, after):
    length = share.shape[0] + tally.shape[0]
    return pl.pallas_call(
        pack_kernel,
        out_shape=jax.ShapeDtypeStruct((length, share.shape[1]), jnp.float32),
        in_specs=[in_vmem, in_vmem] + [anywhere] * len(after),
        out_specs=in_vmem,
        compiler_params=params(8),
        name="pack",
    )(share, tally, *after)


def centroid_kernel(gathered_ref, centroid_ref, unit_ref):
    groups, length, width = gathered_ref.shape
    share = length - SUBLANES
    per_owner = centroid_ref.shape[0]
    tally = jnp.sum(gathered_ref[:, share, :LANES], 0, keepdims=True)
    column = jnp.broadcast_to(tally, (LANES, LANES)).T[:per_owner, :]
    sums = jnp.concatenate([gathered_ref[group, :share, :] for group in range(groups)], 0)
    centroids = sums / jnp.concatenate([column] * (width // LANES), 1)
    centroid_ref[...] = centroids
    scale = lax.rsqrt(jnp.sum(centroids * centroids, -1, keepdims=True) + epsilon)
    unit_ref[...] = (centroids * scale).astype(jnp.bfloat16)


def make_centroids(gathered, per_owner):
    shape = (per_owner, gathered.shape[2])
    return pl.pallas_call(
        centroid_kernel,
        out_shape=(
            jax.ShapeDtypeStruct(shape, jnp.float32),
            jax.ShapeDtypeStruct(shape, jnp.bfloat16),
        ),
        in_specs=[in_vmem],
        out_specs=(in_vmem, in_vmem),
        compiler_params=params(8),
        name="centroids",
    )(gathered)


def place_kernel(per_owner, start_ref, slot_ref, back_ref, near_ref, cosine_ref, held, result):
    owner_count, double, _ = back_ref.shape
    span = double // 2
    rows = slot_ref.shape[0]
    held[...] = jnp.full(held.shape, -1, jnp.int32)
    held[:rows, :] = slot_ref[...]
    result[...] = jnp.zeros(result.shape, jnp.float32)
    lane = lax.broadcasted_iota(jnp.int32, (span, LANES), 1)
    for owner in range(owner_count):
        start = start_ref[owner]
        first = pl.ds(jnp.right_shift(start, 7), span)
        shift = jnp.bitwise_and(start, LANES - 1)
        slots = held[first, :]
        mine = (slots >= owner * per_owner) & (slots < (owner + 1) * per_owner)
        for kind in range(2):
            turned = pltpu.roll(back_ref[owner, kind * span : (kind + 1) * span, :], shift, 1)
            earlier = pltpu.roll(turned, 1, 0)
            moved = jnp.where(lane >= shift, turned, earlier)
            result[kind, first, :] = jnp.where(mine, moved, result[kind, first, :])
    near_ref[...] = result[0, :rows, :]
    cosine_ref[...] = result[1, :rows, :]


def place_rows(starts, slots, back, per_owner):
    span = back.shape[1] // 2
    rows = slots.shape[0]
    return pl.pallas_call(
        functools.partial(place_kernel, per_owner),
        out_shape=(jax.ShapeDtypeStruct(slots.shape, jnp.float32),) * 2,
        in_specs=[in_smem, in_vmem, in_vmem],
        out_specs=(in_vmem, in_vmem),
        scratch_shapes=[
            pltpu.VMEM((rows + span, LANES), jnp.int32),
            pltpu.VMEM((2, rows + span, LANES), jnp.float32),
        ],
        compiler_params=params(8),
        name="place",
    )(starts, slots, back)


def turns(count):
    order = sorted(range(count), key=lambda turn: (min(turn, count - turn), turn))
    if count == 8:
        order = [0, 1, 2, 3, 7, 6, 5, 4]
    return order


def per_device(embeddings, assign, cluster_slot):
    row_count, width = embeddings.shape
    owner_count = lax.axis_size("docs")
    per_owner = cluster_slot.shape[0] // owner_count
    capacity = row_count // owner_count + row_count // (4 * owner_count)
    padded = round_up(capacity, LANES)
    blocks = padded // LANES
    me = lax.axis_index("docs").astype(jnp.int32).reshape(1)
    turns_of = turns(owner_count)

    slots, starts = make_plan(
        assign.reshape(-1, LANES), cluster_slot.reshape(-1, LANES), owner_count, per_owner, row_count - capacity
    )

    sent = []
    for place, turn in enumerate(turns_of):
        sent.append(unit_piece(starts, me, embeddings, turn, 0, capacity, sent[-1:] if place > 1 else []))

    def travel(place, piece):
        turn = turns_of[place]
        return lax.ppermute(piece, "docs", [(i, (i + turn) % owner_count) for i in range(owner_count)])

    chunks = [sent[0]] + [travel(place, sent[place]) for place in (1, 2, 3)]
    sum_labels = summed_labels(starts, slots, owner_count, per_owner, capacity)
    partial_sums = slot_sums(starts, sum_labels, embeddings, per_owner, capacity, sent[1:8])
    partial_sums = hold_until(partial_sums, chunks[1:3])
    wire_labels = sent_labels(starts, slots, owner_count, per_owner, capacity, partial_sums)
    got_labels = lax.all_to_all(wire_labels, "docs", split_axis=0, concat_axis=0, tiled=True)
    rows, columns, group_tally = arrived_labels(me, got_labels, turns_of, blocks, width)
    group_share = lax.psum_scatter(partial_sums, "grp", scatter_dimension=1, tiled=True)
    group_share = hold_until(group_share, [chunks[3], got_labels])
    share = lax.psum_scatter(group_share, "docs", scatter_dimension=0, tiled=True)[0]
    for place in range(4, owner_count):
        after = [chunks[4]] if place == owner_count - 1 else [chunks[3], got_labels]
        chunks.append(travel(place, hold_until(sent[place], after)))

    bests = [jnp.full((owner_count * blocks, LANES), -2.0, jnp.float32)]
    flat = None
    for place in range(owner_count - 1):
        after = []
        if place == owner_count - 2:
            packed = pack_share(share, group_tally, bests[-2:-1])
            centroids, centroid_unit = make_centroids(lax.all_gather(packed, "grp"), per_owner)
            after = [centroid_unit]
        best, flat = gram_step(rows, columns, bests[-1], flat, chunks[place], place * padded, after)
        bests.append(best)
    results = gram_step(
        rows, columns, bests[-1], flat, chunks[-1], (owner_count - 1) * padded, final=(centroid_unit, me, turns_of)
    )
    back = lax.all_to_all(results, "docs", split_axis=0, concat_axis=0, tiled=True)
    near, cosine = place_rows(starts, slots, back, per_owner)
    return (centroids, near.reshape(-1), cosine.reshape(-1))


def solution(mesh):
    placed = (P(("grp", "docs"), None), P(("grp", "docs")), P())
    return jax.shard_map(
        per_device,
        mesh=mesh,
        in_specs=placed,
        out_specs=(P("docs", None), P(("grp", "docs")), P(("grp", "docs"))),
        check_vma=False,
    )
```

```python
import functools

import jax
import jax.numpy as jnp
from jax import lax
from jax.experimental import pallas as pl
from jax.experimental.pallas import tpu as pltpu
from jax.sharding import PartitionSpec as P

epsilon = 1e-06
LANES = 128
SUBLANES = 8
MIB = 1024 * 1024
TILE = 512
in_vmem = pl.BlockSpec(memory_space=pltpu.VMEM)
in_smem = pl.BlockSpec(memory_space=pltpu.SMEM)
anywhere = pl.BlockSpec(memory_space=pl.ANY)
brief = pl.CostEstimate(flops=1000, bytes_accessed=1000, transcendentals=0)


def round_up(value, step):
    return -(-value // step) * step


def params(mib=44):
    return pltpu.CompilerParams(vmem_limit_bytes=mib * MIB)


def look_up(table_ref, index):
    lane = jnp.bitwise_and(index, LANES - 1)
    row = jnp.right_shift(index, 7)
    found = jnp.zeros(index.shape, jnp.int32)
    for part in range(table_ref.shape[0]):
        entries = jnp.broadcast_to(table_ref[part : part + 1, :], index.shape)
        found = jnp.where(row == part, jnp.take_along_axis(entries, lane, axis=1), found)
    return found


def rows_below(slots, bound):
    return jnp.sum((slots < bound).astype(jnp.float32)).astype(jnp.int32)


def plan_kernel(per_owner, limit, assign_ref, table_ref, slot_ref, start_ref):
    slots = look_up(table_ref, assign_ref[...])
    slot_ref[...] = slots
    for owner in range(start_ref.shape[0]):
        start_ref[owner] = jnp.minimum(rows_below(slots, owner * per_owner), limit)


def make_plan(assign_rows, table, owner_count, per_owner, limit):
    return pl.pallas_call(
        functools.partial(plan_kernel, per_owner, limit),
        out_shape=(
            jax.ShapeDtypeStruct(assign_rows.shape, jnp.int32),
            jax.ShapeDtypeStruct((owner_count,), jnp.int32),
        ),
        in_specs=[in_vmem, in_vmem],
        out_specs=(in_vmem, in_smem),
        compiler_params=params(8),
        name="plan",
    )(assign_rows, table)


def unit_kernel(steps, offset, turn, start_ref, me_ref, rows_ref, *refs):
    unit_ref, held, sem = refs[-3:]
    part = unit_ref.shape[0] // steps
    window = part + SUBLANES
    start = start_ref[lax.rem(me_ref[0] + turn, start_ref.shape[0])] + offset

    def first(step):
        return aligned_start(start + step * part, rows_ref.shape[0], window)

    copies = [
        pltpu.make_async_copy(rows_ref.at[pl.ds(first(step), window), :], held.at[step], sem.at[step])
        for step in range(steps)
    ]
    for copy in copies:
        copy.start()
    for step in range(steps):
        copies[step].wait()
        shift = start + step * part - first(step)
        groups = held[step].reshape(window // SUBLANES, SUBLANES, -1)
        turned = pltpu.roll(groups, SUBLANES - shift, 1)
        line = lax.broadcasted_iota(jnp.int32, (part // SUBLANES, SUBLANES, groups.shape[2]), 1)
        values = jnp.where(line < SUBLANES - shift, turned[:-1], turned[1:]).reshape(part, -1)
        scale = lax.rsqrt(jnp.sum(values * values, -1, keepdims=True) + epsilon)
        unit_ref[step * part : (step + 1) * part, :] = (values * scale).astype(jnp.bfloat16)


def unit_piece(starts, me, embeddings, turn, offset, rows, after):
    width = embeddings.shape[1]
    steps = rows // LANES if rows % LANES == 0 else 1
    return pl.pallas_call(
        functools.partial(unit_kernel, steps, offset, turn),
        out_shape=jax.ShapeDtypeStruct((rows, width), jnp.bfloat16),
        in_specs=[in_smem, in_smem, anywhere] + [anywhere] * len(after),
        out_specs=in_vmem,
        scratch_shapes=[
            pltpu.VMEM((steps, rows // steps + SUBLANES, width), jnp.float32),
            pltpu.SemaphoreType.DMA((steps,)),
        ],
        compiler_params=params(),
        cost_estimate=brief,
        name="unit",
    )(starts, me, embeddings, *after)


def hold_until(values, arrived):
    def nothing(*refs):
        pass

    return pl.pallas_call(
        nothing,
        out_shape=jax.ShapeDtypeStruct(values.shape, values.dtype),
        in_specs=[anywhere] * (1 + len(arrived)),
        out_specs=anywhere,
        input_output_aliases={0: 0},
        compiler_params=params(48),
        cost_estimate=brief,
        name="hold",
    )(values, *arrived)


def aligned_start(start, row_count, window):
    begin = jnp.minimum(jnp.left_shift(jnp.right_shift(start, 3), 3), row_count - window)
    return pl.multiple_of(begin, SUBLANES)


def flat_window(held, start, rows):
    span = round_up(rows + 1, SUBLANES)
    shift = jnp.bitwise_and(start, LANES - 1)
    block = held[pl.ds(jnp.right_shift(start, 7), span), :]
    turned = pltpu.roll(block, jnp.bitwise_and(LANES - shift, LANES - 1), 1)
    following = pltpu.roll(turned, span - 1, 0)
    lane = lax.broadcasted_iota(jnp.int32, block.shape, 1)
    return jnp.where(lane < LANES - shift, turned, following)


def window_labels(held, slots, owner, start, per_owner, capacity, blocks):
    low = owner * per_owner
    mine = (slots >= low) & (slots < low + per_owner)
    held[: slots.shape[0], :] = jnp.where(mine, slots - low, -1)
    labels = flat_window(held, start, blocks)
    place = lax.broadcasted_iota(jnp.int32, labels.shape, 0) * LANES + lax.broadcasted_iota(
        jnp.int32, labels.shape, 1
    )
    return jnp.where(place < capacity, labels, -1)


def summed_kernel(per_owner, capacity, start_ref, slot_ref, sum_ref, held):
    owner_count = sum_ref.shape[0]
    held[...] = jnp.full(held.shape, -1, jnp.int32)
    slots = slot_ref[...]
    window = capacity + SUBLANES
    wide = sum_ref.shape[1] // LANES
    for owner in range(owner_count):
        aligned = aligned_start(start_ref[owner], slots.size, window)
        labels = window_labels(held, slots, owner, aligned, per_owner, window, wide)
        for block in range(wide):
            sum_ref[owner : owner + 1, block * LANES : (block + 1) * LANES] = labels[block : block + 1, :]


def summed_labels(starts, slots, owner_count, per_owner, capacity):
    return pl.pallas_call(
        functools.partial(summed_kernel, per_owner, capacity),
        out_shape=jax.ShapeDtypeStruct((owner_count, round_up(capacity + SUBLANES, LANES)), jnp.int32),
        in_specs=[in_smem, in_vmem],
        out_specs=in_vmem,
        scratch_shapes=[pltpu.VMEM((slots.shape[0] + 2 * SUBLANES, LANES), jnp.int32)],
        compiler_params=params(8),
        name="summed",
    )(starts, slots)


def sent_kernel(per_owner, capacity, start_ref, slot_ref, after_ref, sent_ref, held):
    owner_count, span, _ = sent_ref.shape
    held[...] = jnp.full(held.shape, -1, jnp.int32)
    slots = slot_ref[...]
    for owner in range(owner_count):
        labels = window_labels(held, slots, owner, start_ref[owner], per_owner, capacity, span - 1)
        sent_ref[owner] = labels[:span, :]


def sent_labels(starts, slots, owner_count, per_owner, capacity, after):
    span = round_up(-(-capacity // LANES) + 1, SUBLANES)
    return pl.pallas_call(
        functools.partial(sent_kernel, per_owner, capacity),
        out_shape=jax.ShapeDtypeStruct((owner_count, span, LANES), jnp.int32),
        in_specs=[in_smem, in_vmem, anywhere],
        out_specs=in_vmem,
        scratch_shapes=[pltpu.VMEM((slots.shape[0] + 2 * SUBLANES, LANES), jnp.int32)],
        compiler_params=params(8),
        name="sent",
    )(starts, slots, after)


def arrived_kernel(blocks, turns_of, me_ref, got_ref, row_ref, column_ref, tally_ref):
    tally = jnp.zeros((LANES, LANES), jnp.float32)
    cluster = lax.broadcasted_iota(jnp.int32, tally.shape, 0)
    for place, turn in enumerate(turns_of):
        source = lax.rem(me_ref[0] + len(turns_of) - turn, len(turns_of))
        for block in range(blocks):
            line = place * blocks + block
            spread = jnp.broadcast_to(got_ref[source, block : block + 1, :], tally.shape)
            row_ref[line : line + 1, :] = spread[:1, :]
            column_ref[line * LANES : (line + 1) * LANES, :] = spread.T
            tally += (spread == cluster).astype(jnp.float32)
    total = jnp.broadcast_to(jnp.sum(tally, 1, keepdims=True), tally.shape)
    tally_ref[...] = jnp.zeros(tally_ref.shape, jnp.float32)
    tally_ref[:, :LANES] = total.T[:SUBLANES, :]


def arrived_labels(me, got, turns_of, blocks, width):
    lines = len(turns_of) * blocks
    return pl.pallas_call(
        functools.partial(arrived_kernel, blocks, turns_of),
        out_shape=(
            jax.ShapeDtypeStruct((lines, LANES), jnp.int32),
            jax.ShapeDtypeStruct((lines * LANES, LANES), jnp.int32),
            jax.ShapeDtypeStruct((SUBLANES, width), jnp.float32),
        ),
        in_specs=[in_smem, in_vmem],
        out_specs=(in_vmem, in_vmem, in_vmem),
        compiler_params=params(8),
        name="arrived",
    )(me, got)


def sum_kernel(start_ref, label_ref, rows_ref, *refs):
    sum_ref, held, sem = refs[-3:]
    owner_count, per_owner, _ = sum_ref.shape
    window = held.shape[1]

    def copy(owner, slot):
        first = aligned_start(start_ref[owner], rows_ref.shape[0], window)
        return pltpu.make_async_copy(rows_ref.at[pl.ds(first, window), :], held.at[slot], sem.at[slot])

    copy(0, 0).start()

    def body(owner, carry):
        slot = lax.rem(owner, 2)

        @pl.when(owner + 1 < owner_count)
        def _():
            copy(owner + 1, 1 - slot).start()

        copy(owner, slot).wait()
        labels = label_ref[pl.ds(owner, 1), :][:, :window]
        cluster = lax.broadcasted_iota(jnp.int32, (per_owner, window), 0)
        member = (labels == cluster).astype(jnp.float32).astype(jnp.bfloat16)
        values = held[slot]
        high = values.astype(jnp.bfloat16)
        rest = values - high.astype(jnp.float32)
        middle = rest.astype(jnp.bfloat16)
        low = (rest - middle.astype(jnp.float32)).astype(jnp.bfloat16)
        total = jnp.dot(member, high, preferred_element_type=jnp.float32)
        total += jnp.dot(member, middle, preferred_element_type=jnp.float32)
        total += jnp.dot(member, low, preferred_element_type=jnp.float32)
        sum_ref[pl.ds(owner, 1)] = total[None]
        return carry

    lax.fori_loop(0, owner_count, body, 0)


def slot_sums(starts, labels, embeddings, per_owner, capacity, after):
    owner_count = labels.shape[0]
    width = embeddings.shape[1]
    return pl.pallas_call(
        sum_kernel,
        out_shape=jax.ShapeDtypeStruct((owner_count, per_owner, width), jnp.float32),
        in_specs=[in_smem, in_vmem, anywhere] + [anywhere] * len(after),
        out_specs=in_vmem,
        scratch_shapes=[
            pltpu.VMEM((2, capacity + SUBLANES, width), jnp.float32),
            pltpu.SemaphoreType.DMA((2,)),
        ],
        compiler_params=params(),
        cost_estimate=pl.CostEstimate(
            flops=6 * owner_count * per_owner * capacity * width,
            bytes_accessed=4 * embeddings.size,
            transcendentals=0,
        ),
        name="sums",
    )(starts, labels, embeddings, *after)


def gram_kernel(begin, rows, wide, after_count, turns_of, *refs):
    chunk_ref, row_ref, column_ref, best_ref, *refs = refs
    flat_ref = centroid_ref = result_ref = None
    if begin:
        flat_ref, *refs = refs
    refs = refs[after_count:]
    if turns_of:
        centroid_ref, me_ref, result_ref, *refs, out_ref, cosine_ref = refs
    else:
        out_ref, flat_ref, *refs = refs
    mine, turned, labels, tiles, even, odd, best, sem, tile_sem = refs
    first = begin // LANES
    size = tiles.shape[2]
    count = -(-begin // size)

    def line_of(tile):
        return jnp.minimum(tile * (size // LANES), first - size // LANES)

    def fetch(tile):
        start = pl.multiple_of(line_of(tile) * LANES, LANES)
        slot = lax.rem(tile, 4)
        return pltpu.make_async_copy(flat_ref.at[:, pl.ds(start, size)], tiles.at[slot], tile_sem.at[slot])

    chunk_copy = pltpu.make_async_copy(chunk_ref, mine.at[pl.ds(0, rows), :], sem.at[0])
    label_copy = pltpu.make_async_copy(column_ref.at[pl.ds(begin, wide), :], labels, sem.at[1])
    chunk_copy.start()
    label_copy.start()
    for tile in range(min(count, 3)):
        fetch(jnp.int32(tile)).start()
    if rows < wide:
        mine[rows:wide, :] = jnp.zeros((wide - rows, mine.shape[1]), mine.dtype)
    if turns_of:
        mine[wide:, :] = centroid_ref[...]
        cosine_ref[...] = jnp.zeros(cosine_ref.shape, jnp.float32)
    out_ref[...] = best_ref[...]
    best[...] = jnp.full(best.shape, -2.0, jnp.float32)
    chunk_copy.wait()
    label_copy.wait()
    turned[...] = mine[:wide, :].T
    if not turns_of:
        flat_copy = pltpu.make_async_copy(turned, flat_ref.at[:, pl.ds(begin, wide)], sem.at[2])
        flat_copy.start()

    def products(right):
        return jnp.dot(mine[...], right, preferred_element_type=jnp.float32)

    halves = 2 if size % (4 * LANES) == 0 else 1

    def multiply(held, slot, half):
        here = slice(half * (size // halves), (half + 1) * (size // halves))
        held[:, here] = products(tiles[slot, :, here])

    def cosines(values, line):
        cluster = lax.broadcasted_iota(jnp.int32, values.shape, 0)
        own = jnp.where(row_ref[pl.ds(line, 1), :] == cluster, values, 0.0)
        cosine_ref[pl.ds(line, 1), :] = jnp.sum(own, 0, keepdims=True)

    def reduce_tile(held, tile, half):
        parts = range(half * (size // halves) // LANES, (half + 1) * (size // halves) // LANES)
        lines = {part: line_of(tile) + part for part in parts}
        tops = {part: jnp.full((SUBLANES, LANES), -2.0, jnp.float32) for part in parts}
        against = {
            part: jnp.broadcast_to(row_ref[pl.ds(lines[part], 1), :], (LANES, LANES)) for part in parts
        }
        for begin_row in range(0, wide, LANES):
            span = slice(begin_row, begin_row + LANES)
            own = labels[span, :]
            fold = best[span, :]
            for part in parts:
                near = jnp.where(own == against[part], held[span, part * LANES : (part + 1) * LANES], -2.0)
                fold = jnp.maximum(fold, near)
                tops[part] = jnp.maximum(tops[part], jnp.max(near.reshape(-1, SUBLANES, LANES), 0))
            best[span, :] = fold
        for part in parts:
            out_ref[pl.ds(lines[part], 1), :] = jnp.maximum(
                out_ref[pl.ds(lines[part], 1), :], jnp.max(tops[part], 0, keepdims=True)
            )
            if turns_of:
                cosines(held[wide:, part * LANES : (part + 1) * LANES], lines[part])

    if begin:
        fetch(jnp.int32(0)).wait()
        for half in range(halves):
            multiply(even, 0, half)

        def body(pair, carry):
            tile = pair * 2
            fetch(tile + 1).wait()

            @pl.when(tile + 3 < count)
            def _():
                fetch(tile + 3).start()

            for half in range(halves):
                multiply(odd, lax.rem(tile + 1, 4), half)
                reduce_tile(even, tile, half)
            fetch(tile + 2).wait()

            @pl.when(tile + 4 < count)
            def _():
                fetch(tile + 4).start()

            for half in range(halves):
                multiply(even, lax.rem(tile + 2, 4), half)
                reduce_tile(odd, tile + 1, half)
            return carry

        lax.fori_loop(0, (count - 1) // 2, body, 0)
        left = even
        if count % 2 == 0:
            left = odd
            fetch(jnp.int32(count - 1)).wait()
            for half in range(halves):
                multiply(odd, (count - 1) % 4, half)
                reduce_tile(even, jnp.int32(count - 2), half)
        for half in range(halves):
            reduce_tile(left, jnp.int32(count - 1), half)
    own = products(turned[...])
    row = lax.broadcasted_iota(jnp.int32, (wide, LANES), 0)
    column = lax.broadcasted_iota(jnp.int32, (wide, LANES), 1)
    for block in range(wide // LANES):
        line = first + block
        here = slice(block * LANES, (block + 1) * LANES)
        allowed = (labels[...] == row_ref[line : line + 1, :]) & (row != column + block * LANES)
        near = jnp.max(jnp.where(allowed, own[:wide, here], -2.0), 0, keepdims=True)
        other = jnp.max(best[here, :].T, 0, keepdims=True)
        out_ref[line : line + 1, :] = jnp.maximum(near, other)
        if turns_of:
            cosines(own[wide:, here], line)
    if turns_of:
        blocks = row_ref.shape[0] // len(turns_of)
        half = result_ref.shape[1] // 2
        result_ref[...] = jnp.zeros(result_ref.shape, jnp.float32)
        for place, turn in enumerate(turns_of):
            source = lax.rem(me_ref[0] + len(turns_of) - turn, len(turns_of))
            lines = slice(place * blocks, (place + 1) * blocks)
            result_ref[source, :blocks, :] = out_ref[lines, :]
            result_ref[source, half : half + blocks, :] = cosine_ref[lines, :]
    else:
        flat_copy.wait()


def gram_step(rows, columns, best, flat, chunk, begin, after=(), final=None):
    length, width = chunk.shape
    wide = round_up(length, LANES)
    tall = wide
    size = min(TILE, begin) if begin else LANES
    flat_shape = jax.ShapeDtypeStruct((width, columns.shape[0]), jnp.bfloat16)
    inputs = [chunk, rows, columns, best]
    in_specs = [anywhere, in_vmem, anywhere, in_vmem]
    aliases = {}
    if begin:
        if not final:
            aliases = {len(inputs): 1}
        inputs.append(flat)
        in_specs.append(anywhere)
    inputs += after
    in_specs += [anywhere] * len(after)
    out_shape = (jax.ShapeDtypeStruct(best.shape, jnp.float32), flat_shape)
    out_specs = (in_vmem, anywhere)
    turns_of = ()
    extra = []
    if final:
        centroid_unit, me, turns_of = final
        tall += centroid_unit.shape[0]
        inputs += [centroid_unit, me]
        in_specs += [in_vmem, in_smem]
        half = round_up(rows.shape[0] // len(turns_of) + 1, SUBLANES)
        out_shape = jax.ShapeDtypeStruct((len(turns_of), 2 * half, LANES), jnp.float32)
        out_specs = in_vmem
        extra = [pltpu.VMEM(best.shape, jnp.float32)] * 2
    return pl.pallas_call(
        functools.partial(gram_kernel, begin, length, wide, len(after), turns_of),
        out_shape=out_shape,
        in_specs=in_specs,
        out_specs=out_specs,
        scratch_shapes=[
            pltpu.VMEM((tall, width), jnp.bfloat16),
            pltpu.VMEM((width, wide), jnp.bfloat16),
            pltpu.VMEM((wide, LANES), jnp.int32),
            pltpu.VMEM((4, width, size), jnp.bfloat16),
            pltpu.VMEM((tall, size), jnp.float32),
            pltpu.VMEM((tall, size), jnp.float32),
            pltpu.VMEM((wide, LANES), jnp.float32),
            pltpu.SemaphoreType.DMA((3,)),
            pltpu.SemaphoreType.DMA((4,)),
        ]
        + extra,
        input_output_aliases=aliases,
        compiler_params=params(),
        cost_estimate=brief,
        name="gram",
    )(*inputs)


def pack_kernel(share_ref, tally_ref, *refs):
    packed_ref = refs[-1]
    packed_ref[: share_ref.shape[0], :] = share_ref[...]
    packed_ref[share_ref.shape[0] :, :] = tally_ref[...]


def pack_share(share, tally, after):
    length = share.shape[0] + tally.shape[0]
    return pl.pallas_call(
        pack_kernel,
        out_shape=jax.ShapeDtypeStruct((length, share.shape[1]), jnp.float32),
        in_specs=[in_vmem, in_vmem] + [anywhere] * len(after),
        out_specs=in_vmem,
        compiler_params=params(8),
        name="pack",
    )(share, tally, *after)


def centroid_kernel(gathered_ref, centroid_ref, unit_ref):
    groups, length, width = gathered_ref.shape
    share = length - SUBLANES
    per_owner = centroid_ref.shape[0]
    tally = jnp.sum(gathered_ref[:, share, :LANES], 0, keepdims=True)
    column = jnp.broadcast_to(tally, (LANES, LANES)).T[:per_owner, :]
    sums = jnp.concatenate([gathered_ref[group, :share, :] for group in range(groups)], 0)
    centroids = sums / jnp.concatenate([column] * (width // LANES), 1)
    centroid_ref[...] = centroids
    scale = lax.rsqrt(jnp.sum(centroids * centroids, -1, keepdims=True) + epsilon)
    unit_ref[...] = (centroids * scale).astype(jnp.bfloat16)


def make_centroids(gathered, per_owner):
    shape = (per_owner, gathered.shape[2])
    return pl.pallas_call(
        centroid_kernel,
        out_shape=(
            jax.ShapeDtypeStruct(shape, jnp.float32),
            jax.ShapeDtypeStruct(shape, jnp.bfloat16),
        ),
        in_specs=[in_vmem],
        out_specs=(in_vmem, in_vmem),
        compiler_params=params(8),
        name="centroids",
    )(gathered)


def place_kernel(per_owner, start_ref, slot_ref, back_ref, near_ref, cosine_ref, held, result):
    owner_count, double, _ = back_ref.shape
    span = double // 2
    rows = slot_ref.shape[0]
    held[...] = jnp.full(held.shape, -1, jnp.int32)
    held[:rows, :] = slot_ref[...]
    result[...] = jnp.zeros(result.shape, jnp.float32)
    lane = lax.broadcasted_iota(jnp.int32, (span, LANES), 1)
    for owner in range(owner_count):
        start = start_ref[owner]
        first = pl.ds(jnp.right_shift(start, 7), span)
        shift = jnp.bitwise_and(start, LANES - 1)
        slots = held[first, :]
        mine = (slots >= owner * per_owner) & (slots < (owner + 1) * per_owner)
        for kind in range(2):
            turned = pltpu.roll(back_ref[owner, kind * span : (kind + 1) * span, :], shift, 1)
            earlier = pltpu.roll(turned, 1, 0)
            moved = jnp.where(lane >= shift, turned, earlier)
            result[kind, first, :] = jnp.where(mine, moved, result[kind, first, :])
    near_ref[...] = result[0, :rows, :]
    cosine_ref[...] = result[1, :rows, :]


def place_rows(starts, slots, back, per_owner):
    span = back.shape[1] // 2
    rows = slots.shape[0]
    return pl.pallas_call(
        functools.partial(place_kernel, per_owner),
        out_shape=(jax.ShapeDtypeStruct(slots.shape, jnp.float32),) * 2,
        in_specs=[in_smem, in_vmem, in_vmem],
        out_specs=(in_vmem, in_vmem),
        scratch_shapes=[
            pltpu.VMEM((rows + span, LANES), jnp.int32),
            pltpu.VMEM((2, rows + span, LANES), jnp.float32),
        ],
        compiler_params=params(8),
        name="place",
    )(starts, slots, back)


def turns(count):
    order = sorted(range(count), key=lambda turn: (min(turn, count - turn), turn))
    if count == 8:
        order = [0, 1, 2, 3, 7, 6, 5, 4]
    return order


def per_device(embeddings, assign, cluster_slot):
    row_count, width = embeddings.shape
    owner_count = lax.axis_size("docs")
    per_owner = cluster_slot.shape[0] // owner_count
    capacity = row_count // owner_count + row_count // (4 * owner_count)
    padded = round_up(capacity, LANES)
    blocks = padded // LANES
    me = lax.axis_index("docs").astype(jnp.int32).reshape(1)
    turns_of = turns(owner_count)

    slots, starts = make_plan(
        assign.reshape(-1, LANES), cluster_slot.reshape(-1, LANES), owner_count, per_owner, row_count - capacity
    )

    sent = []
    for place, turn in enumerate(turns_of):
        sent.append(unit_piece(starts, me, embeddings, turn, 0, capacity, sent[-1:] if place > 1 else []))

    def travel(place, piece):
        turn = turns_of[place]
        return lax.ppermute(piece, "docs", [(i, (i + turn) % owner_count) for i in range(owner_count)])

    chunks = [sent[0]] + [travel(place, sent[place]) for place in (1, 2, 3)]
    sum_labels = summed_labels(starts, slots, owner_count, per_owner, capacity)
    partial_sums = slot_sums(starts, sum_labels, embeddings, per_owner, capacity, sent[1:8])
    partial_sums = hold_until(partial_sums, chunks[1:3])
    wire_labels = sent_labels(starts, slots, owner_count, per_owner, capacity, partial_sums)
    got_labels = lax.all_to_all(wire_labels, "docs", split_axis=0, concat_axis=0, tiled=True)
    rows, columns, group_tally = arrived_labels(me, got_labels, turns_of, blocks, width)
    group_share = lax.psum_scatter(partial_sums, "grp", scatter_dimension=1, tiled=True)
    group_share = hold_until(group_share, [chunks[3], got_labels])
    share = lax.psum_scatter(group_share, "docs", scatter_dimension=0, tiled=True)[0]
    for place in range(4, owner_count):
        after = [chunks[4]] if place == owner_count - 1 else [chunks[3], got_labels]
        chunks.append(travel(place, hold_until(sent[place], after)))

    bests = [jnp.full((owner_count * blocks, LANES), -2.0, jnp.float32)]
    flat = None
    for place in range(owner_count - 1):
        after = []
        if place == owner_count - 2:
            packed = pack_share(share, group_tally, bests[-2:-1])
            centroids, centroid_unit = make_centroids(lax.all_gather(packed, "grp"), per_owner)
            after = [centroid_unit]
        best, flat = gram_step(rows, columns, bests[-1], flat, chunks[place], place * padded, after)
        bests.append(best)
    results = gram_step(
        rows, columns, bests[-1], flat, chunks[-1], (owner_count - 1) * padded, final=(centroid_unit, me, turns_of)
    )
    back = lax.all_to_all(results, "docs", split_axis=0, concat_axis=0, tiled=True)
    near, cosine = place_rows(starts, slots, back, per_owner)
    return (centroids, near.reshape(-1), cosine.reshape(-1))


def solution(mesh):
    placed = (P(("grp", "docs"), None), P(("grp", "docs")), P())
    return jax.shard_map(
        per_device,
        mesh=mesh,
        in_specs=placed,
        out_specs=(P("docs", None), P(("grp", "docs")), P(("grp", "docs"))),
        check_vma=False,
    )
```

```python
import functools

import jax
import jax.numpy as jnp
from jax import lax
from jax.experimental import pallas as pl
from jax.experimental.pallas import tpu as pltpu
from jax.sharding import PartitionSpec as P

epsilon = 1e-06
LANES = 128
SUBLANES = 8
MIB = 1024 * 1024
TILE = 512
in_vmem = pl.BlockSpec(memory_space=pltpu.VMEM)
in_smem = pl.BlockSpec(memory_space=pltpu.SMEM)
anywhere = pl.BlockSpec(memory_space=pl.ANY)
brief = pl.CostEstimate(flops=1000, bytes_accessed=1000, transcendentals=0)


def round_up(value, step):
    return -(-value // step) * step


def params(mib=44):
    return pltpu.CompilerParams(vmem_limit_bytes=mib * MIB)


def look_up(table_ref, index):
    lane = jnp.bitwise_and(index, LANES - 1)
    row = jnp.right_shift(index, 7)
    found = jnp.zeros(index.shape, jnp.int32)
    for part in range(table_ref.shape[0]):
        entries = jnp.broadcast_to(table_ref[part : part + 1, :], index.shape)
        found = jnp.where(row == part, jnp.take_along_axis(entries, lane, axis=1), found)
    return found


def rows_below(slots, bound):
    return jnp.sum((slots < bound).astype(jnp.float32)).astype(jnp.int32)


def plan_kernel(per_owner, limit, assign_ref, table_ref, slot_ref, start_ref):
    slots = look_up(table_ref, assign_ref[...])
    slot_ref[...] = slots
    for owner in range(start_ref.shape[0]):
        start_ref[owner] = jnp.minimum(rows_below(slots, owner * per_owner), limit)


def make_plan(assign_rows, table, owner_count, per_owner, limit):
    return pl.pallas_call(
        functools.partial(plan_kernel, per_owner, limit),
        out_shape=(
            jax.ShapeDtypeStruct(assign_rows.shape, jnp.int32),
            jax.ShapeDtypeStruct((owner_count,), jnp.int32),
        ),
        in_specs=[in_vmem, in_vmem],
        out_specs=(in_vmem, in_smem),
        compiler_params=params(8),
        name="plan",
    )(assign_rows, table)


def unit_kernel(steps, offset, turn, start_ref, me_ref, rows_ref, *refs):
    unit_ref, held, sem = refs[-3:]
    part = unit_ref.shape[0] // steps
    window = part + SUBLANES
    start = start_ref[lax.rem(me_ref[0] + turn, start_ref.shape[0])] + offset

    def first(step):
        return aligned_start(start + step * part, rows_ref.shape[0], window)

    copies = [
        pltpu.make_async_copy(rows_ref.at[pl.ds(first(step), window), :], held.at[step], sem.at[step])
        for step in range(steps)
    ]
    for copy in copies:
        copy.start()
    for step in range(steps):
        copies[step].wait()
        shift = start + step * part - first(step)
        groups = held[step].reshape(window // SUBLANES, SUBLANES, -1)
        turned = pltpu.roll(groups, SUBLANES - shift, 1)
        line = lax.broadcasted_iota(jnp.int32, (part // SUBLANES, SUBLANES, groups.shape[2]), 1)
        values = jnp.where(line < SUBLANES - shift, turned[:-1], turned[1:]).reshape(part, -1)
        scale = lax.rsqrt(jnp.sum(values * values, -1, keepdims=True) + epsilon)
        unit_ref[step * part : (step + 1) * part, :] = (values * scale).astype(jnp.bfloat16)


def unit_piece(starts, me, embeddings, turn, offset, rows, after):
    width = embeddings.shape[1]
    steps = rows // LANES if rows % LANES == 0 else 1
    return pl.pallas_call(
        functools.partial(unit_kernel, steps, offset, turn),
        out_shape=jax.ShapeDtypeStruct((rows, width), jnp.bfloat16),
        in_specs=[in_smem, in_smem, anywhere] + [anywhere] * len(after),
        out_specs=in_vmem,
        scratch_shapes=[
            pltpu.VMEM((steps, rows // steps + SUBLANES, width), jnp.float32),
            pltpu.SemaphoreType.DMA((steps,)),
        ],
        compiler_params=params(),
        cost_estimate=brief,
        name="unit",
    )(starts, me, embeddings, *after)


def hold_until(values, arrived, mib=8):
    def nothing(*refs):
        pass

    return pl.pallas_call(
        nothing,
        out_shape=jax.ShapeDtypeStruct(values.shape, values.dtype),
        in_specs=[anywhere] * (1 + len(arrived)),
        out_specs=anywhere,
        input_output_aliases={0: 0},
        compiler_params=params(mib),
        cost_estimate=brief,
        name="hold",
    )(values, *arrived)


def aligned_start(start, row_count, window):
    begin = jnp.minimum(jnp.left_shift(jnp.right_shift(start, 3), 3), row_count - window)
    return pl.multiple_of(begin, SUBLANES)


def flat_window(held, start, rows):
    span = round_up(rows + 1, SUBLANES)
    shift = jnp.bitwise_and(start, LANES - 1)
    block = held[pl.ds(jnp.right_shift(start, 7), span), :]
    turned = pltpu.roll(block, jnp.bitwise_and(LANES - shift, LANES - 1), 1)
    following = pltpu.roll(turned, span - 1, 0)
    lane = lax.broadcasted_iota(jnp.int32, block.shape, 1)
    return jnp.where(lane < LANES - shift, turned, following)


def window_labels(held, slots, owner, start, per_owner, capacity, blocks):
    low = owner * per_owner
    mine = (slots >= low) & (slots < low + per_owner)
    held[: slots.shape[0], :] = jnp.where(mine, slots - low, -1)
    labels = flat_window(held, start, blocks)
    place = lax.broadcasted_iota(jnp.int32, labels.shape, 0) * LANES + lax.broadcasted_iota(
        jnp.int32, labels.shape, 1
    )
    return jnp.where(place < capacity, labels, -1)


def summed_kernel(per_owner, capacity, start_ref, slot_ref, sum_ref, held):
    owner_count = sum_ref.shape[0]
    held[...] = jnp.full(held.shape, -1, jnp.int32)
    slots = slot_ref[...]
    window = capacity + SUBLANES
    wide = sum_ref.shape[1] // LANES
    for owner in range(owner_count):
        aligned = aligned_start(start_ref[owner], slots.size, window)
        labels = window_labels(held, slots, owner, aligned, per_owner, window, wide)
        for block in range(wide):
            sum_ref[owner : owner + 1, block * LANES : (block + 1) * LANES] = labels[block : block + 1, :]


def summed_labels(starts, slots, owner_count, per_owner, capacity):
    return pl.pallas_call(
        functools.partial(summed_kernel, per_owner, capacity),
        out_shape=jax.ShapeDtypeStruct((owner_count, round_up(capacity + SUBLANES, LANES)), jnp.int32),
        in_specs=[in_smem, in_vmem],
        out_specs=in_vmem,
        scratch_shapes=[pltpu.VMEM((slots.shape[0] + 2 * SUBLANES, LANES), jnp.int32)],
        compiler_params=params(8),
        name="summed",
    )(starts, slots)


def sent_kernel(per_owner, capacity, start_ref, slot_ref, after_ref, sent_ref, held):
    owner_count, span, _ = sent_ref.shape
    held[...] = jnp.full(held.shape, -1, jnp.int32)
    slots = slot_ref[...]
    for owner in range(owner_count):
        labels = window_labels(held, slots, owner, start_ref[owner], per_owner, capacity, span - 1)
        sent_ref[owner] = labels[:span, :]


def sent_labels(starts, slots, owner_count, per_owner, capacity, after):
    span = round_up(-(-capacity // LANES) + 1, SUBLANES)
    return pl.pallas_call(
        functools.partial(sent_kernel, per_owner, capacity),
        out_shape=jax.ShapeDtypeStruct((owner_count, span, LANES), jnp.int32),
        in_specs=[in_smem, in_vmem, anywhere],
        out_specs=in_vmem,
        scratch_shapes=[pltpu.VMEM((slots.shape[0] + 2 * SUBLANES, LANES), jnp.int32)],
        compiler_params=params(8),
        name="sent",
    )(starts, slots, after)


def arrived_kernel(blocks, turns_of, me_ref, got_ref, row_ref, column_ref, tally_ref):
    tally = jnp.zeros((LANES, LANES), jnp.float32)
    cluster = lax.broadcasted_iota(jnp.int32, tally.shape, 0)
    for place, turn in enumerate(turns_of):
        source = lax.rem(me_ref[0] + len(turns_of) - turn, len(turns_of))
        for block in range(blocks):
            line = place * blocks + block
            spread = jnp.broadcast_to(got_ref[source, block : block + 1, :], tally.shape)
            row_ref[line : line + 1, :] = spread[:1, :]
            column_ref[line * LANES : (line + 1) * LANES, :] = spread.T
            tally += (spread == cluster).astype(jnp.float32)
    total = jnp.broadcast_to(jnp.sum(tally, 1, keepdims=True), tally.shape)
    tally_ref[...] = jnp.zeros(tally_ref.shape, jnp.float32)
    tally_ref[:, :LANES] = total.T[:SUBLANES, :]


def arrived_labels(me, got, turns_of, blocks, width):
    lines = len(turns_of) * blocks
    return pl.pallas_call(
        functools.partial(arrived_kernel, blocks, turns_of),
        out_shape=(
            jax.ShapeDtypeStruct((lines, LANES), jnp.int32),
            jax.ShapeDtypeStruct((lines * LANES, LANES), jnp.int32),
            jax.ShapeDtypeStruct((SUBLANES, width), jnp.float32),
        ),
        in_specs=[in_smem, in_vmem],
        out_specs=(in_vmem, in_vmem, in_vmem),
        compiler_params=params(8),
        name="arrived",
    )(me, got)


def sum_kernel(start_ref, label_ref, rows_ref, *refs):
    sum_ref, held, sem = refs[-3:]
    owner_count, per_owner, _ = sum_ref.shape
    window = held.shape[1]

    def copy(owner, slot):
        first = aligned_start(start_ref[owner], rows_ref.shape[0], window)
        return pltpu.make_async_copy(rows_ref.at[pl.ds(first, window), :], held.at[slot], sem.at[slot])

    copy(0, 0).start()

    def body(owner, carry):
        slot = lax.rem(owner, 2)

        @pl.when(owner + 1 < owner_count)
        def _():
            copy(owner + 1, 1 - slot).start()

        copy(owner, slot).wait()
        labels = label_ref[pl.ds(owner, 1), :][:, :window]
        cluster = lax.broadcasted_iota(jnp.int32, (per_owner, window), 0)
        member = (labels == cluster).astype(jnp.float32).astype(jnp.bfloat16)
        values = held[slot]
        high = values.astype(jnp.bfloat16)
        rest = values - high.astype(jnp.float32)
        middle = rest.astype(jnp.bfloat16)
        low = (rest - middle.astype(jnp.float32)).astype(jnp.bfloat16)
        total = jnp.dot(member, high, preferred_element_type=jnp.float32)
        total += jnp.dot(member, middle, preferred_element_type=jnp.float32)
        total += jnp.dot(member, low, preferred_element_type=jnp.float32)
        sum_ref[pl.ds(owner, 1)] = total[None]
        return carry

    lax.fori_loop(0, owner_count, body, 0)


def slot_sums(starts, labels, embeddings, per_owner, capacity, after):
    owner_count = labels.shape[0]
    width = embeddings.shape[1]
    return pl.pallas_call(
        sum_kernel,
        out_shape=jax.ShapeDtypeStruct((owner_count, per_owner, width), jnp.float32),
        in_specs=[in_smem, in_vmem, anywhere] + [anywhere] * len(after),
        out_specs=in_vmem,
        scratch_shapes=[
            pltpu.VMEM((2, capacity + SUBLANES, width), jnp.float32),
            pltpu.SemaphoreType.DMA((2,)),
        ],
        compiler_params=params(),
        cost_estimate=pl.CostEstimate(
            flops=6 * owner_count * per_owner * capacity * width,
            bytes_accessed=4 * embeddings.size,
            transcendentals=0,
        ),
        name="sums",
    )(starts, labels, embeddings, *after)


def gram_kernel(begin, rows, wide, after_count, turns_of, *refs):
    chunk_ref, row_ref, column_ref, best_ref, *refs = refs
    flat_ref = centroid_ref = result_ref = None
    if begin:
        flat_ref, *refs = refs
    refs = refs[after_count:]
    if turns_of:
        centroid_ref, me_ref, result_ref, *refs, out_ref, cosine_ref = refs
    else:
        out_ref, flat_ref, *refs = refs
    mine, turned, labels, tiles, even, odd, best, sem, tile_sem = refs
    first = begin // LANES
    size = tiles.shape[2]
    count = -(-begin // size)

    def line_of(tile):
        return jnp.minimum(tile * (size // LANES), first - size // LANES)

    def fetch(tile):
        start = pl.multiple_of(line_of(tile) * LANES, LANES)
        slot = lax.rem(tile, 4)
        return pltpu.make_async_copy(flat_ref.at[:, pl.ds(start, size)], tiles.at[slot], tile_sem.at[slot])

    chunk_copy = pltpu.make_async_copy(chunk_ref, mine.at[pl.ds(0, rows), :], sem.at[0])
    label_copy = pltpu.make_async_copy(column_ref.at[pl.ds(begin, wide), :], labels, sem.at[1])
    chunk_copy.start()
    label_copy.start()
    for tile in range(min(count, 3)):
        fetch(jnp.int32(tile)).start()
    if rows < wide:
        mine[rows:wide, :] = jnp.zeros((wide - rows, mine.shape[1]), mine.dtype)
    if turns_of:
        mine[wide:, :] = centroid_ref[...]
        cosine_ref[...] = jnp.zeros(cosine_ref.shape, jnp.float32)
    out_ref[...] = best_ref[...]
    best[...] = jnp.full(best.shape, -2.0, jnp.float32)
    chunk_copy.wait()
    label_copy.wait()
    turned[...] = mine[:wide, :].T
    if not turns_of:
        flat_copy = pltpu.make_async_copy(turned, flat_ref.at[:, pl.ds(begin, wide)], sem.at[2])
        flat_copy.start()

    def products(right):
        return jnp.dot(mine[...], right, preferred_element_type=jnp.float32)

    halves = 2 if size % (4 * LANES) == 0 else 1

    def multiply(held, slot, half):
        here = slice(half * (size // halves), (half + 1) * (size // halves))
        held[:, here] = products(tiles[slot, :, here])

    def cosines(values, line):
        cluster = lax.broadcasted_iota(jnp.int32, values.shape, 0)
        own = jnp.where(row_ref[pl.ds(line, 1), :] == cluster, values, 0.0)
        cosine_ref[pl.ds(line, 1), :] = jnp.sum(own, 0, keepdims=True)

    def reduce_tile(held, tile, half):
        parts = range(half * (size // halves) // LANES, (half + 1) * (size // halves) // LANES)
        lines = {part: line_of(tile) + part for part in parts}
        tops = {part: jnp.full((SUBLANES, LANES), -2.0, jnp.float32) for part in parts}
        against = {
            part: jnp.broadcast_to(row_ref[pl.ds(lines[part], 1), :], (LANES, LANES)) for part in parts
        }
        for begin_row in range(0, wide, LANES):
            span = slice(begin_row, begin_row + LANES)
            own = labels[span, :]
            fold = best[span, :]
            for part in parts:
                near = jnp.where(own == against[part], held[span, part * LANES : (part + 1) * LANES], -2.0)
                fold = jnp.maximum(fold, near)
                tops[part] = jnp.maximum(tops[part], jnp.max(near.reshape(-1, SUBLANES, LANES), 0))
            best[span, :] = fold
        for part in parts:
            out_ref[pl.ds(lines[part], 1), :] = jnp.maximum(
                out_ref[pl.ds(lines[part], 1), :], jnp.max(tops[part], 0, keepdims=True)
            )
            if turns_of:
                cosines(held[wide:, part * LANES : (part + 1) * LANES], lines[part])

    if begin:
        fetch(jnp.int32(0)).wait()
        for half in range(halves):
            multiply(even, 0, half)

        def body(pair, carry):
            tile = pair * 2
            fetch(tile + 1).wait()

            @pl.when(tile + 3 < count)
            def _():
                fetch(tile + 3).start()

            for half in range(halves):
                multiply(odd, lax.rem(tile + 1, 4), half)
                reduce_tile(even, tile, half)
            fetch(tile + 2).wait()

            @pl.when(tile + 4 < count)
            def _():
                fetch(tile + 4).start()

            for half in range(halves):
                multiply(even, lax.rem(tile + 2, 4), half)
                reduce_tile(odd, tile + 1, half)
            return carry

        lax.fori_loop(0, (count - 1) // 2, body, 0)
        left = even
        if count % 2 == 0:
            left = odd
            fetch(jnp.int32(count - 1)).wait()
            for half in range(halves):
                multiply(odd, (count - 1) % 4, half)
                reduce_tile(even, jnp.int32(count - 2), half)
        for half in range(halves):
            reduce_tile(left, jnp.int32(count - 1), half)
    own = products(turned[...])
    row = lax.broadcasted_iota(jnp.int32, (wide, LANES), 0)
    column = lax.broadcasted_iota(jnp.int32, (wide, LANES), 1)
    for block in range(wide // LANES):
        line = first + block
        here = slice(block * LANES, (block + 1) * LANES)
        allowed = (labels[...] == row_ref[line : line + 1, :]) & (row != column + block * LANES)
        near = jnp.max(jnp.where(allowed, own[:wide, here], -2.0), 0, keepdims=True)
        other = jnp.max(best[here, :].T, 0, keepdims=True)
        out_ref[line : line + 1, :] = jnp.maximum(near, other)
        if turns_of:
            cosines(own[wide:, here], line)
    if turns_of:
        blocks = row_ref.shape[0] // len(turns_of)
        half = result_ref.shape[1] // 2
        result_ref[...] = jnp.zeros(result_ref.shape, jnp.float32)
        for place, turn in enumerate(turns_of):
            source = lax.rem(me_ref[0] + len(turns_of) - turn, len(turns_of))
            lines = slice(place * blocks, (place + 1) * blocks)
            result_ref[source, :blocks, :] = out_ref[lines, :]
            result_ref[source, half : half + blocks, :] = cosine_ref[lines, :]
    else:
        flat_copy.wait()


def gram_step(rows, columns, best, flat, chunk, begin, after=(), final=None):
    length, width = chunk.shape
    wide = round_up(length, LANES)
    tall = wide
    size = min(TILE, begin) if begin else LANES
    flat_shape = jax.ShapeDtypeStruct((width, columns.shape[0]), jnp.bfloat16)
    inputs = [chunk, rows, columns, best]
    in_specs = [anywhere, in_vmem, anywhere, in_vmem]
    aliases = {}
    if begin:
        if not final:
            aliases = {len(inputs): 1}
        inputs.append(flat)
        in_specs.append(anywhere)
    inputs += after
    in_specs += [anywhere] * len(after)
    out_shape = (jax.ShapeDtypeStruct(best.shape, jnp.float32), flat_shape)
    out_specs = (in_vmem, anywhere)
    turns_of = ()
    extra = []
    if final:
        centroid_unit, me, turns_of = final
        tall += centroid_unit.shape[0]
        inputs += [centroid_unit, me]
        in_specs += [in_vmem, in_smem]
        half = round_up(rows.shape[0] // len(turns_of) + 1, SUBLANES)
        out_shape = jax.ShapeDtypeStruct((len(turns_of), 2 * half, LANES), jnp.float32)
        out_specs = in_vmem
        extra = [pltpu.VMEM(best.shape, jnp.float32)] * 2
    return pl.pallas_call(
        functools.partial(gram_kernel, begin, length, wide, len(after), turns_of),
        out_shape=out_shape,
        in_specs=in_specs,
        out_specs=out_specs,
        scratch_shapes=[
            pltpu.VMEM((tall, width), jnp.bfloat16),
            pltpu.VMEM((width, wide), jnp.bfloat16),
            pltpu.VMEM((wide, LANES), jnp.int32),
            pltpu.VMEM((4, width, size), jnp.bfloat16),
            pltpu.VMEM((tall, size), jnp.float32),
            pltpu.VMEM((tall, size), jnp.float32),
            pltpu.VMEM((wide, LANES), jnp.float32),
            pltpu.SemaphoreType.DMA((3,)),
            pltpu.SemaphoreType.DMA((4,)),
        ]
        + extra,
        input_output_aliases=aliases,
        compiler_params=params(),
        cost_estimate=brief,
        name="gram",
    )(*inputs)


def pack_kernel(share_ref, tally_ref, *refs):
    packed_ref = refs[-1]
    packed_ref[: share_ref.shape[0], :] = share_ref[...]
    packed_ref[share_ref.shape[0] :, :] = tally_ref[...]


def pack_share(share, tally, after):
    length = share.shape[0] + tally.shape[0]
    return pl.pallas_call(
        pack_kernel,
        out_shape=jax.ShapeDtypeStruct((length, share.shape[1]), jnp.float32),
        in_specs=[in_vmem, in_vmem] + [anywhere] * len(after),
        out_specs=in_vmem,
        compiler_params=params(8),
        name="pack",
    )(share, tally, *after)


def centroid_kernel(gathered_ref, centroid_ref, unit_ref):
    groups, length, width = gathered_ref.shape
    share = length - SUBLANES
    per_owner = centroid_ref.shape[0]
    tally = jnp.sum(gathered_ref[:, share, :LANES], 0, keepdims=True)
    column = jnp.broadcast_to(tally, (LANES, LANES)).T[:per_owner, :]
    sums = jnp.concatenate([gathered_ref[group, :share, :] for group in range(groups)], 0)
    centroids = sums / jnp.concatenate([column] * (width // LANES), 1)
    centroid_ref[...] = centroids
    scale = lax.rsqrt(jnp.sum(centroids * centroids, -1, keepdims=True) + epsilon)
    unit_ref[...] = (centroids * scale).astype(jnp.bfloat16)


def make_centroids(gathered, per_owner):
    shape = (per_owner, gathered.shape[2])
    return pl.pallas_call(
        centroid_kernel,
        out_shape=(
            jax.ShapeDtypeStruct(shape, jnp.float32),
            jax.ShapeDtypeStruct(shape, jnp.bfloat16),
        ),
        in_specs=[in_vmem],
        out_specs=(in_vmem, in_vmem),
        compiler_params=params(8),
        name="centroids",
    )(gathered)


def place_kernel(per_owner, start_ref, slot_ref, back_ref, near_ref, cosine_ref, held, result):
    owner_count, double, _ = back_ref.shape
    span = double // 2
    rows = slot_ref.shape[0]
    held[...] = jnp.full(held.shape, -1, jnp.int32)
    held[:rows, :] = slot_ref[...]
    result[...] = jnp.zeros(result.shape, jnp.float32)
    lane = lax.broadcasted_iota(jnp.int32, (span, LANES), 1)
    for owner in range(owner_count):
        start = start_ref[owner]
        first = pl.ds(jnp.right_shift(start, 7), span)
        shift = jnp.bitwise_and(start, LANES - 1)
        slots = held[first, :]
        mine = (slots >= owner * per_owner) & (slots < (owner + 1) * per_owner)
        for kind in range(2):
            turned = pltpu.roll(back_ref[owner, kind * span : (kind + 1) * span, :], shift, 1)
            earlier = pltpu.roll(turned, 1, 0)
            moved = jnp.where(lane >= shift, turned, earlier)
            result[kind, first, :] = jnp.where(mine, moved, result[kind, first, :])
    near_ref[...] = result[0, :rows, :]
    cosine_ref[...] = result[1, :rows, :]


def place_rows(starts, slots, back, per_owner):
    span = back.shape[1] // 2
    rows = slots.shape[0]
    return pl.pallas_call(
        functools.partial(place_kernel, per_owner),
        out_shape=(jax.ShapeDtypeStruct(slots.shape, jnp.float32),) * 2,
        in_specs=[in_smem, in_vmem, in_vmem],
        out_specs=(in_vmem, in_vmem),
        scratch_shapes=[
            pltpu.VMEM((rows + span, LANES), jnp.int32),
            pltpu.VMEM((2, rows + span, LANES), jnp.float32),
        ],
        compiler_params=params(8),
        name="place",
    )(starts, slots, back)


def turns(count):
    order = sorted(range(count), key=lambda turn: (min(turn, count - turn), turn))
    if count == 8:
        order = [0, 1, 2, 3, 7, 6, 5, 4]
    return order


def per_device(embeddings, assign, cluster_slot):
    row_count, width = embeddings.shape
    owner_count = lax.axis_size("docs")
    per_owner = cluster_slot.shape[0] // owner_count
    capacity = row_count // owner_count + row_count // (4 * owner_count)
    padded = round_up(capacity, LANES)
    blocks = padded // LANES
    me = lax.axis_index("docs").astype(jnp.int32).reshape(1)
    turns_of = turns(owner_count)

    slots, starts = make_plan(
        assign.reshape(-1, LANES), cluster_slot.reshape(-1, LANES), owner_count, per_owner, row_count - capacity
    )

    sent = []
    for place, turn in enumerate(turns_of):
        sent.append(unit_piece(starts, me, embeddings, turn, 0, capacity, sent[-1:] if place > 1 else []))

    def travel(place, piece):
        turn = turns_of[place]
        return lax.ppermute(piece, "docs", [(i, (i + turn) % owner_count) for i in range(owner_count)])

    chunks = [sent[0]] + [travel(place, sent[place]) for place in (1, 2, 3)]
    sum_labels = summed_labels(starts, slots, owner_count, per_owner, capacity)
    partial_sums = slot_sums(starts, sum_labels, embeddings, per_owner, capacity, sent[1:8])
    partial_sums = hold_until(partial_sums, chunks[1:3], 62)
    wire_labels = sent_labels(starts, slots, owner_count, per_owner, capacity, sent[7])
    wire_labels = hold_until(wire_labels, chunks[1:3])
    got_labels = lax.all_to_all(wire_labels, "docs", split_axis=0, concat_axis=0, tiled=True)
    rows, columns, group_tally = arrived_labels(me, got_labels, turns_of, blocks, width)
    group_share = lax.psum_scatter(partial_sums, "grp", scatter_dimension=1, tiled=True)
    group_share = hold_until(group_share, [chunks[3], got_labels])
    share = lax.psum_scatter(group_share, "docs", scatter_dimension=0, tiled=True)[0]
    for place in range(4, owner_count):
        after = [chunks[4]] if place == owner_count - 1 else [chunks[3], got_labels]
        chunks.append(travel(place, hold_until(sent[place], after)))

    bests = [jnp.full((owner_count * blocks, LANES), -2.0, jnp.float32)]
    flat = None
    for place in range(owner_count - 1):
        after = []
        if place == owner_count - 2:
            packed = pack_share(share, group_tally, bests[-2:-1])
            centroids, centroid_unit = make_centroids(lax.all_gather(packed, "grp"), per_owner)
            after = [centroid_unit]
        best, flat = gram_step(rows, columns, bests[-1], flat, chunks[place], place * padded, after)
        bests.append(best)
    results = gram_step(
        rows, columns, bests[-1], flat, chunks[-1], (owner_count - 1) * padded, final=(centroid_unit, me, turns_of)
    )
    back = lax.all_to_all(results, "docs", split_axis=0, concat_axis=0, tiled=True)
    near, cosine = place_rows(starts, slots, back, per_owner)
    return (centroids, near.reshape(-1), cosine.reshape(-1))


def solution(mesh):
    placed = (P(("grp", "docs"), None), P(("grp", "docs")), P())
    return jax.shard_map(
        per_device,
        mesh=mesh,
        in_specs=placed,
        out_specs=(P("docs", None), P(("grp", "docs")), P(("grp", "docs"))),
        check_vma=False,
    )
```

```python
import functools

import jax
import jax.numpy as jnp
from jax import lax
from jax.experimental import pallas as pl
from jax.experimental.pallas import tpu as pltpu
from jax.sharding import PartitionSpec as P

epsilon = 1e-06
LANES = 128
SUBLANES = 8
MIB = 1024 * 1024
TILE = 512
in_vmem = pl.BlockSpec(memory_space=pltpu.VMEM)
in_smem = pl.BlockSpec(memory_space=pltpu.SMEM)
anywhere = pl.BlockSpec(memory_space=pl.ANY)
brief = pl.CostEstimate(flops=1000, bytes_accessed=1000, transcendentals=0)


def round_up(value, step):
    return -(-value // step) * step


def params(mib=44):
    return pltpu.CompilerParams(vmem_limit_bytes=mib * MIB)


def look_up(table_ref, index):
    lane = jnp.bitwise_and(index, LANES - 1)
    row = jnp.right_shift(index, 7)
    found = jnp.zeros(index.shape, jnp.int32)
    for part in range(table_ref.shape[0]):
        entries = jnp.broadcast_to(table_ref[part : part + 1, :], index.shape)
        found = jnp.where(row == part, jnp.take_along_axis(entries, lane, axis=1), found)
    return found


def rows_below(slots, bound):
    return jnp.sum((slots < bound).astype(jnp.float32)).astype(jnp.int32)


def plan_kernel(per_owner, limit, assign_ref, table_ref, slot_ref, start_ref):
    slots = look_up(table_ref, assign_ref[...])
    slot_ref[...] = slots
    for owner in range(start_ref.shape[0]):
        start_ref[owner] = jnp.minimum(rows_below(slots, owner * per_owner), limit)


def make_plan(assign_rows, table, owner_count, per_owner, limit):
    return pl.pallas_call(
        functools.partial(plan_kernel, per_owner, limit),
        out_shape=(
            jax.ShapeDtypeStruct(assign_rows.shape, jnp.int32),
            jax.ShapeDtypeStruct((owner_count,), jnp.int32),
        ),
        in_specs=[in_vmem, in_vmem],
        out_specs=(in_vmem, in_smem),
        compiler_params=params(8),
        name="plan",
    )(assign_rows, table)


def unit_kernel(steps, offset, turn, start_ref, me_ref, rows_ref, *refs):
    unit_ref, held, sem = refs[-3:]
    part = unit_ref.shape[0] // steps
    window = part + SUBLANES
    start = start_ref[lax.rem(me_ref[0] + turn, start_ref.shape[0])] + offset

    def first(step):
        return aligned_start(start + step * part, rows_ref.shape[0], window)

    copies = [
        pltpu.make_async_copy(rows_ref.at[pl.ds(first(step), window), :], held.at[step], sem.at[step])
        for step in range(steps)
    ]
    for copy in copies:
        copy.start()
    for step in range(steps):
        copies[step].wait()
        shift = start + step * part - first(step)
        groups = held[step].reshape(window // SUBLANES, SUBLANES, -1)
        turned = pltpu.roll(groups, SUBLANES - shift, 1)
        line = lax.broadcasted_iota(jnp.int32, (part // SUBLANES, SUBLANES, groups.shape[2]), 1)
        values = jnp.where(line < SUBLANES - shift, turned[:-1], turned[1:]).reshape(part, -1)
        scale = lax.rsqrt(jnp.sum(values * values, -1, keepdims=True) + epsilon)
        unit_ref[step * part : (step + 1) * part, :] = (values * scale).astype(jnp.bfloat16)


def unit_piece(starts, me, embeddings, turn, offset, rows, after):
    width = embeddings.shape[1]
    steps = rows // LANES if rows % LANES == 0 else 1
    return pl.pallas_call(
        functools.partial(unit_kernel, steps, offset, turn),
        out_shape=jax.ShapeDtypeStruct((rows, width), jnp.bfloat16),
        in_specs=[in_smem, in_smem, anywhere] + [anywhere] * len(after),
        out_specs=in_vmem,
        scratch_shapes=[
            pltpu.VMEM((steps, rows // steps + SUBLANES, width), jnp.float32),
            pltpu.SemaphoreType.DMA((steps,)),
        ],
        compiler_params=params(),
        cost_estimate=brief,
        name="unit",
    )(starts, me, embeddings, *after)


def hold_until(values, arrived, mib=8):
    def nothing(*refs):
        pass

    return pl.pallas_call(
        nothing,
        out_shape=jax.ShapeDtypeStruct(values.shape, values.dtype),
        in_specs=[anywhere] * (1 + len(arrived)),
        out_specs=anywhere,
        input_output_aliases={0: 0},
        compiler_params=params(mib),
        cost_estimate=brief,
        name="hold",
    )(values, *arrived)


def aligned_start(start, row_count, window):
    begin = jnp.minimum(jnp.left_shift(jnp.right_shift(start, 3), 3), row_count - window)
    return pl.multiple_of(begin, SUBLANES)


def flat_window(held, start, rows):
    span = round_up(rows + 1, SUBLANES)
    shift = jnp.bitwise_and(start, LANES - 1)
    block = held[pl.ds(jnp.right_shift(start, 7), span), :]
    turned = pltpu.roll(block, jnp.bitwise_and(LANES - shift, LANES - 1), 1)
    following = pltpu.roll(turned, span - 1, 0)
    lane = lax.broadcasted_iota(jnp.int32, block.shape, 1)
    return jnp.where(lane < LANES - shift, turned, following)


def window_labels(held, slots, owner, start, per_owner, capacity, blocks):
    low = owner * per_owner
    mine = (slots >= low) & (slots < low + per_owner)
    held[: slots.shape[0], :] = jnp.where(mine, slots - low, -1)
    labels = flat_window(held, start, blocks)
    place = lax.broadcasted_iota(jnp.int32, labels.shape, 0) * LANES + lax.broadcasted_iota(
        jnp.int32, labels.shape, 1
    )
    return jnp.where(place < capacity, labels, -1)


def summed_kernel(per_owner, capacity, start_ref, slot_ref, sum_ref, held):
    owner_count = sum_ref.shape[0]
    held[...] = jnp.full(held.shape, -1, jnp.int32)
    slots = slot_ref[...]
    window = capacity + SUBLANES
    wide = sum_ref.shape[1] // LANES
    for owner in range(owner_count):
        aligned = aligned_start(start_ref[owner], slots.size, window)
        labels = window_labels(held, slots, owner, aligned, per_owner, window, wide)
        for block in range(wide):
            sum_ref[owner : owner + 1, block * LANES : (block + 1) * LANES] = labels[block : block + 1, :]


def summed_labels(starts, slots, owner_count, per_owner, capacity):
    return pl.pallas_call(
        functools.partial(summed_kernel, per_owner, capacity),
        out_shape=jax.ShapeDtypeStruct((owner_count, round_up(capacity + SUBLANES, LANES)), jnp.int32),
        in_specs=[in_smem, in_vmem],
        out_specs=in_vmem,
        scratch_shapes=[pltpu.VMEM((slots.shape[0] + 2 * SUBLANES, LANES), jnp.int32)],
        compiler_params=params(8),
        name="summed",
    )(starts, slots)


def sent_kernel(per_owner, capacity, start_ref, slot_ref, after_ref, sent_ref, held):
    owner_count, span, _ = sent_ref.shape
    held[...] = jnp.full(held.shape, -1, jnp.int32)
    slots = slot_ref[...]
    for owner in range(owner_count):
        labels = window_labels(held, slots, owner, start_ref[owner], per_owner, capacity, span - 1)
        sent_ref[owner] = labels[:span, :]


def sent_labels(starts, slots, owner_count, per_owner, capacity, after):
    span = round_up(-(-capacity // LANES) + 1, SUBLANES)
    return pl.pallas_call(
        functools.partial(sent_kernel, per_owner, capacity),
        out_shape=jax.ShapeDtypeStruct((owner_count, span, LANES), jnp.int32),
        in_specs=[in_smem, in_vmem, anywhere],
        out_specs=in_vmem,
        scratch_shapes=[pltpu.VMEM((slots.shape[0] + 2 * SUBLANES, LANES), jnp.int32)],
        compiler_params=params(8),
        name="sent",
    )(starts, slots, after)


def arrived_kernel(blocks, turns_of, me_ref, got_ref, row_ref, column_ref, tally_ref):
    tally = jnp.zeros((LANES, LANES), jnp.float32)
    cluster = lax.broadcasted_iota(jnp.int32, tally.shape, 0)
    for place, turn in enumerate(turns_of):
        source = lax.rem(me_ref[0] + len(turns_of) - turn, len(turns_of))
        for block in range(blocks):
            line = place * blocks + block
            spread = jnp.broadcast_to(got_ref[source, block : block + 1, :], tally.shape)
            row_ref[line : line + 1, :] = spread[:1, :]
            column_ref[line * LANES : (line + 1) * LANES, :] = spread.T
            tally += (spread == cluster).astype(jnp.float32)
    total = jnp.broadcast_to(jnp.sum(tally, 1, keepdims=True), tally.shape)
    tally_ref[...] = jnp.zeros(tally_ref.shape, jnp.float32)
    tally_ref[:, :LANES] = total.T[:SUBLANES, :]


def arrived_labels(me, got, turns_of, blocks, width):
    lines = len(turns_of) * blocks
    return pl.pallas_call(
        functools.partial(arrived_kernel, blocks, turns_of),
        out_shape=(
            jax.ShapeDtypeStruct((lines, LANES), jnp.int32),
            jax.ShapeDtypeStruct((lines * LANES, LANES), jnp.int32),
            jax.ShapeDtypeStruct((SUBLANES, width), jnp.float32),
        ),
        in_specs=[in_smem, in_vmem],
        out_specs=(in_vmem, in_vmem, in_vmem),
        compiler_params=params(8),
        name="arrived",
    )(me, got)


def sum_kernel(start_ref, label_ref, rows_ref, *refs):
    sum_ref, held, sem = refs[-3:]
    owner_count, per_owner, _ = sum_ref.shape
    window = held.shape[1]

    def copy(owner, slot):
        first = aligned_start(start_ref[owner], rows_ref.shape[0], window)
        return pltpu.make_async_copy(rows_ref.at[pl.ds(first, window), :], held.at[slot], sem.at[slot])

    copy(0, 0).start()

    def body(owner, carry):
        slot = lax.rem(owner, 2)

        @pl.when(owner + 1 < owner_count)
        def _():
            copy(owner + 1, 1 - slot).start()

        copy(owner, slot).wait()
        labels = label_ref[pl.ds(owner, 1), :][:, :window]
        cluster = lax.broadcasted_iota(jnp.int32, (per_owner, window), 0)
        member = (labels == cluster).astype(jnp.float32).astype(jnp.bfloat16)
        values = held[slot]
        high = values.astype(jnp.bfloat16)
        rest = values - high.astype(jnp.float32)
        middle = rest.astype(jnp.bfloat16)
        low = (rest - middle.astype(jnp.float32)).astype(jnp.bfloat16)
        total = jnp.dot(member, high, preferred_element_type=jnp.float32)
        total += jnp.dot(member, middle, preferred_element_type=jnp.float32)
        total += jnp.dot(member, low, preferred_element_type=jnp.float32)
        sum_ref[pl.ds(owner, 1)] = total[None]
        return carry

    lax.fori_loop(0, owner_count, body, 0)


def slot_sums(starts, labels, embeddings, per_owner, capacity, after):
    owner_count = labels.shape[0]
    width = embeddings.shape[1]
    return pl.pallas_call(
        sum_kernel,
        out_shape=jax.ShapeDtypeStruct((owner_count, per_owner, width), jnp.float32),
        in_specs=[in_smem, in_vmem, anywhere] + [anywhere] * len(after),
        out_specs=in_vmem,
        scratch_shapes=[
            pltpu.VMEM((2, capacity + SUBLANES, width), jnp.float32),
            pltpu.SemaphoreType.DMA((2,)),
        ],
        compiler_params=params(),
        cost_estimate=pl.CostEstimate(
            flops=6 * owner_count * per_owner * capacity * width,
            bytes_accessed=4 * embeddings.size,
            transcendentals=0,
        ),
        name="sums",
    )(starts, labels, embeddings, *after)


def gram_kernel(begin, rows, wide, after_count, turns_of, *refs):
    chunk_ref, row_ref, column_ref, best_ref, *refs = refs
    flat_ref = centroid_ref = result_ref = None
    if begin:
        flat_ref, *refs = refs
    refs = refs[after_count:]
    if turns_of:
        centroid_ref, me_ref, result_ref, *refs, out_ref, cosine_ref = refs
    else:
        out_ref, flat_ref, *refs = refs
    mine, turned, labels, tiles, even, odd, best, sem, tile_sem = refs
    first = begin // LANES
    size = tiles.shape[2]
    count = -(-begin // size)

    def line_of(tile):
        return jnp.minimum(tile * (size // LANES), first - size // LANES)

    def fetch(tile):
        start = pl.multiple_of(line_of(tile) * LANES, LANES)
        slot = lax.rem(tile, 4)
        return pltpu.make_async_copy(flat_ref.at[:, pl.ds(start, size)], tiles.at[slot], tile_sem.at[slot])

    chunk_copy = pltpu.make_async_copy(chunk_ref, mine.at[pl.ds(0, rows), :], sem.at[0])
    label_copy = pltpu.make_async_copy(column_ref.at[pl.ds(begin, wide), :], labels, sem.at[1])
    chunk_copy.start()
    label_copy.start()
    for tile in range(min(count, 3)):
        fetch(jnp.int32(tile)).start()
    if rows < wide:
        mine[rows:wide, :] = jnp.zeros((wide - rows, mine.shape[1]), mine.dtype)
    if turns_of:
        mine[wide:, :] = centroid_ref[...]
        cosine_ref[...] = jnp.zeros(cosine_ref.shape, jnp.float32)
    out_ref[...] = best_ref[...]
    best[...] = jnp.full(best.shape, -2.0, jnp.float32)
    chunk_copy.wait()
    label_copy.wait()
    turned[...] = mine[:wide, :].T
    if not turns_of:
        flat_copy = pltpu.make_async_copy(turned, flat_ref.at[:, pl.ds(begin, wide)], sem.at[2])
        flat_copy.start()

    def products(right):
        return jnp.dot(mine[...], right, preferred_element_type=jnp.float32)

    halves = 2 if size % (4 * LANES) == 0 else 1

    def multiply(held, slot, half):
        here = slice(half * (size // halves), (half + 1) * (size // halves))
        held[:, here] = products(tiles[slot, :, here])

    def cosines(values, line):
        cluster = lax.broadcasted_iota(jnp.int32, values.shape, 0)
        own = jnp.where(row_ref[pl.ds(line, 1), :] == cluster, values, 0.0)
        cosine_ref[pl.ds(line, 1), :] = jnp.sum(own, 0, keepdims=True)

    def reduce_tile(held, tile, half):
        parts = range(half * (size // halves) // LANES, (half + 1) * (size // halves) // LANES)
        lines = {part: line_of(tile) + part for part in parts}
        tops = {part: jnp.full((SUBLANES, LANES), -2.0, jnp.float32) for part in parts}
        against = {
            part: jnp.broadcast_to(row_ref[pl.ds(lines[part], 1), :], (LANES, LANES)) for part in parts
        }
        for begin_row in range(0, wide, LANES):
            span = slice(begin_row, begin_row + LANES)
            own = labels[span, :]
            fold = best[span, :]
            for part in parts:
                near = jnp.where(own == against[part], held[span, part * LANES : (part + 1) * LANES], -2.0)
                fold = jnp.maximum(fold, near)
                tops[part] = jnp.maximum(tops[part], jnp.max(near.reshape(-1, SUBLANES, LANES), 0))
            best[span, :] = fold
        for part in parts:
            out_ref[pl.ds(lines[part], 1), :] = jnp.maximum(
                out_ref[pl.ds(lines[part], 1), :], jnp.max(tops[part], 0, keepdims=True)
            )
            if turns_of:
                cosines(held[wide:, part * LANES : (part + 1) * LANES], lines[part])

    if begin:
        fetch(jnp.int32(0)).wait()
        for half in range(halves):
            multiply(even, 0, half)

        def body(pair, carry):
            tile = pair * 2
            fetch(tile + 1).wait()

            @pl.when(tile + 3 < count)
            def _():
                fetch(tile + 3).start()

            for half in range(halves):
                multiply(odd, lax.rem(tile + 1, 4), half)
                reduce_tile(even, tile, half)
            fetch(tile + 2).wait()

            @pl.when(tile + 4 < count)
            def _():
                fetch(tile + 4).start()

            for half in range(halves):
                multiply(even, lax.rem(tile + 2, 4), half)
                reduce_tile(odd, tile + 1, half)
            return carry

        lax.fori_loop(0, (count - 1) // 2, body, 0)
        left = even
        if count % 2 == 0:
            left = odd
            fetch(jnp.int32(count - 1)).wait()
            for half in range(halves):
                multiply(odd, (count - 1) % 4, half)
                reduce_tile(even, jnp.int32(count - 2), half)
        for half in range(halves):
            reduce_tile(left, jnp.int32(count - 1), half)
    own = products(turned[...])
    row = lax.broadcasted_iota(jnp.int32, (wide, LANES), 0)
    column = lax.broadcasted_iota(jnp.int32, (wide, LANES), 1)
    for block in range(wide // LANES):
        line = first + block
        here = slice(block * LANES, (block + 1) * LANES)
        allowed = (labels[...] == row_ref[line : line + 1, :]) & (row != column + block * LANES)
        near = jnp.max(jnp.where(allowed, own[:wide, here], -2.0), 0, keepdims=True)
        other = jnp.max(best[here, :].T, 0, keepdims=True)
        out_ref[line : line + 1, :] = jnp.maximum(near, other)
        if turns_of:
            cosines(own[wide:, here], line)
    if turns_of:
        blocks = row_ref.shape[0] // len(turns_of)
        half = result_ref.shape[1] // 2
        result_ref[...] = jnp.zeros(result_ref.shape, jnp.float32)
        for place, turn in enumerate(turns_of):
            source = lax.rem(me_ref[0] + len(turns_of) - turn, len(turns_of))
            lines = slice(place * blocks, (place + 1) * blocks)
            result_ref[source, :blocks, :] = out_ref[lines, :]
            result_ref[source, half : half + blocks, :] = cosine_ref[lines, :]
    else:
        flat_copy.wait()


def gram_step(rows, columns, best, flat, chunk, begin, after=(), final=None):
    length, width = chunk.shape
    wide = round_up(length, LANES)
    tall = wide
    size = min(TILE, begin) if begin else LANES
    flat_shape = jax.ShapeDtypeStruct((width, columns.shape[0]), jnp.bfloat16)
    inputs = [chunk, rows, columns, best]
    in_specs = [anywhere, in_vmem, anywhere, in_vmem]
    aliases = {}
    if begin:
        if not final:
            aliases = {len(inputs): 1}
        inputs.append(flat)
        in_specs.append(anywhere)
    inputs += after
    in_specs += [anywhere] * len(after)
    out_shape = (jax.ShapeDtypeStruct(best.shape, jnp.float32), flat_shape)
    out_specs = (in_vmem, anywhere)
    turns_of = ()
    extra = []
    if final:
        centroid_unit, me, turns_of = final
        tall += centroid_unit.shape[0]
        inputs += [centroid_unit, me]
        in_specs += [in_vmem, in_smem]
        half = round_up(rows.shape[0] // len(turns_of) + 1, SUBLANES)
        out_shape = jax.ShapeDtypeStruct((len(turns_of), 2 * half, LANES), jnp.float32)
        out_specs = in_vmem
        extra = [pltpu.VMEM(best.shape, jnp.float32)] * 2
    return pl.pallas_call(
        functools.partial(gram_kernel, begin, length, wide, len(after), turns_of),
        out_shape=out_shape,
        in_specs=in_specs,
        out_specs=out_specs,
        scratch_shapes=[
            pltpu.VMEM((tall, width), jnp.bfloat16),
            pltpu.VMEM((width, wide), jnp.bfloat16),
            pltpu.VMEM((wide, LANES), jnp.int32),
            pltpu.VMEM((4, width, size), jnp.bfloat16),
            pltpu.VMEM((tall, size), jnp.float32),
            pltpu.VMEM((tall, size), jnp.float32),
            pltpu.VMEM((wide, LANES), jnp.float32),
            pltpu.SemaphoreType.DMA((3,)),
            pltpu.SemaphoreType.DMA((4,)),
        ]
        + extra,
        input_output_aliases=aliases,
        compiler_params=params(),
        cost_estimate=brief,
        name="gram",
    )(*inputs)


def pack_kernel(share_ref, tally_ref, *refs):
    packed_ref = refs[-1]
    packed_ref[: share_ref.shape[0], :] = share_ref[...]
    packed_ref[share_ref.shape[0] :, :] = tally_ref[...]


def pack_share(share, tally, after):
    length = share.shape[0] + tally.shape[0]
    return pl.pallas_call(
        pack_kernel,
        out_shape=jax.ShapeDtypeStruct((length, share.shape[1]), jnp.float32),
        in_specs=[in_vmem, in_vmem] + [anywhere] * len(after),
        out_specs=in_vmem,
        compiler_params=params(8),
        name="pack",
    )(share, tally, *after)


def centroid_kernel(gathered_ref, centroid_ref, unit_ref):
    groups, length, width = gathered_ref.shape
    share = length - SUBLANES
    per_owner = centroid_ref.shape[0]
    tally = jnp.sum(gathered_ref[:, share, :LANES], 0, keepdims=True)
    column = jnp.broadcast_to(tally, (LANES, LANES)).T[:per_owner, :]
    sums = jnp.concatenate([gathered_ref[group, :share, :] for group in range(groups)], 0)
    centroids = sums / jnp.concatenate([column] * (width // LANES), 1)
    centroid_ref[...] = centroids
    scale = lax.rsqrt(jnp.sum(centroids * centroids, -1, keepdims=True) + epsilon)
    unit_ref[...] = (centroids * scale).astype(jnp.bfloat16)


def make_centroids(gathered, per_owner):
    shape = (per_owner, gathered.shape[2])
    return pl.pallas_call(
        centroid_kernel,
        out_shape=(
            jax.ShapeDtypeStruct(shape, jnp.float32),
            jax.ShapeDtypeStruct(shape, jnp.bfloat16),
        ),
        in_specs=[in_vmem],
        out_specs=(in_vmem, in_vmem),
        compiler_params=params(8),
        name="centroids",
    )(gathered)


def place_kernel(per_owner, start_ref, slot_ref, back_ref, near_ref, cosine_ref, held, result):
    owner_count, double, _ = back_ref.shape
    span = double // 2
    rows = slot_ref.shape[0]
    held[...] = jnp.full(held.shape, -1, jnp.int32)
    held[:rows, :] = slot_ref[...]
    result[...] = jnp.zeros(result.shape, jnp.float32)
    lane = lax.broadcasted_iota(jnp.int32, (span, LANES), 1)
    for owner in range(owner_count):
        start = start_ref[owner]
        first = pl.ds(jnp.right_shift(start, 7), span)
        shift = jnp.bitwise_and(start, LANES - 1)
        slots = held[first, :]
        mine = (slots >= owner * per_owner) & (slots < (owner + 1) * per_owner)
        for kind in range(2):
            turned = pltpu.roll(back_ref[owner, kind * span : (kind + 1) * span, :], shift, 1)
            earlier = pltpu.roll(turned, 1, 0)
            moved = jnp.where(lane >= shift, turned, earlier)
            result[kind, first, :] = jnp.where(mine, moved, result[kind, first, :])
    near_ref[...] = result[0, :rows, :]
    cosine_ref[...] = result[1, :rows, :]


def place_rows(starts, slots, back, per_owner):
    span = back.shape[1] // 2
    rows = slots.shape[0]
    return pl.pallas_call(
        functools.partial(place_kernel, per_owner),
        out_shape=(jax.ShapeDtypeStruct(slots.shape, jnp.float32),) * 2,
        in_specs=[in_smem, in_vmem, in_vmem],
        out_specs=(in_vmem, in_vmem),
        scratch_shapes=[
            pltpu.VMEM((rows + span, LANES), jnp.int32),
            pltpu.VMEM((2, rows + span, LANES), jnp.float32),
        ],
        compiler_params=params(8),
        name="place",
    )(starts, slots, back)


def turns(count):
    order = sorted(range(count), key=lambda turn: (min(turn, count - turn), turn))
    if count == 8:
        order = [0, 1, 2, 3, 7, 6, 5, 4]
    return order


def per_device(embeddings, assign, cluster_slot):
    row_count, width = embeddings.shape
    owner_count = lax.axis_size("docs")
    per_owner = cluster_slot.shape[0] // owner_count
    capacity = row_count // owner_count + row_count // (4 * owner_count)
    padded = round_up(capacity, LANES)
    blocks = padded // LANES
    me = lax.axis_index("docs").astype(jnp.int32).reshape(1)
    turns_of = turns(owner_count)

    slots, starts = make_plan(
        assign.reshape(-1, LANES), cluster_slot.reshape(-1, LANES), owner_count, per_owner, row_count - capacity
    )

    last = owner_count - 1
    cuts = [0, 2 * LANES, capacity] if capacity == padded and blocks > 4 else [0, capacity]
    parts = [(low, high - low) for low, high in zip(cuts, cuts[1:])]
    sent = []
    for place, turn in enumerate(turns_of):
        for low, length in parts if place == last else [(0, capacity)]:
            sent.append(unit_piece(starts, me, embeddings, turn, low, length, sent[-1:] if place > 1 else []))

    def travel(place, piece):
        turn = turns_of[place]
        return lax.ppermute(piece, "docs", [(i, (i + turn) % owner_count) for i in range(owner_count)])

    chunks = [sent[0]] + [travel(place, sent[place]) for place in (1, 2, 3)]
    sum_labels = summed_labels(starts, slots, owner_count, per_owner, capacity)
    partial_sums = slot_sums(starts, sum_labels, embeddings, per_owner, capacity, sent[1:9])
    partial_sums = hold_until(partial_sums, chunks[1:3], 62)
    wire_labels = sent_labels(starts, slots, owner_count, per_owner, capacity, sent[7])
    wire_labels = hold_until(wire_labels, chunks[1:3])
    got_labels = lax.all_to_all(wire_labels, "docs", split_axis=0, concat_axis=0, tiled=True)
    rows, columns, group_tally = arrived_labels(me, got_labels, turns_of, blocks, width)
    group_share = lax.psum_scatter(partial_sums, "grp", scatter_dimension=1, tiled=True)
    group_share = hold_until(group_share, [chunks[3], got_labels])
    share = lax.psum_scatter(group_share, "docs", scatter_dimension=0, tiled=True)[0]
    for place in range(4, last):
        chunks.append(travel(place, hold_until(sent[place], [chunks[3], got_labels])))

    bests = [jnp.full((owner_count * blocks, LANES), -2.0, jnp.float32)]
    flat = None
    for place in range(last):
        after = []
        if place == 4:
            ends = [travel(last, hold_until(piece, [chunks[last - 2], bests[-1]])) for piece in sent[last:]]
        if place == last - 1:
            packed = pack_share(share, group_tally, bests[-2:-1])
            centroids, centroid_unit = make_centroids(lax.all_gather(packed, "grp"), per_owner)
            after = [centroid_unit]
        best, flat = gram_step(rows, columns, bests[-1], flat, chunks[place], place * padded, after)
        bests.append(best)
    for (low, _), chunk in zip(parts[:-1], ends):
        best, flat = gram_step(rows, columns, bests[-1], flat, chunk, last * padded + low)
        bests.append(best)
    results = gram_step(
        rows, columns, bests[-1], flat, ends[-1], last * padded + cuts[-2], final=(centroid_unit, me, turns_of)
    )
    back = lax.all_to_all(results, "docs", split_axis=0, concat_axis=0, tiled=True)
    near, cosine = place_rows(starts, slots, back, per_owner)
    return (centroids, near.reshape(-1), cosine.reshape(-1))


def solution(mesh):
    placed = (P(("grp", "docs"), None), P(("grp", "docs")), P())
    return jax.shard_map(
        per_device,
        mesh=mesh,
        in_specs=placed,
        out_specs=(P("docs", None), P(("grp", "docs")), P(("grp", "docs"))),
        check_vma=False,
    )
```

```python
import functools

import jax
import jax.numpy as jnp
from jax import lax
from jax.experimental import pallas as pl
from jax.experimental.pallas import tpu as pltpu
from jax.sharding import PartitionSpec as P

epsilon = 1e-06
LANES = 128
SUBLANES = 8
MIB = 1024 * 1024
TILE = 768
in_vmem = pl.BlockSpec(memory_space=pltpu.VMEM)
in_smem = pl.BlockSpec(memory_space=pltpu.SMEM)
anywhere = pl.BlockSpec(memory_space=pl.ANY)
brief = pl.CostEstimate(flops=1000, bytes_accessed=1000, transcendentals=0)


def round_up(value, step):
    return -(-value // step) * step


def params(mib=44):
    return pltpu.CompilerParams(vmem_limit_bytes=mib * MIB)


def look_up(table_ref, index):
    lane = jnp.bitwise_and(index, LANES - 1)
    row = jnp.right_shift(index, 7)
    found = jnp.zeros(index.shape, jnp.int32)
    for part in range(table_ref.shape[0]):
        entries = jnp.broadcast_to(table_ref[part : part + 1, :], index.shape)
        found = jnp.where(row == part, jnp.take_along_axis(entries, lane, axis=1), found)
    return found


def rows_below(slots, bound):
    return jnp.sum((slots < bound).astype(jnp.float32)).astype(jnp.int32)


def plan_kernel(per_owner, limit, assign_ref, table_ref, slot_ref, start_ref):
    slots = look_up(table_ref, assign_ref[...])
    slot_ref[...] = slots
    for owner in range(start_ref.shape[0]):
        start_ref[owner] = jnp.minimum(rows_below(slots, owner * per_owner), limit)


def make_plan(assign_rows, table, owner_count, per_owner, limit):
    return pl.pallas_call(
        functools.partial(plan_kernel, per_owner, limit),
        out_shape=(
            jax.ShapeDtypeStruct(assign_rows.shape, jnp.int32),
            jax.ShapeDtypeStruct((owner_count,), jnp.int32),
        ),
        in_specs=[in_vmem, in_vmem],
        out_specs=(in_vmem, in_smem),
        compiler_params=params(8),
        name="plan",
    )(assign_rows, table)


def unit_kernel(steps, offset, turn, start_ref, me_ref, rows_ref, *refs):
    unit_ref, held, sem = refs[-3:]
    part = unit_ref.shape[0] // steps
    window = part + SUBLANES
    start = start_ref[lax.rem(me_ref[0] + turn, start_ref.shape[0])] + offset

    def first(step):
        return aligned_start(start + step * part, rows_ref.shape[0], window)

    copies = [
        pltpu.make_async_copy(rows_ref.at[pl.ds(first(step), window), :], held.at[step], sem.at[step])
        for step in range(steps)
    ]
    for copy in copies:
        copy.start()
    for step in range(steps):
        copies[step].wait()
        shift = start + step * part - first(step)
        groups = held[step].reshape(window // SUBLANES, SUBLANES, -1)
        turned = pltpu.roll(groups, SUBLANES - shift, 1)
        line = lax.broadcasted_iota(jnp.int32, (part // SUBLANES, SUBLANES, groups.shape[2]), 1)
        values = jnp.where(line < SUBLANES - shift, turned[:-1], turned[1:]).reshape(part, -1)
        scale = lax.rsqrt(jnp.sum(values * values, -1, keepdims=True) + epsilon)
        unit_ref[step * part : (step + 1) * part, :] = (values * scale).astype(jnp.bfloat16)


def unit_piece(starts, me, embeddings, turn, offset, rows, after):
    width = embeddings.shape[1]
    steps = rows // LANES if rows % LANES == 0 else 1
    return pl.pallas_call(
        functools.partial(unit_kernel, steps, offset, turn),
        out_shape=jax.ShapeDtypeStruct((rows, width), jnp.bfloat16),
        in_specs=[in_smem, in_smem, anywhere] + [anywhere] * len(after),
        out_specs=in_vmem,
        scratch_shapes=[
            pltpu.VMEM((steps, rows // steps + SUBLANES, width), jnp.float32),
            pltpu.SemaphoreType.DMA((steps,)),
        ],
        compiler_params=params(),
        cost_estimate=brief,
        name="unit",
    )(starts, me, embeddings, *after)


def hold_until(values, arrived, mib=8):
    def nothing(*refs):
        pass

    return pl.pallas_call(
        nothing,
        out_shape=jax.ShapeDtypeStruct(values.shape, values.dtype),
        in_specs=[anywhere] * (1 + len(arrived)),
        out_specs=anywhere,
        input_output_aliases={0: 0},
        compiler_params=params(mib),
        cost_estimate=brief,
        name="hold",
    )(values, *arrived)


def aligned_start(start, row_count, window):
    begin = jnp.minimum(jnp.left_shift(jnp.right_shift(start, 3), 3), row_count - window)
    return pl.multiple_of(begin, SUBLANES)


def flat_window(held, start, rows):
    span = round_up(rows + 1, SUBLANES)
    shift = jnp.bitwise_and(start, LANES - 1)
    block = held[pl.ds(jnp.right_shift(start, 7), span), :]
    turned = pltpu.roll(block, jnp.bitwise_and(LANES - shift, LANES - 1), 1)
    following = pltpu.roll(turned, span - 1, 0)
    lane = lax.broadcasted_iota(jnp.int32, block.shape, 1)
    return jnp.where(lane < LANES - shift, turned, following)


def window_labels(held, slots, owner, start, per_owner, capacity, blocks):
    low = owner * per_owner
    mine = (slots >= low) & (slots < low + per_owner)
    held[: slots.shape[0], :] = jnp.where(mine, slots - low, -1)
    labels = flat_window(held, start, blocks)
    place = lax.broadcasted_iota(jnp.int32, labels.shape, 0) * LANES + lax.broadcasted_iota(
        jnp.int32, labels.shape, 1
    )
    return jnp.where(place < capacity, labels, -1)


def summed_kernel(per_owner, capacity, start_ref, slot_ref, sum_ref, held):
    owner_count = sum_ref.shape[0]
    held[...] = jnp.full(held.shape, -1, jnp.int32)
    slots = slot_ref[...]
    window = capacity + SUBLANES
    wide = sum_ref.shape[1] // LANES
    for owner in range(owner_count):
        aligned = aligned_start(start_ref[owner], slots.size, window)
        labels = window_labels(held, slots, owner, aligned, per_owner, window, wide)
        for block in range(wide):
            sum_ref[owner : owner + 1, block * LANES : (block + 1) * LANES] = labels[block : block + 1, :]


def summed_labels(starts, slots, owner_count, per_owner, capacity):
    return pl.pallas_call(
        functools.partial(summed_kernel, per_owner, capacity),
        out_shape=jax.ShapeDtypeStruct((owner_count, round_up(capacity + SUBLANES, LANES)), jnp.int32),
        in_specs=[in_smem, in_vmem],
        out_specs=in_vmem,
        scratch_shapes=[pltpu.VMEM((slots.shape[0] + 2 * SUBLANES, LANES), jnp.int32)],
        compiler_params=params(8),
        name="summed",
    )(starts, slots)


def sent_kernel(per_owner, capacity, start_ref, slot_ref, after_ref, sent_ref, held):
    owner_count, span, _ = sent_ref.shape
    held[...] = jnp.full(held.shape, -1, jnp.int32)
    slots = slot_ref[...]
    for owner in range(owner_count):
        labels = window_labels(held, slots, owner, start_ref[owner], per_owner, capacity, span - 1)
        sent_ref[owner] = labels[:span, :]


def sent_labels(starts, slots, owner_count, per_owner, capacity, after):
    span = round_up(-(-capacity // LANES) + 1, SUBLANES)
    return pl.pallas_call(
        functools.partial(sent_kernel, per_owner, capacity),
        out_shape=jax.ShapeDtypeStruct((owner_count, span, LANES), jnp.int32),
        in_specs=[in_smem, in_vmem, anywhere],
        out_specs=in_vmem,
        scratch_shapes=[pltpu.VMEM((slots.shape[0] + 2 * SUBLANES, LANES), jnp.int32)],
        compiler_params=params(8),
        name="sent",
    )(starts, slots, after)


def arrived_kernel(blocks, turns_of, me_ref, got_ref, row_ref, column_ref, tally_ref):
    tally = jnp.zeros((LANES, LANES), jnp.float32)
    cluster = lax.broadcasted_iota(jnp.int32, tally.shape, 0)
    for place, turn in enumerate(turns_of):
        source = lax.rem(me_ref[0] + len(turns_of) - turn, len(turns_of))
        for block in range(blocks):
            line = place * blocks + block
            spread = jnp.broadcast_to(got_ref[source, block : block + 1, :], tally.shape)
            row_ref[line : line + 1, :] = spread[:1, :]
            column_ref[line * LANES : (line + 1) * LANES, :] = spread.T
            tally += (spread == cluster).astype(jnp.float32)
    total = jnp.broadcast_to(jnp.sum(tally, 1, keepdims=True), tally.shape)
    tally_ref[...] = jnp.zeros(tally_ref.shape, jnp.float32)
    tally_ref[:, :LANES] = total.T[:SUBLANES, :]


def arrived_labels(me, got, turns_of, blocks, width):
    lines = len(turns_of) * blocks
    return pl.pallas_call(
        functools.partial(arrived_kernel, blocks, turns_of),
        out_shape=(
            jax.ShapeDtypeStruct((lines, LANES), jnp.int32),
            jax.ShapeDtypeStruct((lines * LANES, LANES), jnp.int32),
            jax.ShapeDtypeStruct((SUBLANES, width), jnp.float32),
        ),
        in_specs=[in_smem, in_vmem],
        out_specs=(in_vmem, in_vmem, in_vmem),
        compiler_params=params(8),
        name="arrived",
    )(me, got)


def sum_kernel(start_ref, label_ref, rows_ref, *refs):
    sum_ref, held, sem = refs[-3:]
    owner_count, per_owner, _ = sum_ref.shape
    window = held.shape[1]

    def copy(owner, slot):
        first = aligned_start(start_ref[owner], rows_ref.shape[0], window)
        return pltpu.make_async_copy(rows_ref.at[pl.ds(first, window), :], held.at[slot], sem.at[slot])

    copy(0, 0).start()

    def body(owner, carry):
        slot = lax.rem(owner, 2)

        @pl.when(owner + 1 < owner_count)
        def _():
            copy(owner + 1, 1 - slot).start()

        copy(owner, slot).wait()
        labels = label_ref[pl.ds(owner, 1), :][:, :window]
        cluster = lax.broadcasted_iota(jnp.int32, (per_owner, window), 0)
        member = (labels == cluster).astype(jnp.float32).astype(jnp.bfloat16)
        values = held[slot]
        high = values.astype(jnp.bfloat16)
        rest = values - high.astype(jnp.float32)
        middle = rest.astype(jnp.bfloat16)
        low = (rest - middle.astype(jnp.float32)).astype(jnp.bfloat16)
        total = jnp.dot(member, high, preferred_element_type=jnp.float32)
        total += jnp.dot(member, middle, preferred_element_type=jnp.float32)
        total += jnp.dot(member, low, preferred_element_type=jnp.float32)
        sum_ref[pl.ds(owner, 1)] = total[None]
        return carry

    lax.fori_loop(0, owner_count, body, 0)


def slot_sums(starts, labels, embeddings, per_owner, capacity, after):
    owner_count = labels.shape[0]
    width = embeddings.shape[1]
    return pl.pallas_call(
        sum_kernel,
        out_shape=jax.ShapeDtypeStruct((owner_count, per_owner, width), jnp.float32),
        in_specs=[in_smem, in_vmem, anywhere] + [anywhere] * len(after),
        out_specs=in_vmem,
        scratch_shapes=[
            pltpu.VMEM((2, capacity + SUBLANES, width), jnp.float32),
            pltpu.SemaphoreType.DMA((2,)),
        ],
        compiler_params=params(),
        cost_estimate=pl.CostEstimate(
            flops=6 * owner_count * per_owner * capacity * width,
            bytes_accessed=4 * embeddings.size,
            transcendentals=0,
        ),
        name="sums",
    )(starts, labels, embeddings, *after)


def gram_kernel(begin, rows, wide, after_count, turns_of, *refs):
    chunk_ref, row_ref, column_ref, best_ref, *refs = refs
    flat_ref = centroid_ref = result_ref = None
    if begin:
        flat_ref, *refs = refs
    refs = refs[after_count:]
    if turns_of:
        centroid_ref, me_ref, result_ref, *refs, out_ref, cosine_ref = refs
    else:
        out_ref, flat_ref, *refs = refs
    mine, turned, labels, tiles, even, odd, best, sem, tile_sem = refs
    first = begin // LANES
    size = tiles.shape[2]
    count = -(-begin // size)

    def line_of(tile):
        return jnp.minimum(tile * (size // LANES), first - size // LANES)

    def fetch(tile):
        start = pl.multiple_of(line_of(tile) * LANES, LANES)
        slot = lax.rem(tile, 4)
        return pltpu.make_async_copy(flat_ref.at[:, pl.ds(start, size)], tiles.at[slot], tile_sem.at[slot])

    chunk_copy = pltpu.make_async_copy(chunk_ref, mine.at[pl.ds(0, rows), :], sem.at[0])
    label_copy = pltpu.make_async_copy(column_ref.at[pl.ds(begin, wide), :], labels, sem.at[1])
    chunk_copy.start()
    label_copy.start()
    for tile in range(min(count, 3)):
        fetch(jnp.int32(tile)).start()
    if rows < wide:
        mine[rows:wide, :] = jnp.zeros((wide - rows, mine.shape[1]), mine.dtype)
    if turns_of:
        mine[wide:, :] = centroid_ref[...]
        cosine_ref[...] = jnp.zeros(cosine_ref.shape, jnp.float32)
    out_ref[...] = best_ref[...]
    best[...] = jnp.full(best.shape, -2.0, jnp.float32)
    chunk_copy.wait()
    label_copy.wait()
    turned[...] = mine[:wide, :].T
    if not turns_of:
        flat_copy = pltpu.make_async_copy(turned, flat_ref.at[:, pl.ds(begin, wide)], sem.at[2])
        flat_copy.start()

    def products(right):
        return jnp.dot(mine[...], right, preferred_element_type=jnp.float32)

    halves = 1

    def multiply(held, slot, half):
        here = slice(half * (size // halves), (half + 1) * (size // halves))
        held[:, here] = products(tiles[slot, :, here])

    def cosines(values, line):
        cluster = lax.broadcasted_iota(jnp.int32, values.shape, 0)
        own = jnp.where(row_ref[pl.ds(line, 1), :] == cluster, values, 0.0)
        cosine_ref[pl.ds(line, 1), :] = jnp.sum(own, 0, keepdims=True)

    def reduce_tile(held, tile, half):
        parts = range(half * (size // halves) // LANES, (half + 1) * (size // halves) // LANES)
        lines = {part: line_of(tile) + part for part in parts}
        tops = {part: jnp.full((SUBLANES, LANES), -2.0, jnp.float32) for part in parts}
        against = {
            part: jnp.broadcast_to(row_ref[pl.ds(lines[part], 1), :], (LANES, LANES)) for part in parts
        }
        for begin_row in range(0, wide, LANES):
            span = slice(begin_row, begin_row + LANES)
            own = labels[span, :]
            fold = best[span, :]
            for part in parts:
                near = jnp.where(own == against[part], held[span, part * LANES : (part + 1) * LANES], -2.0)
                fold = jnp.maximum(fold, near)
                tops[part] = jnp.maximum(tops[part], jnp.max(near.reshape(-1, SUBLANES, LANES), 0))
            best[span, :] = fold
        for part in parts:
            out_ref[pl.ds(lines[part], 1), :] = jnp.maximum(
                out_ref[pl.ds(lines[part], 1), :], jnp.max(tops[part], 0, keepdims=True)
            )
            if turns_of:
                cosines(held[wide:, part * LANES : (part + 1) * LANES], lines[part])

    if begin:
        fetch(jnp.int32(0)).wait()
        for half in range(halves):
            multiply(even, 0, half)

        def body(pair, carry):
            tile = pair * 2
            fetch(tile + 1).wait()

            @pl.when(tile + 3 < count)
            def _():
                fetch(tile + 3).start()

            for half in range(halves):
                multiply(odd, lax.rem(tile + 1, 4), half)
                reduce_tile(even, tile, half)
            fetch(tile + 2).wait()

            @pl.when(tile + 4 < count)
            def _():
                fetch(tile + 4).start()

            for half in range(halves):
                multiply(even, lax.rem(tile + 2, 4), half)
                reduce_tile(odd, tile + 1, half)
            return carry

        lax.fori_loop(0, (count - 1) // 2, body, 0)
        left = even
        if count % 2 == 0:
            left = odd
            fetch(jnp.int32(count - 1)).wait()
            for half in range(halves):
                multiply(odd, (count - 1) % 4, half)
                reduce_tile(even, jnp.int32(count - 2), half)
        for half in range(halves):
            reduce_tile(left, jnp.int32(count - 1), half)
    own = products(turned[...])
    row = lax.broadcasted_iota(jnp.int32, (wide, LANES), 0)
    column = lax.broadcasted_iota(jnp.int32, (wide, LANES), 1)
    for block in range(wide // LANES):
        line = first + block
        here = slice(block * LANES, (block + 1) * LANES)
        allowed = (labels[...] == row_ref[line : line + 1, :]) & (row != column + block * LANES)
        near = jnp.max(jnp.where(allowed, own[:wide, here], -2.0), 0, keepdims=True)
        other = jnp.max(best[here, :].T, 0, keepdims=True)
        out_ref[line : line + 1, :] = jnp.maximum(near, other)
        if turns_of:
            cosines(own[wide:, here], line)
    if turns_of:
        blocks = row_ref.shape[0] // len(turns_of)
        half = result_ref.shape[1] // 2
        result_ref[...] = jnp.zeros(result_ref.shape, jnp.float32)
        for place, turn in enumerate(turns_of):
            source = lax.rem(me_ref[0] + len(turns_of) - turn, len(turns_of))
            lines = slice(place * blocks, (place + 1) * blocks)
            result_ref[source, :blocks, :] = out_ref[lines, :]
            result_ref[source, half : half + blocks, :] = cosine_ref[lines, :]
    else:
        flat_copy.wait()


def gram_step(rows, columns, best, flat, chunk, begin, after=(), final=None):
    length, width = chunk.shape
    wide = round_up(length, LANES)
    tall = wide
    size = min(TILE if begin >= 2 * TILE else 4 * LANES, begin) if begin else LANES
    flat_shape = jax.ShapeDtypeStruct((width, columns.shape[0]), jnp.bfloat16)
    inputs = [chunk, rows, columns, best]
    in_specs = [anywhere, in_vmem, anywhere, in_vmem]
    aliases = {}
    if begin:
        if not final:
            aliases = {len(inputs): 1}
        inputs.append(flat)
        in_specs.append(anywhere)
    inputs += after
    in_specs += [anywhere] * len(after)
    out_shape = (jax.ShapeDtypeStruct(best.shape, jnp.float32), flat_shape)
    out_specs = (in_vmem, anywhere)
    turns_of = ()
    extra = []
    if final:
        centroid_unit, me, turns_of = final
        tall += centroid_unit.shape[0]
        inputs += [centroid_unit, me]
        in_specs += [in_vmem, in_smem]
        half = round_up(rows.shape[0] // len(turns_of) + 1, SUBLANES)
        out_shape = jax.ShapeDtypeStruct((len(turns_of), 2 * half, LANES), jnp.float32)
        out_specs = in_vmem
        extra = [pltpu.VMEM(best.shape, jnp.float32)] * 2
    return pl.pallas_call(
        functools.partial(gram_kernel, begin, length, wide, len(after), turns_of),
        out_shape=out_shape,
        in_specs=in_specs,
        out_specs=out_specs,
        scratch_shapes=[
            pltpu.VMEM((tall, width), jnp.bfloat16),
            pltpu.VMEM((width, wide), jnp.bfloat16),
            pltpu.VMEM((wide, LANES), jnp.int32),
            pltpu.VMEM((4, width, size), jnp.bfloat16),
            pltpu.VMEM((tall, size), jnp.float32),
            pltpu.VMEM((tall, size), jnp.float32),
            pltpu.VMEM((wide, LANES), jnp.float32),
            pltpu.SemaphoreType.DMA((3,)),
            pltpu.SemaphoreType.DMA((4,)),
        ]
        + extra,
        input_output_aliases=aliases,
        compiler_params=params(),
        cost_estimate=brief,
        name="gram",
    )(*inputs)


def pack_kernel(share_ref, tally_ref, *refs):
    packed_ref = refs[-1]
    packed_ref[: share_ref.shape[0], :] = share_ref[...]
    packed_ref[share_ref.shape[0] :, :] = tally_ref[...]


def pack_share(share, tally, after):
    length = share.shape[0] + tally.shape[0]
    return pl.pallas_call(
        pack_kernel,
        out_shape=jax.ShapeDtypeStruct((length, share.shape[1]), jnp.float32),
        in_specs=[in_vmem, in_vmem] + [anywhere] * len(after),
        out_specs=in_vmem,
        compiler_params=params(8),
        name="pack",
    )(share, tally, *after)


def centroid_kernel(gathered_ref, centroid_ref, unit_ref):
    groups, length, width = gathered_ref.shape
    share = length - SUBLANES
    per_owner = centroid_ref.shape[0]
    tally = jnp.sum(gathered_ref[:, share, :LANES], 0, keepdims=True)
    column = jnp.broadcast_to(tally, (LANES, LANES)).T[:per_owner, :]
    sums = jnp.concatenate([gathered_ref[group, :share, :] for group in range(groups)], 0)
    centroids = sums / jnp.concatenate([column] * (width // LANES), 1)
    centroid_ref[...] = centroids
    scale = lax.rsqrt(jnp.sum(centroids * centroids, -1, keepdims=True) + epsilon)
    unit_ref[...] = (centroids * scale).astype(jnp.bfloat16)


def make_centroids(gathered, per_owner):
    shape = (per_owner, gathered.shape[2])
    return pl.pallas_call(
        centroid_kernel,
        out_shape=(
            jax.ShapeDtypeStruct(shape, jnp.float32),
            jax.ShapeDtypeStruct(shape, jnp.bfloat16),
        ),
        in_specs=[in_vmem],
        out_specs=(in_vmem, in_vmem),
        compiler_params=params(8),
        name="centroids",
    )(gathered)


def place_kernel(per_owner, start_ref, slot_ref, back_ref, near_ref, cosine_ref, held, result):
    owner_count, double, _ = back_ref.shape
    span = double // 2
    rows = slot_ref.shape[0]
    held[...] = jnp.full(held.shape, -1, jnp.int32)
    held[:rows, :] = slot_ref[...]
    result[...] = jnp.zeros(result.shape, jnp.float32)
    lane = lax.broadcasted_iota(jnp.int32, (span, LANES), 1)
    for owner in range(owner_count):
        start = start_ref[owner]
        first = pl.ds(jnp.right_shift(start, 7), span)
        shift = jnp.bitwise_and(start, LANES - 1)
        slots = held[first, :]
        mine = (slots >= owner * per_owner) & (slots < (owner + 1) * per_owner)
        for kind in range(2):
            turned = pltpu.roll(back_ref[owner, kind * span : (kind + 1) * span, :], shift, 1)
            earlier = pltpu.roll(turned, 1, 0)
            moved = jnp.where(lane >= shift, turned, earlier)
            result[kind, first, :] = jnp.where(mine, moved, result[kind, first, :])
    near_ref[...] = result[0, :rows, :]
    cosine_ref[...] = result[1, :rows, :]


def place_rows(starts, slots, back, per_owner):
    span = back.shape[1] // 2
    rows = slots.shape[0]
    return pl.pallas_call(
        functools.partial(place_kernel, per_owner),
        out_shape=(jax.ShapeDtypeStruct(slots.shape, jnp.float32),) * 2,
        in_specs=[in_smem, in_vmem, in_vmem],
        out_specs=(in_vmem, in_vmem),
        scratch_shapes=[
            pltpu.VMEM((rows + span, LANES), jnp.int32),
            pltpu.VMEM((2, rows + span, LANES), jnp.float32),
        ],
        compiler_params=params(8),
        name="place",
    )(starts, slots, back)


def turns(count):
    order = sorted(range(count), key=lambda turn: (min(turn, count - turn), turn))
    if count == 8:
        order = [0, 1, 2, 3, 7, 6, 5, 4]
    return order


def per_device(embeddings, assign, cluster_slot):
    row_count, width = embeddings.shape
    owner_count = lax.axis_size("docs")
    per_owner = cluster_slot.shape[0] // owner_count
    capacity = row_count // owner_count + row_count // (4 * owner_count)
    padded = round_up(capacity, LANES)
    blocks = padded // LANES
    me = lax.axis_index("docs").astype(jnp.int32).reshape(1)
    turns_of = turns(owner_count)

    slots, starts = make_plan(
        assign.reshape(-1, LANES), cluster_slot.reshape(-1, LANES), owner_count, per_owner, row_count - capacity
    )

    sent = []
    for place, turn in enumerate(turns_of):
        sent.append(unit_piece(starts, me, embeddings, turn, 0, capacity, sent[-1:] if place > 1 else []))

    def travel(place, piece):
        turn = turns_of[place]
        return lax.ppermute(piece, "docs", [(i, (i + turn) % owner_count) for i in range(owner_count)])

    chunks = [sent[0]] + [travel(place, sent[place]) for place in (1, 2, 3)]
    sum_labels = summed_labels(starts, slots, owner_count, per_owner, capacity)
    partial_sums = slot_sums(starts, sum_labels, embeddings, per_owner, capacity, sent[1:8])
    partial_sums = hold_until(partial_sums, chunks[1:3], 62)
    wire_labels = sent_labels(starts, slots, owner_count, per_owner, capacity, sent[7])
    wire_labels = hold_until(wire_labels, chunks[1:3])
    got_labels = lax.all_to_all(wire_labels, "docs", split_axis=0, concat_axis=0, tiled=True)
    rows, columns, group_tally = arrived_labels(me, got_labels, turns_of, blocks, width)
    group_share = lax.psum_scatter(partial_sums, "grp", scatter_dimension=1, tiled=True)
    group_share = hold_until(group_share, [chunks[3], got_labels])
    share = lax.psum_scatter(group_share, "docs", scatter_dimension=0, tiled=True)[0]
    for place in range(4, owner_count):
        after = [chunks[4]] if place == owner_count - 1 else [chunks[3], got_labels]
        chunks.append(travel(place, hold_until(sent[place], after)))

    bests = [jnp.full((owner_count * blocks, LANES), -2.0, jnp.float32)]
    flat = None
    for place in range(owner_count - 1):
        after = []
        if place == owner_count - 2:
            packed = pack_share(share, group_tally, bests[-2:-1])
            centroids, centroid_unit = make_centroids(lax.all_gather(packed, "grp"), per_owner)
            after = [centroid_unit]
        best, flat = gram_step(rows, columns, bests[-1], flat, chunks[place], place * padded, after)
        bests.append(best)
    results = gram_step(
        rows, columns, bests[-1], flat, chunks[-1], (owner_count - 1) * padded, final=(centroid_unit, me, turns_of)
    )
    back = lax.all_to_all(results, "docs", split_axis=0, concat_axis=0, tiled=True)
    near, cosine = place_rows(starts, slots, back, per_owner)
    return (centroids, near.reshape(-1), cosine.reshape(-1))


def solution(mesh):
    placed = (P(("grp", "docs"), None), P(("grp", "docs")), P())
    return jax.shard_map(
        per_device,
        mesh=mesh,
        in_specs=placed,
        out_specs=(P("docs", None), P(("grp", "docs")), P(("grp", "docs"))),
        check_vma=False,
    )
```

```python
import functools

import jax
import jax.numpy as jnp
from jax import lax
from jax.experimental import pallas as pl
from jax.experimental.pallas import tpu as pltpu
from jax.sharding import PartitionSpec as P

epsilon = 1e-06
LANES = 128
SUBLANES = 8
MIB = 1024 * 1024
TILE = 512
in_vmem = pl.BlockSpec(memory_space=pltpu.VMEM)
in_smem = pl.BlockSpec(memory_space=pltpu.SMEM)
anywhere = pl.BlockSpec(memory_space=pl.ANY)
brief = pl.CostEstimate(flops=1000, bytes_accessed=1000, transcendentals=0)


def round_up(value, step):
    return -(-value // step) * step


def params(mib=44):
    return pltpu.CompilerParams(vmem_limit_bytes=mib * MIB)


def look_up(table_ref, index):
    lane = jnp.bitwise_and(index, LANES - 1)
    row = jnp.right_shift(index, 7)
    found = jnp.zeros(index.shape, jnp.int32)
    for part in range(table_ref.shape[0]):
        entries = jnp.broadcast_to(table_ref[part : part + 1, :], index.shape)
        found = jnp.where(row == part, jnp.take_along_axis(entries, lane, axis=1), found)
    return found


def rows_below(slots, bound):
    return jnp.sum((slots < bound).astype(jnp.float32)).astype(jnp.int32)


def plan_kernel(per_owner, limit, assign_ref, table_ref, slot_ref, start_ref):
    slots = look_up(table_ref, assign_ref[...])
    slot_ref[...] = slots
    for owner in range(start_ref.shape[0]):
        start_ref[owner] = jnp.minimum(rows_below(slots, owner * per_owner), limit)


def make_plan(assign_rows, table, owner_count, per_owner, limit):
    return pl.pallas_call(
        functools.partial(plan_kernel, per_owner, limit),
        out_shape=(
            jax.ShapeDtypeStruct(assign_rows.shape, jnp.int32),
            jax.ShapeDtypeStruct((owner_count,), jnp.int32),
        ),
        in_specs=[in_vmem, in_vmem],
        out_specs=(in_vmem, in_smem),
        compiler_params=params(8),
        name="plan",
    )(assign_rows, table)


def unit_kernel(steps, offset, turn, start_ref, me_ref, rows_ref, *refs):
    unit_ref, held, sem = refs[-3:]
    part = unit_ref.shape[0] // steps
    window = part + SUBLANES
    start = start_ref[lax.rem(me_ref[0] + turn, start_ref.shape[0])] + offset

    def first(step):
        return aligned_start(start + step * part, rows_ref.shape[0], window)

    copies = [
        pltpu.make_async_copy(rows_ref.at[pl.ds(first(step), window), :], held.at[step], sem.at[step])
        for step in range(steps)
    ]
    for copy in copies:
        copy.start()
    for step in range(steps):
        copies[step].wait()
        shift = start + step * part - first(step)
        groups = held[step].reshape(window // SUBLANES, SUBLANES, -1)
        turned = pltpu.roll(groups, SUBLANES - shift, 1)
        line = lax.broadcasted_iota(jnp.int32, (part // SUBLANES, SUBLANES, groups.shape[2]), 1)
        values = jnp.where(line < SUBLANES - shift, turned[:-1], turned[1:]).reshape(part, -1)
        scale = lax.rsqrt(jnp.sum(values * values, -1, keepdims=True) + epsilon)
        unit_ref[step * part : (step + 1) * part, :] = (values * scale).astype(jnp.bfloat16)


def unit_piece(starts, me, embeddings, turn, offset, rows, after):
    width = embeddings.shape[1]
    steps = rows // LANES if rows % LANES == 0 else 1
    return pl.pallas_call(
        functools.partial(unit_kernel, steps, offset, turn),
        out_shape=jax.ShapeDtypeStruct((rows, width), jnp.bfloat16),
        in_specs=[in_smem, in_smem, anywhere] + [anywhere] * len(after),
        out_specs=in_vmem,
        scratch_shapes=[
            pltpu.VMEM((steps, rows // steps + SUBLANES, width), jnp.float32),
            pltpu.SemaphoreType.DMA((steps,)),
        ],
        compiler_params=params(),
        cost_estimate=brief,
        name="unit",
    )(starts, me, embeddings, *after)


def hold_until(values, arrived, mib=8):
    def nothing(*refs):
        pass

    return pl.pallas_call(
        nothing,
        out_shape=jax.ShapeDtypeStruct(values.shape, values.dtype),
        in_specs=[anywhere] * (1 + len(arrived)),
        out_specs=anywhere,
        input_output_aliases={0: 0},
        compiler_params=params(mib),
        cost_estimate=brief,
        name="hold",
    )(values, *arrived)


def aligned_start(start, row_count, window):
    begin = jnp.minimum(jnp.left_shift(jnp.right_shift(start, 3), 3), row_count - window)
    return pl.multiple_of(begin, SUBLANES)


def flat_window(held, start, rows):
    span = round_up(rows + 1, SUBLANES)
    shift = jnp.bitwise_and(start, LANES - 1)
    block = held[pl.ds(jnp.right_shift(start, 7), span), :]
    turned = pltpu.roll(block, jnp.bitwise_and(LANES - shift, LANES - 1), 1)
    following = pltpu.roll(turned, span - 1, 0)
    lane = lax.broadcasted_iota(jnp.int32, block.shape, 1)
    return jnp.where(lane < LANES - shift, turned, following)


def window_labels(held, slots, owner, start, per_owner, capacity, blocks):
    low = owner * per_owner
    mine = (slots >= low) & (slots < low + per_owner)
    held[: slots.shape[0], :] = jnp.where(mine, slots - low, -1)
    labels = flat_window(held, start, blocks)
    place = lax.broadcasted_iota(jnp.int32, labels.shape, 0) * LANES + lax.broadcasted_iota(
        jnp.int32, labels.shape, 1
    )
    return jnp.where(place < capacity, labels, -1)


def summed_kernel(per_owner, capacity, start_ref, slot_ref, sum_ref, held):
    owner_count = sum_ref.shape[0]
    held[...] = jnp.full(held.shape, -1, jnp.int32)
    slots = slot_ref[...]
    window = capacity + SUBLANES
    wide = sum_ref.shape[1] // LANES
    for owner in range(owner_count):
        aligned = aligned_start(start_ref[owner], slots.size, window)
        labels = window_labels(held, slots, owner, aligned, per_owner, window, wide)
        for block in range(wide):
            sum_ref[owner : owner + 1, block * LANES : (block + 1) * LANES] = labels[block : block + 1, :]


def summed_labels(starts, slots, owner_count, per_owner, capacity):
    return pl.pallas_call(
        functools.partial(summed_kernel, per_owner, capacity),
        out_shape=jax.ShapeDtypeStruct((owner_count, round_up(capacity + SUBLANES, LANES)), jnp.int32),
        in_specs=[in_smem, in_vmem],
        out_specs=in_vmem,
        scratch_shapes=[pltpu.VMEM((slots.shape[0] + 2 * SUBLANES, LANES), jnp.int32)],
        compiler_params=params(8),
        name="summed",
    )(starts, slots)


def sent_kernel(per_owner, capacity, start_ref, slot_ref, after_ref, sent_ref, held):
    owner_count, span, _ = sent_ref.shape
    held[...] = jnp.full(held.shape, -1, jnp.int32)
    slots = slot_ref[...]
    for owner in range(owner_count):
        labels = window_labels(held, slots, owner, start_ref[owner], per_owner, capacity, span - 1)
        sent_ref[owner] = labels[:span, :]


def sent_labels(starts, slots, owner_count, per_owner, capacity, after):
    span = round_up(-(-capacity // LANES) + 1, SUBLANES)
    return pl.pallas_call(
        functools.partial(sent_kernel, per_owner, capacity),
        out_shape=jax.ShapeDtypeStruct((owner_count, span, LANES), jnp.int32),
        in_specs=[in_smem, in_vmem, anywhere],
        out_specs=in_vmem,
        scratch_shapes=[pltpu.VMEM((slots.shape[0] + 2 * SUBLANES, LANES), jnp.int32)],
        compiler_params=params(8),
        name="sent",
    )(starts, slots, after)


def arrived_kernel(blocks, turns_of, me_ref, got_ref, row_ref, column_ref, tally_ref):
    tally = jnp.zeros((LANES, LANES), jnp.float32)
    cluster = lax.broadcasted_iota(jnp.int32, tally.shape, 0)
    for place, turn in enumerate(turns_of):
        source = lax.rem(me_ref[0] + len(turns_of) - turn, len(turns_of))
        for block in range(blocks):
            line = place * blocks + block
            spread = jnp.broadcast_to(got_ref[source, block : block + 1, :], tally.shape)
            row_ref[line : line + 1, :] = spread[:1, :]
            column_ref[line * LANES : (line + 1) * LANES, :] = spread.T
            tally += (spread == cluster).astype(jnp.float32)
    total = jnp.broadcast_to(jnp.sum(tally, 1, keepdims=True), tally.shape)
    tally_ref[...] = jnp.zeros(tally_ref.shape, jnp.float32)
    tally_ref[:, :LANES] = total.T[:SUBLANES, :]


def arrived_labels(me, got, turns_of, blocks, width):
    lines = len(turns_of) * blocks
    return pl.pallas_call(
        functools.partial(arrived_kernel, blocks, turns_of),
        out_shape=(
            jax.ShapeDtypeStruct((lines, LANES), jnp.int32),
            jax.ShapeDtypeStruct((lines * LANES, LANES), jnp.int32),
            jax.ShapeDtypeStruct((SUBLANES, width), jnp.float32),
        ),
        in_specs=[in_smem, in_vmem],
        out_specs=(in_vmem, in_vmem, in_vmem),
        compiler_params=params(8),
        name="arrived",
    )(me, got)


def sum_kernel(start_ref, label_ref, rows_ref, *refs):
    sum_ref, held, sem = refs[-3:]
    owner_count, per_owner, _ = sum_ref.shape
    window = held.shape[1]
    widest = float(jnp.finfo(jnp.bfloat16).max)

    def copy(owner, slot):
        first = aligned_start(start_ref[owner], rows_ref.shape[0], window)
        return pltpu.make_async_copy(rows_ref.at[pl.ds(first, window), :], held.at[slot], sem.at[slot])

    copy(0, 0).start()

    def body(owner, carry):
        slot = lax.rem(owner, 2)

        @pl.when(owner + 1 < owner_count)
        def _():
            copy(owner + 1, 1 - slot).start()

        copy(owner, slot).wait()
        labels = label_ref[pl.ds(owner, 1), :][:, :window]
        cluster = lax.broadcasted_iota(jnp.int32, (per_owner, window), 0)
        member = (labels == cluster).astype(jnp.float32).astype(jnp.bfloat16)
        values = held[slot]
        high = jnp.clip(values, -widest, widest).astype(jnp.bfloat16)
        rest = values - high.astype(jnp.float32)
        middle = rest.astype(jnp.bfloat16)
        low = (rest - middle.astype(jnp.float32)).astype(jnp.bfloat16)
        total = jnp.dot(member, high, preferred_element_type=jnp.float32)
        total += jnp.dot(member, middle, preferred_element_type=jnp.float32)
        total += jnp.dot(member, low, preferred_element_type=jnp.float32)
        sum_ref[pl.ds(owner, 1)] = total[None]
        return carry

    lax.fori_loop(0, owner_count, body, 0)


def slot_sums(starts, labels, embeddings, per_owner, capacity, after):
    owner_count = labels.shape[0]
    width = embeddings.shape[1]
    return pl.pallas_call(
        sum_kernel,
        out_shape=jax.ShapeDtypeStruct((owner_count, per_owner, width), jnp.float32),
        in_specs=[in_smem, in_vmem, anywhere] + [anywhere] * len(after),
        out_specs=in_vmem,
        scratch_shapes=[
            pltpu.VMEM((2, capacity + SUBLANES, width), jnp.float32),
            pltpu.SemaphoreType.DMA((2,)),
        ],
        compiler_params=params(),
        cost_estimate=pl.CostEstimate(
            flops=6 * owner_count * per_owner * capacity * width,
            bytes_accessed=4 * embeddings.size,
            transcendentals=0,
        ),
        name="sums",
    )(starts, labels, embeddings, *after)


def gram_kernel(begin, rows, wide, after_count, turns_of, *refs):
    chunk_ref, row_ref, column_ref, best_ref, *refs = refs
    flat_ref = centroid_ref = result_ref = None
    if begin:
        flat_ref, *refs = refs
    refs = refs[after_count:]
    if turns_of:
        centroid_ref, me_ref, result_ref, *refs, out_ref, cosine_ref = refs
    else:
        out_ref, flat_ref, *refs = refs
    mine, turned, labels, tiles, even, odd, best, sem, tile_sem = refs
    first = begin // LANES
    size = tiles.shape[2]
    count = -(-begin // size)

    def line_of(tile):
        return jnp.minimum(tile * (size // LANES), first - size // LANES)

    def fetch(tile):
        start = pl.multiple_of(line_of(tile) * LANES, LANES)
        slot = lax.rem(tile, 4)
        return pltpu.make_async_copy(flat_ref.at[:, pl.ds(start, size)], tiles.at[slot], tile_sem.at[slot])

    chunk_copy = pltpu.make_async_copy(chunk_ref, mine.at[pl.ds(0, rows), :], sem.at[0])
    label_copy = pltpu.make_async_copy(column_ref.at[pl.ds(begin, wide), :], labels, sem.at[1])
    chunk_copy.start()
    label_copy.start()
    for tile in range(min(count, 3)):
        fetch(jnp.int32(tile)).start()
    if rows < wide:
        mine[rows:wide, :] = jnp.zeros((wide - rows, mine.shape[1]), mine.dtype)
    if turns_of:
        mine[wide:, :] = centroid_ref[...]
        cosine_ref[...] = jnp.zeros(cosine_ref.shape, jnp.float32)
    out_ref[...] = best_ref[...]
    best[...] = jnp.full(best.shape, -2.0, jnp.float32)
    chunk_copy.wait()
    label_copy.wait()
    turned[...] = mine[:wide, :].T
    if not turns_of:
        flat_copy = pltpu.make_async_copy(turned, flat_ref.at[:, pl.ds(begin, wide)], sem.at[2])
        flat_copy.start()

    def products(right):
        return jnp.dot(mine[...], right, preferred_element_type=jnp.float32)

    halves = 2 if size % (4 * LANES) == 0 else 1

    def multiply(held, slot, half):
        here = slice(half * (size // halves), (half + 1) * (size // halves))
        held[:, here] = products(tiles[slot, :, here])

    def cosines(values, line):
        cluster = lax.broadcasted_iota(jnp.int32, values.shape, 0)
        own = jnp.where(row_ref[pl.ds(line, 1), :] == cluster, values, 0.0)
        cosine_ref[pl.ds(line, 1), :] = jnp.sum(own, 0, keepdims=True)

    def reduce_tile(held, tile, half):
        parts = range(half * (size // halves) // LANES, (half + 1) * (size // halves) // LANES)
        lines = {part: line_of(tile) + part for part in parts}
        tops = {part: jnp.full((SUBLANES, LANES), -2.0, jnp.float32) for part in parts}
        against = {
            part: jnp.broadcast_to(row_ref[pl.ds(lines[part], 1), :], (LANES, LANES)) for part in parts
        }
        for begin_row in range(0, wide, LANES):
            span = slice(begin_row, begin_row + LANES)
            own = labels[span, :]
            fold = best[span, :]
            for part in parts:
                near = jnp.where(own == against[part], held[span, part * LANES : (part + 1) * LANES], -2.0)
                fold = jnp.maximum(fold, near)
                tops[part] = jnp.maximum(tops[part], jnp.max(near.reshape(-1, SUBLANES, LANES), 0))
            best[span, :] = fold
        for part in parts:
            out_ref[pl.ds(lines[part], 1), :] = jnp.maximum(
                out_ref[pl.ds(lines[part], 1), :], jnp.max(tops[part], 0, keepdims=True)
            )
            if turns_of:
                cosines(held[wide:, part * LANES : (part + 1) * LANES], lines[part])

    if begin:
        fetch(jnp.int32(0)).wait()
        for half in range(halves):
            multiply(even, 0, half)

        def body(pair, carry):
            tile = pair * 2
            fetch(tile + 1).wait()

            @pl.when(tile + 3 < count)
            def _():
                fetch(tile + 3).start()

            for half in range(halves):
                multiply(odd, lax.rem(tile + 1, 4), half)
                reduce_tile(even, tile, half)
            fetch(tile + 2).wait()

            @pl.when(tile + 4 < count)
            def _():
                fetch(tile + 4).start()

            for half in range(halves):
                multiply(even, lax.rem(tile + 2, 4), half)
                reduce_tile(odd, tile + 1, half)
            return carry

        lax.fori_loop(0, (count - 1) // 2, body, 0)
        left = even
        if count % 2 == 0:
            left = odd
            fetch(jnp.int32(count - 1)).wait()
            for half in range(halves):
                multiply(odd, (count - 1) % 4, half)
                reduce_tile(even, jnp.int32(count - 2), half)
        for half in range(halves):
            reduce_tile(left, jnp.int32(count - 1), half)
    own = products(turned[...])
    row = lax.broadcasted_iota(jnp.int32, (wide, LANES), 0)
    column = lax.broadcasted_iota(jnp.int32, (wide, LANES), 1)
    for block in range(wide // LANES):
        line = first + block
        here = slice(block * LANES, (block + 1) * LANES)
        allowed = (labels[...] == row_ref[line : line + 1, :]) & (row != column + block * LANES)
        near = jnp.max(jnp.where(allowed, own[:wide, here], -2.0), 0, keepdims=True)
        other = jnp.max(best[here, :].T, 0, keepdims=True)
        out_ref[line : line + 1, :] = jnp.maximum(near, other)
        if turns_of:
            cosines(own[wide:, here], line)
    if turns_of:
        blocks = row_ref.shape[0] // len(turns_of)
        half = result_ref.shape[1] // 2
        result_ref[...] = jnp.zeros(result_ref.shape, jnp.float32)
        for place, turn in enumerate(turns_of):
            source = lax.rem(me_ref[0] + len(turns_of) - turn, len(turns_of))
            lines = slice(place * blocks, (place + 1) * blocks)
            result_ref[source, :blocks, :] = out_ref[lines, :]
            result_ref[source, half : half + blocks, :] = cosine_ref[lines, :]
    else:
        flat_copy.wait()


def gram_step(rows, columns, best, flat, chunk, begin, after=(), final=None):
    length, width = chunk.shape
    wide = round_up(length, LANES)
    tall = wide
    size = min(TILE, begin) if begin else LANES
    flat_shape = jax.ShapeDtypeStruct((width, columns.shape[0]), jnp.bfloat16)
    inputs = [chunk, rows, columns, best]
    in_specs = [anywhere, in_vmem, anywhere, in_vmem]
    aliases = {}
    if begin:
        if not final:
            aliases = {len(inputs): 1}
        inputs.append(flat)
        in_specs.append(anywhere)
    inputs += after
    in_specs += [anywhere] * len(after)
    out_shape = (jax.ShapeDtypeStruct(best.shape, jnp.float32), flat_shape)
    out_specs = (in_vmem, anywhere)
    turns_of = ()
    extra = []
    if final:
        centroid_unit, me, turns_of = final
        tall += centroid_unit.shape[0]
        inputs += [centroid_unit, me]
        in_specs += [in_vmem, in_smem]
        half = round_up(rows.shape[0] // len(turns_of) + 1, SUBLANES)
        out_shape = jax.ShapeDtypeStruct((len(turns_of), 2 * half, LANES), jnp.float32)
        out_specs = in_vmem
        extra = [pltpu.VMEM(best.shape, jnp.float32)] * 2
    return pl.pallas_call(
        functools.partial(gram_kernel, begin, length, wide, len(after), turns_of),
        out_shape=out_shape,
        in_specs=in_specs,
        out_specs=out_specs,
        scratch_shapes=[
            pltpu.VMEM((tall, width), jnp.bfloat16),
            pltpu.VMEM((width, wide), jnp.bfloat16),
            pltpu.VMEM((wide, LANES), jnp.int32),
            pltpu.VMEM((4, width, size), jnp.bfloat16),
            pltpu.VMEM((tall, size), jnp.float32),
            pltpu.VMEM((tall, size), jnp.float32),
            pltpu.VMEM((wide, LANES), jnp.float32),
            pltpu.SemaphoreType.DMA((3,)),
            pltpu.SemaphoreType.DMA((4,)),
        ]
        + extra,
        input_output_aliases=aliases,
        compiler_params=params(),
        cost_estimate=brief,
        name="gram",
    )(*inputs)


def pack_kernel(share_ref, tally_ref, *refs):
    packed_ref = refs[-1]
    packed_ref[: share_ref.shape[0], :] = share_ref[...]
    packed_ref[share_ref.shape[0] :, :] = tally_ref[...]


def pack_share(share, tally, after):
    length = share.shape[0] + tally.shape[0]
    return pl.pallas_call(
        pack_kernel,
        out_shape=jax.ShapeDtypeStruct((length, share.shape[1]), jnp.float32),
        in_specs=[in_vmem, in_vmem] + [anywhere] * len(after),
        out_specs=in_vmem,
        compiler_params=params(8),
        name="pack",
    )(share, tally, *after)


def centroid_kernel(gathered_ref, centroid_ref, unit_ref):
    groups, length, width = gathered_ref.shape
    share = length - SUBLANES
    per_owner = centroid_ref.shape[0]
    tally = jnp.sum(gathered_ref[:, share, :LANES], 0, keepdims=True)
    column = jnp.broadcast_to(tally, (LANES, LANES)).T[:per_owner, :]
    sums = jnp.concatenate([gathered_ref[group, :share, :] for group in range(groups)], 0)
    centroids = sums / jnp.concatenate([column] * (width // LANES), 1)
    centroid_ref[...] = centroids
    scale = lax.rsqrt(jnp.sum(centroids * centroids, -1, keepdims=True) + epsilon)
    unit_ref[...] = (centroids * scale).astype(jnp.bfloat16)


def make_centroids(gathered, per_owner):
    shape = (per_owner, gathered.shape[2])
    return pl.pallas_call(
        centroid_kernel,
        out_shape=(
            jax.ShapeDtypeStruct(shape, jnp.float32),
            jax.ShapeDtypeStruct(shape, jnp.bfloat16),
        ),
        in_specs=[in_vmem],
        out_specs=(in_vmem, in_vmem),
        compiler_params=params(8),
        name="centroids",
    )(gathered)


def place_kernel(per_owner, start_ref, slot_ref, back_ref, near_ref, cosine_ref, held, result):
    owner_count, double, _ = back_ref.shape
    span = double // 2
    rows = slot_ref.shape[0]
    held[...] = jnp.full(held.shape, -1, jnp.int32)
    held[:rows, :] = slot_ref[...]
    result[...] = jnp.zeros(result.shape, jnp.float32)
    lane = lax.broadcasted_iota(jnp.int32, (span, LANES), 1)
    for owner in range(owner_count):
        start = start_ref[owner]
        first = pl.ds(jnp.right_shift(start, 7), span)
        shift = jnp.bitwise_and(start, LANES - 1)
        slots = held[first, :]
        mine = (slots >= owner * per_owner) & (slots < (owner + 1) * per_owner)
        for kind in range(2):
            turned = pltpu.roll(back_ref[owner, kind * span : (kind + 1) * span, :], shift, 1)
            earlier = pltpu.roll(turned, 1, 0)
            moved = jnp.where(lane >= shift, turned, earlier)
            result[kind, first, :] = jnp.where(mine, moved, result[kind, first, :])
    near_ref[...] = result[0, :rows, :]
    cosine_ref[...] = result[1, :rows, :]


def place_rows(starts, slots, back, per_owner):
    span = back.shape[1] // 2
    rows = slots.shape[0]
    return pl.pallas_call(
        functools.partial(place_kernel, per_owner),
        out_shape=(jax.ShapeDtypeStruct(slots.shape, jnp.float32),) * 2,
        in_specs=[in_smem, in_vmem, in_vmem],
        out_specs=(in_vmem, in_vmem),
        scratch_shapes=[
            pltpu.VMEM((rows + span, LANES), jnp.int32),
            pltpu.VMEM((2, rows + span, LANES), jnp.float32),
        ],
        compiler_params=params(8),
        name="place",
    )(starts, slots, back)


def turns(count):
    order = sorted(range(count), key=lambda turn: (min(turn, count - turn), turn))
    if count == 8:
        order = [0, 1, 2, 3, 7, 6, 5, 4]
    return order


def per_device(embeddings, assign, cluster_slot):
    row_count, width = embeddings.shape
    owner_count = lax.axis_size("docs")
    per_owner = cluster_slot.shape[0] // owner_count
    capacity = row_count // owner_count + row_count // (4 * owner_count)
    padded = round_up(capacity, LANES)
    blocks = padded // LANES
    me = lax.axis_index("docs").astype(jnp.int32).reshape(1)
    turns_of = turns(owner_count)

    slots, starts = make_plan(
        assign.reshape(-1, LANES), cluster_slot.reshape(-1, LANES), owner_count, per_owner, row_count - capacity
    )

    sent = []
    for place, turn in enumerate(turns_of):
        sent.append(unit_piece(starts, me, embeddings, turn, 0, capacity, sent[-1:] if place > 1 else []))

    def travel(place, piece):
        turn = turns_of[place]
        return lax.ppermute(piece, "docs", [(i, (i + turn) % owner_count) for i in range(owner_count)])

    chunks = [sent[0]] + [travel(place, sent[place]) for place in (1, 2, 3)]
    sum_labels = summed_labels(starts, slots, owner_count, per_owner, capacity)
    partial_sums = slot_sums(starts, sum_labels, embeddings, per_owner, capacity, sent[1:8])
    partial_sums = hold_until(partial_sums, chunks[1:3], 62)
    wire_labels = sent_labels(starts, slots, owner_count, per_owner, capacity, sent[7])
    wire_labels = hold_until(wire_labels, chunks[1:3])
    got_labels = lax.all_to_all(wire_labels, "docs", split_axis=0, concat_axis=0, tiled=True)
    rows, columns, group_tally = arrived_labels(me, got_labels, turns_of, blocks, width)
    group_share = lax.psum_scatter(partial_sums, "grp", scatter_dimension=1, tiled=True)
    group_share = hold_until(group_share, [chunks[3], got_labels])
    share = lax.psum_scatter(group_share, "docs", scatter_dimension=0, tiled=True)[0]
    for place in range(4, owner_count):
        after = [chunks[4]] if place == owner_count - 1 else [chunks[3], got_labels]
        chunks.append(travel(place, hold_until(sent[place], after)))

    bests = [jnp.full((owner_count * blocks, LANES), -2.0, jnp.float32)]
    flat = None
    for place in range(owner_count - 1):
        after = []
        if place == owner_count - 2:
            packed = pack_share(share, group_tally, bests[-2:-1])
            centroids, centroid_unit = make_centroids(lax.all_gather(packed, "grp"), per_owner)
            after = [centroid_unit]
        best, flat = gram_step(rows, columns, bests[-1], flat, chunks[place], place * padded, after)
        bests.append(best)
    results = gram_step(
        rows, columns, bests[-1], flat, chunks[-1], (owner_count - 1) * padded, final=(centroid_unit, me, turns_of)
    )
    back = lax.all_to_all(results, "docs", split_axis=0, concat_axis=0, tiled=True)
    near, cosine = place_rows(starts, slots, back, per_owner)
    return (centroids, near.reshape(-1), cosine.reshape(-1))


def solution(mesh):
    placed = (P(("grp", "docs"), None), P(("grp", "docs")), P())
    return jax.shard_map(
        per_device,
        mesh=mesh,
        in_specs=placed,
        out_specs=(P("docs", None), P(("grp", "docs")), P(("grp", "docs"))),
        check_vma=False,
    )
```

```python
import functools

import jax
import jax.numpy as jnp
from jax import lax
from jax.experimental import pallas as pl
from jax.experimental.pallas import tpu as pltpu
from jax.sharding import PartitionSpec as P

epsilon = 1e-06
LANES = 128
SUBLANES = 8
MIB = 1024 * 1024
TILE = 512
in_vmem = pl.BlockSpec(memory_space=pltpu.VMEM)
in_smem = pl.BlockSpec(memory_space=pltpu.SMEM)
anywhere = pl.BlockSpec(memory_space=pl.ANY)
brief = pl.CostEstimate(flops=1000, bytes_accessed=1000, transcendentals=0)


def round_up(value, step):
    return -(-value // step) * step


def params(mib=44):
    return pltpu.CompilerParams(vmem_limit_bytes=mib * MIB)


def look_up(table_ref, index):
    lane = jnp.bitwise_and(index, LANES - 1)
    row = jnp.right_shift(index, 7)
    found = jnp.zeros(index.shape, jnp.int32)
    for part in range(table_ref.shape[0]):
        entries = jnp.broadcast_to(table_ref[part : part + 1, :], index.shape)
        found = jnp.where(row == part, jnp.take_along_axis(entries, lane, axis=1), found)
    return found


def rows_below(slots, bound):
    return jnp.sum((slots < bound).astype(jnp.float32)).astype(jnp.int32)


def plan_kernel(per_owner, limit, assign_ref, table_ref, slot_ref, start_ref):
    slots = look_up(table_ref, assign_ref[...])
    slot_ref[...] = slots
    for owner in range(start_ref.shape[0]):
        start_ref[owner] = jnp.minimum(rows_below(slots, owner * per_owner), limit)


def make_plan(assign_rows, table, owner_count, per_owner, limit):
    return pl.pallas_call(
        functools.partial(plan_kernel, per_owner, limit),
        out_shape=(
            jax.ShapeDtypeStruct(assign_rows.shape, jnp.int32),
            jax.ShapeDtypeStruct((owner_count,), jnp.int32),
        ),
        in_specs=[in_vmem, in_vmem],
        out_specs=(in_vmem, in_smem),
        compiler_params=params(8),
        name="plan",
    )(assign_rows, table)


def unit_kernel(steps, offset, turn, start_ref, me_ref, rows_ref, *refs):
    unit_ref, held, sem = refs[-3:]
    part = unit_ref.shape[0] // steps
    window = part + SUBLANES
    start = start_ref[lax.rem(me_ref[0] + turn, start_ref.shape[0])] + offset

    def first(step):
        return aligned_start(start + step * part, rows_ref.shape[0], window)

    copies = [
        pltpu.make_async_copy(rows_ref.at[pl.ds(first(step), window), :], held.at[step], sem.at[step])
        for step in range(steps)
    ]
    for copy in copies:
        copy.start()
    for step in range(steps):
        copies[step].wait()
        shift = start + step * part - first(step)
        groups = held[step].reshape(window // SUBLANES, SUBLANES, -1)
        turned = pltpu.roll(groups, SUBLANES - shift, 1)
        line = lax.broadcasted_iota(jnp.int32, (part // SUBLANES, SUBLANES, groups.shape[2]), 1)
        values = jnp.where(line < SUBLANES - shift, turned[:-1], turned[1:]).reshape(part, -1)
        scale = lax.rsqrt(jnp.sum(values * values, -1, keepdims=True) + epsilon)
        unit_ref[step * part : (step + 1) * part, :] = (values * scale).astype(jnp.bfloat16)


def unit_piece(starts, me, embeddings, turn, offset, rows, after):
    width = embeddings.shape[1]
    steps = rows // LANES if rows % LANES == 0 else 1
    return pl.pallas_call(
        functools.partial(unit_kernel, steps, offset, turn),
        out_shape=jax.ShapeDtypeStruct((rows, width), jnp.bfloat16),
        in_specs=[in_smem, in_smem, anywhere] + [anywhere] * len(after),
        out_specs=in_vmem,
        scratch_shapes=[
            pltpu.VMEM((steps, rows // steps + SUBLANES, width), jnp.float32),
            pltpu.SemaphoreType.DMA((steps,)),
        ],
        compiler_params=params(),
        cost_estimate=brief,
        name="unit",
    )(starts, me, embeddings, *after)


def hold_until(values, arrived, mib=8):
    def nothing(*refs):
        pass

    return pl.pallas_call(
        nothing,
        out_shape=jax.ShapeDtypeStruct(values.shape, values.dtype),
        in_specs=[anywhere] * (1 + len(arrived)),
        out_specs=anywhere,
        input_output_aliases={0: 0},
        compiler_params=params(mib),
        cost_estimate=brief,
        name="hold",
    )(values, *arrived)


def aligned_start(start, row_count, window):
    begin = jnp.minimum(jnp.left_shift(jnp.right_shift(start, 3), 3), row_count - window)
    return pl.multiple_of(begin, SUBLANES)


def flat_window(held, start, rows):
    span = round_up(rows + 1, SUBLANES)
    shift = jnp.bitwise_and(start, LANES - 1)
    block = held[pl.ds(jnp.right_shift(start, 7), span), :]
    turned = pltpu.roll(block, jnp.bitwise_and(LANES - shift, LANES - 1), 1)
    following = pltpu.roll(turned, span - 1, 0)
    lane = lax.broadcasted_iota(jnp.int32, block.shape, 1)
    return jnp.where(lane < LANES - shift, turned, following)


def window_labels(held, slots, owner, start, per_owner, capacity, blocks):
    low = owner * per_owner
    mine = (slots >= low) & (slots < low + per_owner)
    held[: slots.shape[0], :] = jnp.where(mine, slots - low, -1)
    labels = flat_window(held, start, blocks)
    place = lax.broadcasted_iota(jnp.int32, labels.shape, 0) * LANES + lax.broadcasted_iota(
        jnp.int32, labels.shape, 1
    )
    return jnp.where(place < capacity, labels, -1)


def summed_kernel(per_owner, capacity, start_ref, slot_ref, sum_ref, held):
    owner_count = sum_ref.shape[0]
    held[...] = jnp.full(held.shape, -1, jnp.int32)
    slots = slot_ref[...]
    window = capacity + SUBLANES
    wide = sum_ref.shape[1] // LANES
    for owner in range(owner_count):
        aligned = aligned_start(start_ref[owner], slots.size, window)
        labels = window_labels(held, slots, owner, aligned, per_owner, window, wide)
        for block in range(wide):
            sum_ref[owner : owner + 1, block * LANES : (block + 1) * LANES] = labels[block : block + 1, :]


def summed_labels(starts, slots, owner_count, per_owner, capacity):
    return pl.pallas_call(
        functools.partial(summed_kernel, per_owner, capacity),
        out_shape=jax.ShapeDtypeStruct((owner_count, round_up(capacity + SUBLANES, LANES)), jnp.int32),
        in_specs=[in_smem, in_vmem],
        out_specs=in_vmem,
        scratch_shapes=[pltpu.VMEM((slots.shape[0] + 2 * SUBLANES, LANES), jnp.int32)],
        compiler_params=params(8),
        name="summed",
    )(starts, slots)


def sent_kernel(per_owner, capacity, start_ref, slot_ref, after_ref, sent_ref, held):
    owner_count, span, _ = sent_ref.shape
    held[...] = jnp.full(held.shape, -1, jnp.int32)
    slots = slot_ref[...]
    for owner in range(owner_count):
        labels = window_labels(held, slots, owner, start_ref[owner], per_owner, capacity, span - 1)
        sent_ref[owner] = labels[:span, :]


def sent_labels(starts, slots, owner_count, per_owner, capacity, after):
    span = round_up(-(-capacity // LANES) + 1, SUBLANES)
    return pl.pallas_call(
        functools.partial(sent_kernel, per_owner, capacity),
        out_shape=jax.ShapeDtypeStruct((owner_count, span, LANES), jnp.int32),
        in_specs=[in_smem, in_vmem, anywhere],
        out_specs=in_vmem,
        scratch_shapes=[pltpu.VMEM((slots.shape[0] + 2 * SUBLANES, LANES), jnp.int32)],
        compiler_params=params(8),
        name="sent",
    )(starts, slots, after)


def arrived_kernel(blocks, turns_of, me_ref, got_ref, row_ref, column_ref, tally_ref):
    tally = jnp.zeros((LANES, LANES), jnp.float32)
    cluster = lax.broadcasted_iota(jnp.int32, tally.shape, 0)
    for place, turn in enumerate(turns_of):
        source = lax.rem(me_ref[0] + len(turns_of) - turn, len(turns_of))
        for block in range(blocks):
            line = place * blocks + block
            spread = jnp.broadcast_to(got_ref[source, block : block + 1, :], tally.shape)
            row_ref[line : line + 1, :] = spread[:1, :]
            column_ref[line * LANES : (line + 1) * LANES, :] = spread.T
            tally += (spread == cluster).astype(jnp.float32)
    total = jnp.broadcast_to(jnp.sum(tally, 1, keepdims=True), tally.shape)
    tally_ref[...] = jnp.zeros(tally_ref.shape, jnp.float32)
    tally_ref[:, :LANES] = total.T[:SUBLANES, :]


def arrived_labels(me, got, turns_of, blocks, width):
    lines = len(turns_of) * blocks
    return pl.pallas_call(
        functools.partial(arrived_kernel, blocks, turns_of),
        out_shape=(
            jax.ShapeDtypeStruct((lines, LANES), jnp.int32),
            jax.ShapeDtypeStruct((lines * LANES, LANES), jnp.int32),
            jax.ShapeDtypeStruct((SUBLANES, width), jnp.float32),
        ),
        in_specs=[in_smem, in_vmem],
        out_specs=(in_vmem, in_vmem, in_vmem),
        compiler_params=params(8),
        name="arrived",
    )(me, got)


def sum_kernel(start_ref, label_ref, rows_ref, *refs):
    sum_ref, held, sem = refs[-3:]
    owner_count, per_owner, _ = sum_ref.shape
    window = held.shape[1]
    widest = float(jnp.finfo(jnp.bfloat16).max)

    def copy(owner, slot):
        first = aligned_start(start_ref[owner], rows_ref.shape[0], window)
        return pltpu.make_async_copy(rows_ref.at[pl.ds(first, window), :], held.at[slot], sem.at[slot])

    copy(0, 0).start()

    def body(owner, carry):
        slot = lax.rem(owner, 2)

        @pl.when(owner + 1 < owner_count)
        def _():
            copy(owner + 1, 1 - slot).start()

        copy(owner, slot).wait()
        labels = label_ref[pl.ds(owner, 1), :][:, :window]
        cluster = lax.broadcasted_iota(jnp.int32, (per_owner, window), 0)
        member = (labels == cluster).astype(jnp.float32).astype(jnp.bfloat16)
        values = held[slot]
        high = jnp.clip(values, -widest, widest).astype(jnp.bfloat16)
        rest = values - high.astype(jnp.float32)
        middle = rest.astype(jnp.bfloat16)
        low = (rest - middle.astype(jnp.float32)).astype(jnp.bfloat16)
        total = jnp.dot(member, high, preferred_element_type=jnp.float32)
        total += jnp.dot(member, middle, preferred_element_type=jnp.float32)
        total += jnp.dot(member, low, preferred_element_type=jnp.float32)
        sum_ref[pl.ds(owner, 1)] = total[None]
        return carry

    lax.fori_loop(0, owner_count, body, 0)


def slot_sums(starts, labels, embeddings, per_owner, capacity, after):
    owner_count = labels.shape[0]
    width = embeddings.shape[1]
    return pl.pallas_call(
        sum_kernel,
        out_shape=jax.ShapeDtypeStruct((owner_count, per_owner, width), jnp.float32),
        in_specs=[in_smem, in_vmem, anywhere] + [anywhere] * len(after),
        out_specs=in_vmem,
        scratch_shapes=[
            pltpu.VMEM((2, capacity + SUBLANES, width), jnp.float32),
            pltpu.SemaphoreType.DMA((2,)),
        ],
        compiler_params=params(),
        cost_estimate=pl.CostEstimate(
            flops=6 * owner_count * per_owner * capacity * width,
            bytes_accessed=4 * embeddings.size,
            transcendentals=0,
        ),
        name="sums",
    )(starts, labels, embeddings, *after)


def gram_kernel(begin, rows, wide, after_count, turns_of, *refs):
    chunk_ref, row_ref, column_ref, best_ref, *refs = refs
    flat_ref = centroid_ref = result_ref = None
    if begin:
        flat_ref, *refs = refs
    refs = refs[after_count:]
    if turns_of:
        centroid_ref, me_ref, result_ref, *refs, out_ref, cosine_ref = refs
    else:
        out_ref, flat_ref, *refs = refs
    mine, turned, labels, tiles, even, odd, best, sem, tile_sem = refs
    first = begin // LANES
    size = tiles.shape[2]
    count = -(-begin // size)

    def line_of(tile):
        return jnp.minimum(tile * (size // LANES), first - size // LANES)

    def fetch(tile):
        start = pl.multiple_of(line_of(tile) * LANES, LANES)
        slot = lax.rem(tile, 4)
        return pltpu.make_async_copy(flat_ref.at[:, pl.ds(start, size)], tiles.at[slot], tile_sem.at[slot])

    chunk_copy = pltpu.make_async_copy(chunk_ref, mine.at[pl.ds(0, rows), :], sem.at[0])
    label_copy = pltpu.make_async_copy(column_ref.at[pl.ds(begin, wide), :], labels, sem.at[1])
    chunk_copy.start()
    label_copy.start()
    for tile in range(min(count, 3)):
        fetch(jnp.int32(tile)).start()
    if rows < wide:
        mine[rows:wide, :] = jnp.zeros((wide - rows, mine.shape[1]), mine.dtype)
    if turns_of:
        mine[wide:, :] = centroid_ref[...]
        cosine_ref[...] = jnp.zeros(cosine_ref.shape, jnp.float32)
    out_ref[...] = best_ref[...]
    best[...] = jnp.full(best.shape, -2.0, jnp.float32)
    chunk_copy.wait()
    label_copy.wait()
    turned[...] = mine[:wide, :].T
    if not turns_of:
        flat_copy = pltpu.make_async_copy(turned, flat_ref.at[:, pl.ds(begin, wide)], sem.at[2])
        flat_copy.start()

    def products(right):
        return jnp.dot(mine[...], right, preferred_element_type=jnp.float32)

    halves = 2 if size % (4 * LANES) == 0 else 1

    def multiply(held, slot, half):
        here = slice(half * (size // halves), (half + 1) * (size // halves))
        held[:, here] = products(tiles[slot, :, here])

    def cosines(values, line):
        cluster = lax.broadcasted_iota(jnp.int32, values.shape, 0)
        own = jnp.where(row_ref[pl.ds(line, 1), :] == cluster, values, 0.0)
        cosine_ref[pl.ds(line, 1), :] = jnp.sum(own, 0, keepdims=True)

    def reduce_tile(held, tile, half):
        parts = range(half * (size // halves) // LANES, (half + 1) * (size // halves) // LANES)
        lines = {part: line_of(tile) + part for part in parts}
        tops = {part: jnp.full((SUBLANES, LANES), -2.0, jnp.float32) for part in parts}
        against = {
            part: jnp.broadcast_to(row_ref[pl.ds(lines[part], 1), :], (LANES, LANES)) for part in parts
        }
        for begin_row in range(0, wide, LANES):
            span = slice(begin_row, begin_row + LANES)
            own = labels[span, :]
            fold = best[span, :]
            for part in parts:
                near = jnp.where(own == against[part], held[span, part * LANES : (part + 1) * LANES], -2.0)
                fold = jnp.maximum(fold, near)
                tops[part] = jnp.maximum(tops[part], jnp.max(near.reshape(-1, SUBLANES, LANES), 0))
            best[span, :] = fold
        for part in parts:
            out_ref[pl.ds(lines[part], 1), :] = jnp.maximum(
                out_ref[pl.ds(lines[part], 1), :], jnp.max(tops[part], 0, keepdims=True)
            )
            if turns_of:
                cosines(held[wide:, part * LANES : (part + 1) * LANES], lines[part])

    if begin:
        fetch(jnp.int32(0)).wait()
        for half in range(halves):
            multiply(even, 0, half)

        def body(pair, carry):
            tile = pair * 2
            fetch(tile + 1).wait()

            @pl.when(tile + 3 < count)
            def _():
                fetch(tile + 3).start()

            for half in range(halves):
                multiply(odd, lax.rem(tile + 1, 4), half)
                reduce_tile(even, tile, half)
            fetch(tile + 2).wait()

            @pl.when(tile + 4 < count)
            def _():
                fetch(tile + 4).start()

            for half in range(halves):
                multiply(even, lax.rem(tile + 2, 4), half)
                reduce_tile(odd, tile + 1, half)
            return carry

        lax.fori_loop(0, (count - 1) // 2, body, 0)
        left = even
        if count % 2 == 0:
            left = odd
            fetch(jnp.int32(count - 1)).wait()
            for half in range(halves):
                multiply(odd, (count - 1) % 4, half)
                reduce_tile(even, jnp.int32(count - 2), half)
        for half in range(halves):
            reduce_tile(left, jnp.int32(count - 1), half)
    own = products(turned[...])
    row = lax.broadcasted_iota(jnp.int32, (wide, LANES), 0)
    column = lax.broadcasted_iota(jnp.int32, (wide, LANES), 1)
    for block in range(wide // LANES):
        line = first + block
        here = slice(block * LANES, (block + 1) * LANES)
        allowed = (labels[...] == row_ref[line : line + 1, :]) & (row != column + block * LANES)
        near = jnp.max(jnp.where(allowed, own[:wide, here], -2.0), 0, keepdims=True)
        other = jnp.max(best[here, :].T, 0, keepdims=True)
        out_ref[line : line + 1, :] = jnp.maximum(near, other)
        if turns_of:
            cosines(own[wide:, here], line)
    if turns_of:
        blocks = row_ref.shape[0] // len(turns_of)
        half = result_ref.shape[1] // 2
        result_ref[...] = jnp.zeros(result_ref.shape, jnp.float32)
        for place, turn in enumerate(turns_of):
            source = lax.rem(me_ref[0] + len(turns_of) - turn, len(turns_of))
            lines = slice(place * blocks, (place + 1) * blocks)
            result_ref[source, :blocks, :] = out_ref[lines, :]
            result_ref[source, half : half + blocks, :] = cosine_ref[lines, :]
    else:
        flat_copy.wait()


def gram_step(rows, columns, best, flat, chunk, begin, after=(), final=None):
    length, width = chunk.shape
    wide = round_up(length, LANES)
    tall = wide
    size = min(TILE, begin) if begin else LANES
    flat_shape = jax.ShapeDtypeStruct((width, columns.shape[0]), jnp.bfloat16)
    inputs = [chunk, rows, columns, best]
    in_specs = [anywhere, in_vmem, anywhere, in_vmem]
    aliases = {}
    if begin:
        if not final:
            aliases = {len(inputs): 1}
        inputs.append(flat)
        in_specs.append(anywhere)
    inputs += after
    in_specs += [anywhere] * len(after)
    out_shape = (jax.ShapeDtypeStruct(best.shape, jnp.float32), flat_shape)
    out_specs = (in_vmem, anywhere)
    turns_of = ()
    extra = []
    if final:
        centroid_unit, me, turns_of = final
        tall += centroid_unit.shape[0]
        inputs += [centroid_unit, me]
        in_specs += [in_vmem, in_smem]
        half = round_up(rows.shape[0] // len(turns_of) + 1, SUBLANES)
        out_shape = jax.ShapeDtypeStruct((len(turns_of), 2 * half, LANES), jnp.float32)
        out_specs = in_vmem
        extra = [pltpu.VMEM(best.shape, jnp.float32)] * 2
    return pl.pallas_call(
        functools.partial(gram_kernel, begin, length, wide, len(after), turns_of),
        out_shape=out_shape,
        in_specs=in_specs,
        out_specs=out_specs,
        scratch_shapes=[
            pltpu.VMEM((tall, width), jnp.bfloat16),
            pltpu.VMEM((width, wide), jnp.bfloat16),
            pltpu.VMEM((wide, LANES), jnp.int32),
            pltpu.VMEM((4, width, size), jnp.bfloat16),
            pltpu.VMEM((tall, size), jnp.float32),
            pltpu.VMEM((tall, size), jnp.float32),
            pltpu.VMEM((wide, LANES), jnp.float32),
            pltpu.SemaphoreType.DMA((3,)),
            pltpu.SemaphoreType.DMA((4,)),
        ]
        + extra,
        input_output_aliases=aliases,
        compiler_params=params(),
        cost_estimate=brief,
        name="gram",
    )(*inputs)


def pack_kernel(share_ref, tally_ref, *refs):
    packed_ref = refs[-1]
    packed_ref[: share_ref.shape[0], :] = share_ref[...]
    packed_ref[share_ref.shape[0] :, :] = tally_ref[...]


def pack_share(share, tally, after):
    length = share.shape[0] + tally.shape[0]
    return pl.pallas_call(
        pack_kernel,
        out_shape=jax.ShapeDtypeStruct((length, share.shape[1]), jnp.float32),
        in_specs=[in_vmem, in_vmem] + [anywhere] * len(after),
        out_specs=in_vmem,
        compiler_params=params(8),
        name="pack",
    )(share, tally, *after)


def centroid_kernel(gathered_ref, centroid_ref, unit_ref):
    groups, length, width = gathered_ref.shape
    share = length - SUBLANES
    per_owner = centroid_ref.shape[0]
    tally = jnp.sum(gathered_ref[:, share, :LANES], 0, keepdims=True)
    column = jnp.broadcast_to(tally, (LANES, LANES)).T[:per_owner, :]
    sums = jnp.concatenate([gathered_ref[group, :share, :] for group in range(groups)], 0)
    centroids = sums / jnp.concatenate([column] * (width // LANES), 1)
    centroid_ref[...] = centroids
    scale = lax.rsqrt(jnp.sum(centroids * centroids, -1, keepdims=True) + epsilon)
    unit_ref[...] = (centroids * scale).astype(jnp.bfloat16)


def make_centroids(gathered, per_owner):
    shape = (per_owner, gathered.shape[2])
    return pl.pallas_call(
        centroid_kernel,
        out_shape=(
            jax.ShapeDtypeStruct(shape, jnp.float32),
            jax.ShapeDtypeStruct(shape, jnp.bfloat16),
        ),
        in_specs=[in_vmem],
        out_specs=(in_vmem, in_vmem),
        compiler_params=params(8),
        name="centroids",
    )(gathered)


def place_kernel(per_owner, start_ref, slot_ref, back_ref, near_ref, cosine_ref, held, result):
    owner_count, double, _ = back_ref.shape
    span = double // 2
    rows = slot_ref.shape[0]
    held[...] = jnp.full(held.shape, -1, jnp.int32)
    held[:rows, :] = slot_ref[...]
    result[...] = jnp.zeros(result.shape, jnp.float32)
    lane = lax.broadcasted_iota(jnp.int32, (span, LANES), 1)
    for owner in range(owner_count):
        start = start_ref[owner]
        first = pl.ds(jnp.right_shift(start, 7), span)
        shift = jnp.bitwise_and(start, LANES - 1)
        slots = held[first, :]
        mine = (slots >= owner * per_owner) & (slots < (owner + 1) * per_owner)
        for kind in range(2):
            turned = pltpu.roll(back_ref[owner, kind * span : (kind + 1) * span, :], shift, 1)
            earlier = pltpu.roll(turned, 1, 0)
            moved = jnp.where(lane >= shift, turned, earlier)
            result[kind, first, :] = jnp.where(mine, moved, result[kind, first, :])
    near_ref[...] = result[0, :rows, :]
    cosine_ref[...] = result[1, :rows, :]


def place_rows(starts, slots, back, per_owner):
    span = back.shape[1] // 2
    rows = slots.shape[0]
    return pl.pallas_call(
        functools.partial(place_kernel, per_owner),
        out_shape=(jax.ShapeDtypeStruct(slots.shape, jnp.float32),) * 2,
        in_specs=[in_smem, in_vmem, in_vmem],
        out_specs=(in_vmem, in_vmem),
        scratch_shapes=[
            pltpu.VMEM((rows + span, LANES), jnp.int32),
            pltpu.VMEM((2, rows + span, LANES), jnp.float32),
        ],
        compiler_params=params(8),
        name="place",
    )(starts, slots, back)


def turns(count):
    order = sorted(range(count), key=lambda turn: (min(turn, count - turn), turn))
    if count == 8:
        order = [0, 2, 1, 3, 7, 6, 5, 4]
    return order


def per_device(embeddings, assign, cluster_slot):
    row_count, width = embeddings.shape
    owner_count = lax.axis_size("docs")
    per_owner = cluster_slot.shape[0] // owner_count
    capacity = row_count // owner_count + row_count // (4 * owner_count)
    padded = round_up(capacity, LANES)
    blocks = padded // LANES
    me = lax.axis_index("docs").astype(jnp.int32).reshape(1)
    turns_of = turns(owner_count)

    slots, starts = make_plan(
        assign.reshape(-1, LANES), cluster_slot.reshape(-1, LANES), owner_count, per_owner, row_count - capacity
    )

    sent = []
    for place, turn in enumerate(turns_of):
        sent.append(unit_piece(starts, me, embeddings, turn, 0, capacity, sent[-1:] if place > 1 else []))

    def travel(place, piece):
        turn = turns_of[place]
        return lax.ppermute(piece, "docs", [(i, (i + turn) % owner_count) for i in range(owner_count)])

    chunks = [sent[0]] + [travel(place, sent[place]) for place in (1, 2, 3)]
    sum_labels = summed_labels(starts, slots, owner_count, per_owner, capacity)
    partial_sums = slot_sums(starts, sum_labels, embeddings, per_owner, capacity, sent[1:8])
    partial_sums = hold_until(partial_sums, chunks[1:3], 62)
    wire_labels = sent_labels(starts, slots, owner_count, per_owner, capacity, sent[7])
    wire_labels = hold_until(wire_labels, chunks[1:3])
    got_labels = lax.all_to_all(wire_labels, "docs", split_axis=0, concat_axis=0, tiled=True)
    rows, columns, group_tally = arrived_labels(me, got_labels, turns_of, blocks, width)
    group_share = lax.psum_scatter(partial_sums, "grp", scatter_dimension=1, tiled=True)
    group_share = hold_until(group_share, [chunks[3], got_labels])
    share = lax.psum_scatter(group_share, "docs", scatter_dimension=0, tiled=True)[0]
    for place in range(4, owner_count):
        after = [chunks[4]] if place == owner_count - 1 else [chunks[3], got_labels]
        chunks.append(travel(place, hold_until(sent[place], after)))

    bests = [jnp.full((owner_count * blocks, LANES), -2.0, jnp.float32)]
    flat = None
    for place in range(owner_count - 1):
        after = []
        if place == owner_count - 2:
            packed = pack_share(share, group_tally, bests[-2:-1])
            centroids, centroid_unit = make_centroids(lax.all_gather(packed, "grp"), per_owner)
            after = [centroid_unit]
        best, flat = gram_step(rows, columns, bests[-1], flat, chunks[place], place * padded, after)
        bests.append(best)
    results = gram_step(
        rows, columns, bests[-1], flat, chunks[-1], (owner_count - 1) * padded, final=(centroid_unit, me, turns_of)
    )
    back = lax.all_to_all(results, "docs", split_axis=0, concat_axis=0, tiled=True)
    near, cosine = place_rows(starts, slots, back, per_owner)
    return (centroids, near.reshape(-1), cosine.reshape(-1))


def solution(mesh):
    placed = (P(("grp", "docs"), None), P(("grp", "docs")), P())
    return jax.shard_map(
        per_device,
        mesh=mesh,
        in_specs=placed,
        out_specs=(P("docs", None), P(("grp", "docs")), P(("grp", "docs"))),
        check_vma=False,
    )
```
